32 devices in a mesh: basin: 2 (over y), row: 4 (over z), col: 2 (over x), sub: 2 (over core).
Axes of the slice: x: 2, y: 2, z: 4, core: 2. Of those that a mesh axis runs over, the one named last changes fastest.
Arguments:
- water_depth: float32 [256, 128, 128], P(('basin', 'row', 'col', 'sub')), parts along dimension 0, may hold values from 0.1 to 3
- flow_east: float32 [256, 128, 128], P(('basin', 'row', 'col', 'sub')), parts along dimension 0, may hold values from -3 to 3
- flow_south: float32 [256, 128, 128], P(('basin', 'row', 'col', 'sub')), parts along dimension 0, may hold values from -3 to 3
- bed_level: float32 [256, 128, 128], P(('basin', 'row', 'col', 'sub')), parts along dimension 0, may hold values from -2 to 2
- manning_n: float32 [256, 128, 128], P(('basin', 'row', 'col', 'sub')), parts along dimension 0, may hold values from 0.03 to 0.15
- placed_before: int32 [256], P('basin'), parts along dimension 0, may hold values from 0 to 127, as said below
- placed_after: int32 [256], P('basin'), parts along dimension 0, may hold values from 0 to 127, as said below
- wet_tiles: int32 [256], P('basin'), parts along dimension 0, may hold values 0 or 1
Outputs:
- new_depth: float32 [256, 128, 128], P(('basin', 'row', 'col', 'sub')), parts along dimension 0
- new_flow_east: float32 [256, 128, 128], P(('basin', 'row', 'col', 'sub')), parts along dimension 0
- new_flow_south: float32 [256, 128, 128], P(('basin', 'row', 'col', 'sub')), parts along dimension 0
The draws below stay inside these ranges and needn't reach their ends.
There are 2 independent parts, one for each index of `basin`. The reference program is written for one: setup_inputs(seed, part) draws one part's arguments, and reference() takes and returns one part's arrays. A program takes and returns all parts, laid end to end along the dimension named above; each array names one. Nothing has to cross between parts.
Inputs may be any that keep to these rules, and one draw needn't show every extreme that they name: placed_before holds every tile once. Slot s lies on the device of index s // 8 over row, col and sub together; the tiles of tile row r sit on the devices of row index r. placed_after holds every tile once. A tile either keeps its slot of placed_before or goes to a slot on another device of the same row index. Each device gives up exactly 4 tiles and takes exactly 4, at most 2 of them from any one device.
All inputs are finite; a program needn't handle non-finite values.
Results may differ from the reference program's by a relative error of at most 0.00002.
Values sent between devices are 32-bit elements; how exact they have to be, the bound alone decides.
No kernel may reach another device: no remote copies, remote signals or barrier semaphores. Data moves between devices by JAX's collectives and lax.ppermute only.
A program may use at most 64 MiB of HBM per device.

```python
import math
import jax
import jax.numpy as jnp

TS = 128
TILE_DEV = 8
STEPS = 6
LANES = 4
GR = 4
GC = 32
TILES = 128
MOVE_OUT = 4


def tile_layouts(key):
    base_key = jax.random.fold_in(key, 11)
    key_rows, key_labels, key_offsets, key_leave = jax.random.split(base_key, 4)
    row_ids = jnp.arange(GR, dtype=jnp.int32)
    orders = jax.vmap(lambda sub_key: jax.random.permutation(sub_key, GC))(jax.random.split(key_rows, GR)).astype(jnp.int32)
    before = orders + row_ids[:, None] * GC
    labels = jax.vmap(lambda sub_key: jax.random.permutation(sub_key, LANES))(jax.random.split(key_labels, GR)).astype(jnp.int32)
    offsets = jax.vmap(lambda sub_key: jnp.repeat(jax.random.permutation(sub_key, LANES - 1) + 1, 2)[:MOVE_OUT])(jax.random.split(key_offsets, GR)).astype(jnp.int32)
    leaving = jax.vmap(lambda sub_key: jax.random.permutation(sub_key, TILE_DEV)[:MOVE_OUT])(jax.random.split(key_leave, GR * LANES)).astype(jnp.int32)
    flat_leave = leaving.reshape(GR, LANES * MOVE_OUT)
    positions = jnp.arange(LANES, dtype=jnp.int32)
    job_index = jnp.arange(MOVE_OUT, dtype=jnp.int32)[None, None, :]
    sender_pos = (positions[None, :, None] - offsets[:, None, :]) % LANES
    sender_lane = jnp.take_along_axis(labels, sender_pos.reshape(GR, LANES * MOVE_OUT), axis=1).reshape(GR, LANES, MOVE_OUT)
    receiver_lane = jnp.broadcast_to(labels[:, :, None], (GR, LANES, MOVE_OUT))
    into_slot = jnp.take_along_axis(flat_leave, (receiver_lane * MOVE_OUT + job_index).reshape(GR, LANES * MOVE_OUT), axis=1)
    from_slot = jnp.take_along_axis(flat_leave, (sender_lane * MOVE_OUT + job_index).reshape(GR, LANES * MOVE_OUT), axis=1)
    target = receiver_lane.reshape(GR, LANES * MOVE_OUT) * TILE_DEV + into_slot
    source = sender_lane.reshape(GR, LANES * MOVE_OUT) * TILE_DEV + from_slot
    moved_ids = jnp.take_along_axis(before, source, axis=1)
    after = jax.vmap(lambda row_data, spots, values: row_data.at[spots].set(values))(before, target, moved_ids)
    return (before.reshape(GR * GC).astype(jnp.int32), after.reshape(GR * GC).astype(jnp.int32))


def draw_placed_before(key, part):
    return tile_layouts(key)[0]


def draw_placed_after(key, part):
    return tile_layouts(key)[1]


def place_ends(values, key, least, top_value):
    shape = values.shape
    index_at = [jax.random.randint(jax.random.fold_in(key, axis), (), 0, shape[axis]) for axis in range(len(shape))]
    values = values.at[tuple(index_at)].set(least)
    longest = shape.index(max(shape))
    index_at[longest] = (index_at[longest] + 1) % shape[longest]
    return values.at[tuple(index_at)].set(top_value)


def block_levels(own_key, dims, pieces, low, largest):
    def one(axis_at, blocks):
        heights = jax.random.uniform(jax.random.fold_in(jax.random.fold_in(own_key, 6), axis_at), (blocks,), jnp.float32, low / len(pieces), largest / len(pieces))
        return jnp.repeat(jnp.exp(heights), dims[axis_at] // blocks).reshape((-1,) + (1,) * (len(dims) - axis_at - 1))

    level = one(*pieces[0])
    for cut in pieces[1:]:
        level = level * one(*cut)
    return level


def bell_draw(own_key, shape, deviation, most, cuts=(), held_as=jnp.bfloat16):
    result = deviation * jax.random.normal(own_key, shape, jnp.float32)
    if cuts:
        result = result * block_levels(own_key, shape, cuts, -0.22, 0.18)
    return jnp.clip(result, -most, most).astype(held_as)


def setup_inputs(seed: int = 0, part: int = 0) -> dict:
    keys = jax.random.split(jax.random.key(seed), 9)
    part_keys = jax.random.split(jax.random.fold_in(keys[8], part), 9)
    water_depth = jnp.clip(jnp.exp(math.log(3.0) - 3.4011974 * jax.random.uniform(part_keys[0], (TILES, TS, TS), jnp.float32) ** block_levels(part_keys[0], (TILES, TS, TS), ((0, 16),), -0.2, 0.2)), 0.1, 3.0)
    flow_east = bell_draw(part_keys[1], (TILES, TS, TS), 0.5, 3.0, ((0, 16),), jnp.float32)
    flow_south = bell_draw(part_keys[2], (TILES, TS, TS), 0.5, 3.0, ((0, 16),), jnp.float32)
    bed_level = bell_draw(part_keys[3], (TILES, TS, TS), 0.3, 2.0, ((0, 16),), jnp.float32)
    manning_n = jnp.clip(jnp.exp(math.log(0.15) - 1.609438 * jax.random.uniform(part_keys[4], (TILES, TS, TS), jnp.float32) ** block_levels(part_keys[4], (TILES, TS, TS), ((0, 16),), -0.2, 0.2)), 0.03, 0.15)
    placed_before = draw_placed_before(jax.random.fold_in(jax.random.fold_in(keys[8], part), 71), part)
    placed_after = draw_placed_after(jax.random.fold_in(jax.random.fold_in(keys[8], part), 71), part)
    wet_tiles = place_ends((jax.random.randint(part_keys[7], (TILES,), 0, 4) < 3).astype(jnp.int32), jax.random.fold_in(part_keys[7], 1), 0, 1)
    return dict(water_depth=water_depth, flow_east=flow_east, flow_south=flow_south, bed_level=bed_level, manning_n=manning_n, placed_before=placed_before, placed_after=placed_after, wet_tiles=wet_tiles)


GRAV = 9.81
STEP_TIME = 0.5
SPACING = 5.0
RATE = 0.1
DEPTH_FLOOR = 0.3


def face_flow(discharge, surface, surface_next, ground, ground_next, manning):
    wetted = jnp.maximum(surface, surface_next) - jnp.maximum(ground, ground_next)
    pressure = GRAV * STEP_TIME * jnp.maximum(wetted, 0.0) * (surface_next - surface) / SPACING
    resistance = 1.0 + GRAV * STEP_TIME * manning * manning * jnp.abs(discharge) / jnp.power(jnp.maximum(wetted, DEPTH_FLOOR), 7.0 / 3.0)
    return (discharge - pressure) / resistance


def inverse(ordering):
    entries = ordering.shape[0]
    return jnp.zeros((entries,), jnp.int32).at[ordering].set(jnp.arange(entries, dtype=jnp.int32))


def assemble(tile_data, where_before):
    ordered = tile_data[where_before]
    return ordered.reshape(GR, GC, TS, TS).transpose(0, 2, 1, 3).reshape(GR * TS, GC * TS)


def disperse(grid, placed_after):
    tile_data = grid.reshape(GR, TS, GC, TS).transpose(0, 2, 1, 3).reshape(GR * GC, TS, TS)
    return tile_data[placed_after]


def reference(water_depth, flow_east, flow_south, bed_level, manning_n, placed_before, placed_after, wet_tiles):
    where_before = inverse(placed_before)
    depth_now = assemble(water_depth, where_before)
    flow_x = assemble(flow_east, where_before)
    flow_y = assemble(flow_south, where_before)
    ground = assemble(bed_level, where_before)
    manning = assemble(manning_n, where_before)
    wet_cells = jnp.repeat(jnp.repeat((wet_tiles == 1).reshape(GR, GC), TS, axis=0), TS, axis=1)
    open_east = jnp.concatenate([wet_cells[:, :-1] & wet_cells[:, 1:], jnp.zeros((GR * TS, 1), jnp.bool_)], axis=1)
    open_south = jnp.concatenate([wet_cells[:-1, :] & wet_cells[1:, :], jnp.zeros((1, GC * TS), jnp.bool_)], axis=0)
    for step_index in range(STEPS):
        surface = depth_now + ground
        surface_east = jnp.concatenate([surface[:, 1:], surface[:, -1:]], axis=1)
        ground_east = jnp.concatenate([ground[:, 1:], ground[:, -1:]], axis=1)
        surface_south = jnp.concatenate([surface[1:, :], surface[-1:, :]], axis=0)
        ground_south = jnp.concatenate([ground[1:, :], ground[-1:, :]], axis=0)
        updated_x = face_flow(flow_x, surface, surface_east, ground, ground_east, manning)
        updated_y = face_flow(flow_y, surface, surface_south, ground, ground_south, manning)
        flow_x = jnp.where(wet_cells, jnp.where(open_east, updated_x, 0.0), flow_x)
        flow_y = jnp.where(wet_cells, jnp.where(open_south, updated_y, 0.0), flow_y)
        inflow_x = jnp.concatenate([jnp.zeros_like(flow_x[:, :1]), jnp.where(open_east[:, :-1], flow_x[:, :-1], 0.0)], axis=1)
        inflow_y = jnp.concatenate([jnp.zeros_like(flow_y[:1, :]), jnp.where(open_south[:-1, :], flow_y[:-1, :], 0.0)], axis=0)
        depth_now = jnp.where(wet_cells, depth_now + RATE * (((inflow_x - flow_x) + inflow_y) - flow_y), depth_now)
    return (disperse(depth_now, placed_after), disperse(flow_x, placed_after), disperse(flow_y, placed_after))
```

```python
import functools
import math

import jax
import jax.numpy as jnp
from jax import lax
from jax.experimental import pallas as pl
from jax.experimental.pallas import tpu as pltpu
from jax.sharding import PartitionSpec as P

STEPS = 6
GRAV = 9.81
STEP_TIME = 0.5
SPACING = 5.0
RATE = 0.1
DEPTH_FLOOR = 0.3

FIELDS = 5
HALO = STEPS
PAIR = 2 * HALO
PACK_ROWS = 32
SIDE = 128
TOP = 16
ROWS = SIDE + 32
LO = 8
HI = SIDE + 24
CHUNK = 24
NT = 4
GROUP = SIDE // NT
CLOSED = 1e30
POWER = -(7.0 / 3.0) / math.log(2.0)

ENTRY = 32
NEAR = {"w": 0, "e": 1, "n": 2, "s": 3, "nw": 4, "ne": 5, "sw": 6, "se": 7}
STEP_TO = ((0, -1), (0, 1), (-1, 0), (1, 0), (-1, -1), (-1, 1), (1, -1), (1, 1))
LEAVE, STAY, RECEIVE = 0, NT * ENTRY, 2 * NT * ENTRY

SMEM = pltpu.SMEM
ANY = pl.ANY


def lane_index():
    return lax.broadcasted_iota(jnp.int32, (1, SIDE), 1)


def index_kernel(
    shape, pos_ref, before_ref, after_ref, wet_ref, table, inv_before, inv_after, count
):
    cols, subs, tile_count, total = shape
    lanes = cols * subs
    row_tiles = lanes * tile_count
    tile_rows = total // row_tiles
    my_row, my_col, my_sub = pos_ref[0], pos_ref[1], pos_ref[2]
    me = my_row * lanes + my_col * subs + my_sub

    def invert(s, carry):
        for u in range(8):
            inv_before[before_ref[s * 8 + u]] = s * 8 + u
            inv_after[after_ref[s * 8 + u]] = s * 8 + u
        return carry

    lax.fori_loop(0, total // 8, invert, 0)
    for i in range(2 * NT):
        table[i * ENTRY] = 0
    for i in range(lanes * 2):
        table[RECEIVE + i] = -1
    for i in range(lanes + 1):
        count[i] = 0

    def modulo(value, size):
        return lax.rem(value + size, size)

    def entry(base, tile, source, target):
        table[base] = 1
        table[base + 1] = jnp.where(wet_ref[tile] == 1, 1, 0)
        table[base + 2] = source
        table[base + 3] = target
        row, col = lax.div(tile, row_tiles), lax.rem(tile, row_tiles)
        for n, (dr, dc) in enumerate(STEP_TO):
            r, c = row + dr, col + dc
            there = (r >= 0) & (r < tile_rows) & (c >= 0) & (c < row_tiles)
            near = jnp.where(there, tile + (dr * row_tiles + dc), tile)
            at = inv_before[near]
            lane = lax.rem(lax.div(at, tile_count), lanes)
            rel = modulo(my_col - lax.div(lane, subs), cols) * subs + modulo(
                my_sub - lax.rem(lane, subs), subs
            )
            table[base + 4 + 3 * n] = jnp.where(there & (wet_ref[near] == 1), 1, 0)
            table[base + 5 + 3 * n] = rel
            table[base + 6 + 3 * n] = lax.rem(at, tile_count)

    def own(s, carry):
        tile = before_ref[me * tile_count + s]
        device = lax.div(inv_after[tile], tile_count)
        stays = device == me

        @pl.when(stays)
        def _():
            at = jnp.minimum(count[0], NT - 1)
            count[0] = at + 1
            entry(STAY + at * ENTRY, tile, s, s)

        @pl.when(jnp.logical_not(stays))
        def _():
            lane = lax.rem(device, lanes)
            rel = modulo(lax.div(lane, subs) - my_col, cols) * subs + modulo(
                lax.rem(lane, subs) - my_sub, subs
            )
            place = jnp.minimum(count[rel], 1)
            count[rel] = place + 1
            at = jnp.minimum(count[lanes], NT - 1)
            count[lanes] = at + 1
            entry(LEAVE + at * ENTRY, tile, s, rel * 2 + place)

        return carry

    lax.fori_loop(0, tile_count, own, 0)

    for rel in range(1, lanes):
        col = modulo(my_col - rel // subs, cols)
        sub = modulo(my_sub - rel % subs, subs)
        device = my_row * lanes + col * subs + sub

        def arriving(s, found):
            at = inv_after[before_ref[device * tile_count + s]]
            mine = lax.div(at, tile_count) == me

            @pl.when(mine)
            def _():
                table[RECEIVE + rel * 2 + jnp.minimum(found, 1)] = lax.rem(at, tile_count)

            return found + jnp.where(mine, 1, 0)

        lax.fori_loop(0, tile_count, arriving, jnp.int32(0))


def make_table(shape, position, before, after, wet):
    cols, subs, _, total = shape
    size = RECEIVE + 2 * cols * subs
    return pl.pallas_call(
        functools.partial(index_kernel, shape),
        name="index_table",
        out_shape=jax.ShapeDtypeStruct((size,), jnp.int32),
        in_specs=[pl.BlockSpec(memory_space=SMEM)] * 4,
        out_specs=pl.BlockSpec(memory_space=SMEM),
        scratch_shapes=[
            SMEM((total,), jnp.int32),
            SMEM((total,), jnp.int32),
            SMEM((cols * subs + 1,), jnp.int32),
        ],
    )(position, before, after, wet)


def pack_kernel(*refs):
    fields = refs[:FIELDS]
    columns, first, last = refs[FIELDS:]
    lane = lane_index()
    packed = jnp.zeros((SIDE, SIDE), jnp.float32)
    for t in range(2):
        for f in range(FIELDS):
            at = PAIR * (t * FIELDS + f)
            moved = pltpu.roll(fields[f][t], at + HALO, 1)
            packed = jnp.where((lane >= at) & (lane < at + PAIR), moved, packed)
            first[t, HALO * f : HALO * (f + 1), :] = fields[f][t, :HALO, :]
            last[t, 2 + HALO * f : 2 + HALO * (f + 1), :] = fields[f][t, SIDE - HALO :, :]
        first[t, FIELDS * HALO :, :] = jnp.zeros((2, SIDE), jnp.float32)
        last[t, :2, :] = jnp.zeros((2, SIDE), jnp.float32)
    columns[0] = packed


def pack_edges(fields, tile_count):
    rows = jax.ShapeDtypeStruct((tile_count, PACK_ROWS, SIDE), jnp.float32)
    return pl.pallas_call(
        pack_kernel,
        name="pack_edges",
        grid=(tile_count // 2,),
        out_shape=(jax.ShapeDtypeStruct((tile_count // 2, SIDE, SIDE), jnp.float32), rows, rows),
        in_specs=[pl.BlockSpec((2, SIDE, SIDE), lambda i: (i, 0, 0))] * FIELDS,
        out_specs=(
            pl.BlockSpec((1, SIDE, SIDE), lambda i: (i, 0, 0)),
            pl.BlockSpec((2, PACK_ROWS, SIDE), lambda i: (i, 0, 0)),
            pl.BlockSpec((2, PACK_ROWS, SIDE), lambda i: (i, 0, 0)),
        ),
    )(*fields)


def face(flow, level, level_next, ground, friction):
    wetted = jnp.maximum(level, level_next) - ground
    drive = (GRAV * STEP_TIME / SPACING) * jnp.maximum(wetted, 0.0) * (level_next - level)
    power = jnp.exp2(POWER * jnp.log(jnp.maximum(wetted, DEPTH_FLOOR)))
    return (flow - drive) / (1.0 + friction * jnp.abs(flow) * power)


def chunks():
    for r in range(LO, HI, CHUNK):
        yield r, min(CHUNK, HI - r)


def assemble(table, base, i, halo_cols, halo_above, halo_below, block, strip):
    lane = lane_index()
    at = GROUP * i

    def near(name):
        place = base + 5 + 3 * NEAR[name]
        return table[place], table[place + 1]

    def inside(lo, hi):
        return (lane >= at + lo) & (lane < at + hi)

    west, east = near("w"), near("e")
    for f in range(FIELDS):
        rows = pl.ds(HALO * f, 8)

        def ends(halo, middle, left, right, out):
            mid = halo[middle[0], middle[1], rows, :]
            block[f][i, out : out + 8, :] = mid
            lower = jnp.where(lane < SIDE // 2, mid, halo[left[0], left[1], rows, :])
            upper = jnp.where(lane < SIDE // 2, halo[right[0], right[1], rows, :], mid)
            value = jnp.where(
                inside(0, 16),
                pltpu.roll(lower, (at + 8) % SIDE, 1),
                pltpu.roll(upper, (at + 24) % SIDE, 1),
            )
            strip[f][out : out + 8, :] = jnp.where(
                inside(0, GROUP), value, strip[f][out : out + 8, :]
            )

        ends(halo_above, near("n"), near("nw"), near("ne"), LO)
        ends(halo_below, near("s"), near("sw"), near("se"), TOP + SIDE)

        def shifted(place, goal):
            source = PAIR * (lax.rem(place[1], 2) * FIELDS + f)
            shift = lax.rem(goal - source + 2 * SIDE, SIDE)
            return pltpu.roll(halo_cols[place[0], lax.div(place[1], 2)], shift, 1)

        core = block[f][i, TOP : TOP + SIDE, :]
        value = strip[f][TOP : TOP + SIDE, :]
        value = jnp.where(inside(0, 8), shifted(west, at + 2), value)
        value = jnp.where(inside(8, 16), pltpu.roll(core, (at + 8) % SIDE, 1), value)
        value = jnp.where(inside(16, 24), pltpu.roll(core, (at + 24) % SIDE, 1), value)
        value = jnp.where(inside(24, GROUP), shifted(east, at + 24 - HALO), value)
        strip[f][TOP : TOP + SIDE, :] = value


def advance_kernel(lanes, base, leaving, *refs):
    table = refs[0]
    inputs = refs[1 : 1 + FIELDS]
    halos = refs[1 + FIELDS : 1 + FIELDS + 3 * lanes]
    n_out = lanes - 1 if leaving else 3
    outs = refs[1 + FIELDS + 3 * lanes : 1 + FIELDS + 3 * lanes + n_out]
    (
        halo_cols, halo_above, halo_below,
        level, flow_x, flow_y, ground, friction, ground_x, ground_y,
        s_level, s_flow_x, s_flow_y, s_ground, s_friction, s_ground_x, s_ground_y,
        hist_level, hist_flow, sem_halo, sem_in, sem_out,
    ) = refs[1 + FIELDS + 3 * lanes + n_out :]
    block = (level, flow_x, flow_y, ground, friction)
    strip = (s_level, s_flow_x, s_flow_y, s_ground, s_friction)
    lane = lane_index()
    core = pl.ds(TOP, SIDE)

    halo_copies = []
    for k in range(lanes):
        for n, target in enumerate((halo_cols, halo_above, halo_below)):
            copy = pltpu.make_async_copy(halos[3 * k + n], target.at[k], sem_halo.at[3 * k + n])
            copy.start()
            halo_copies.append(copy)

    def entry(i):
        at = base + i * ENTRY
        return table[at] == 1, table[at + 1] == 1, table[at + 2], table[at + 3]

    def near_wet(i, name):
        return table[base + i * ENTRY + 4 + 3 * NEAR[name]] == 1

    def loads(i, slot):
        return [
            pltpu.make_async_copy(inputs[f].at[slot], block[f].at[i, core, :], sem_in.at[i, f])
            for f in range(FIELDS)
        ]

    for i in range(NT):
        valid, _, slot, _ = entry(i)

        @pl.when(valid)
        def _():
            for copy in loads(i, slot):
                copy.start()

    for copy in halo_copies:
        copy.wait()
    for i in range(NT):
        valid, wet, slot, _ = entry(i)

        @pl.when(valid)
        def _():
            for copy in loads(i, slot):
                copy.wait()

        @pl.when(valid & wet)
        def _():
            assemble(
                table, base + i * ENTRY, i, halo_cols, halo_above, halo_below, block, strip
            )

    def lane_wet(center, left, right):
        value = jnp.zeros((1, SIDE), jnp.int32)
        for i in range(NT):
            at = GROUP * i
            mid = jnp.where(jnp.bool_(True) if center == "c" else near_wet(i, center), 1, 0)
            sides = jnp.where(
                lane < at + 8,
                jnp.where(near_wet(i, left), 1, 0),
                jnp.where(lane < at + 24, mid, jnp.where(near_wet(i, right), 1, 0)),
            )
            value = jnp.where((lane >= at) & (lane < at + GROUP), sides, value)
        return value

    wet_above = lane_wet("n", "nw", "ne")
    wet_core = lane_wet("c", "w", "e")
    wet_below = lane_wet("s", "sw", "se")

    def row_bands(r, rows, above, core_value, below):
        row = r + lax.broadcasted_iota(jnp.int32, (rows, 1), 0)
        return jnp.where(row < TOP, above, jnp.where(row < TOP + SIDE, core_value, below))

    for r, rows in chunks():
        at, south = pl.ds(r, rows), pl.ds(r + 1, rows)
        z = s_ground[at, :]
        here = row_bands(r, rows, wet_above, wet_core, wet_below)
        next_row = row_bands(r + 1, rows, wet_above, wet_core, wet_below)
        open_x = (here == 1) & (pltpu.roll(here, SIDE - 1, 1) == 1)
        open_y = (here == 1) & (next_row == 1)
        s_ground_x[at, :] = jnp.where(
            open_x, jnp.maximum(z, pltpu.roll(z, SIDE - 1, 1)), CLOSED
        )
        s_ground_y[at, :] = jnp.where(open_y, jnp.maximum(z, s_ground[south, :]), CLOSED)
        hist_flow[0, at, :] = jnp.where(open_x, s_flow_x[at, :], 0.0)
        s_flow_y[at, :] = jnp.where(open_y, s_flow_y[at, :], 0.0)
        m = s_friction[at, :]
        s_friction[at, :] = (GRAV * STEP_TIME) * m * m
        hist_level[0, at, :] = s_level[at, :] + z

    def strip_step(step, carry):
        for r, rows in chunks():
            at, south = pl.ds(r, rows), pl.ds(r + 1, rows)
            e = hist_level[step, at, :]
            c = s_friction[at, :]
            hist_flow[step + 1, at, :] = face(
                hist_flow[step, at, :], e, pltpu.roll(e, SIDE - 1, 1), s_ground_x[at, :], c
            )
            s_flow_y[at, :] = face(
                s_flow_y[at, :], e, hist_level[step, south, :], s_ground_y[at, :], c
            )
        for r, rows in chunks():
            at, north = pl.ds(r, rows), pl.ds(r - 1, rows)
            qx = hist_flow[step + 1, at, :]
            hist_level[step + 1, at, :] = hist_level[step, at, :] + RATE * (
                (pltpu.roll(qx, 1, 1) - qx) + (s_flow_y[north, :] - s_flow_y[at, :])
            )
        return carry

    lax.fori_loop(0, STEPS, strip_step, 0)

    def stores(i, target):
        pieces = (level, flow_x, flow_y)
        if not leaving:
            return [
                (
                    None,
                    [
                        pltpu.make_async_copy(
                            pieces[f].at[i, core, :], outs[f].at[target], sem_out.at[i, f]
                        )
                        for f in range(3)
                    ],
                )
            ]
        return [
            (
                lax.div(target, 2) == k,
                [
                    pltpu.make_async_copy(
                        pieces[f].at[i, core, :],
                        outs[k - 1].at[lax.rem(target, 2), f],
                        sem_out.at[i, f],
                    )
                    for f in range(3)
                ],
            )
            for k in range(1, lanes)
        ]

    def each_store(i, valid, target, act):
        for chosen, copies in stores(i, target):
            @pl.when(valid if chosen is None else valid & chosen)
            def _():
                for copy in copies:
                    act(copy)

    for i in range(NT):
        valid, wet, _, target = entry(i)
        to_east = (SIDE - 1 - GROUP * i - 24) % SIDE
        to_west = (SIDE - GROUP * i - 7) % SIDE
        at_east, at_west = lane == SIDE - 1, lane == 0

        @pl.when(valid & wet)
        def _():
            flag = {name: jnp.where(near_wet(i, name), 1, 0) for name in NEAR}
            above = jnp.where(at_east, flag["n"] * flag["ne"], flag["n"])
            middle = jnp.where(at_east, flag["e"], 1)
            below = jnp.where(at_east, flag["s"] * flag["se"], flag["s"])
            for r, rows in chunks():
                at, south = pl.ds(r, rows), pl.ds(r + 1, rows)
                z = ground[i, at, :]
                z_east = jnp.where(
                    at_east, pltpu.roll(s_ground[at, :], to_east, 1), pltpu.roll(z, SIDE - 1, 1)
                )
                open_x = row_bands(r, rows, above, middle, below) == 1
                open_y = row_bands(r + 1, rows, flag["n"], 1, flag["s"]) * row_bands(
                    r, rows, flag["n"], 1, flag["s"]
                )
                open_y = open_y == 1
                ground_x[i, at, :] = jnp.where(open_x, jnp.maximum(z, z_east), CLOSED)
                ground_y[i, at, :] = jnp.where(
                    open_y, jnp.maximum(z, ground[i, south, :]), CLOSED
                )
                flow_x[i, at, :] = jnp.where(open_x, flow_x[i, at, :], 0.0)
                flow_y[i, at, :] = jnp.where(open_y, flow_y[i, at, :], 0.0)
                m = friction[i, at, :]
                friction[i, at, :] = (GRAV * STEP_TIME) * m * m
                level[i, at, :] = level[i, at, :] + z

            def tile_step(step, carry):
                for r, rows in chunks():
                    at, south = pl.ds(r, rows), pl.ds(r + 1, rows)
                    e = level[i, at, :]
                    c = friction[i, at, :]
                    e_east = jnp.where(
                        at_east,
                        pltpu.roll(hist_level[step, at, :], to_east, 1),
                        pltpu.roll(e, SIDE - 1, 1),
                    )
                    flow_x[i, at, :] = face(flow_x[i, at, :], e, e_east, ground_x[i, at, :], c)
                    flow_y[i, at, :] = face(
                        flow_y[i, at, :], e, level[i, south, :], ground_y[i, at, :], c
                    )
                for r, rows in chunks():
                    at, north = pl.ds(r, rows), pl.ds(r - 1, rows)
                    qx = flow_x[i, at, :]
                    qx_west = jnp.where(
                        at_west,
                        pltpu.roll(hist_flow[step + 1, at, :], to_west, 1),
                        pltpu.roll(qx, 1, 1),
                    )
                    level[i, at, :] = level[i, at, :] + RATE * (
                        (qx_west - qx) + (flow_y[i, north, :] - flow_y[i, at, :])
                    )
                return carry

            lax.fori_loop(0, STEPS, tile_step, 0)
            level[i, core, :] = level[i, core, :] - ground[i, core, :]

        each_store(i, valid, target, lambda copy: copy.start())

    for i in range(NT):
        valid, _, _, target = entry(i)
        each_store(i, valid, target, lambda copy: copy.wait())


def advance(table, fields, halos, base, leaving):
    lanes = len(halos)
    tile_count = fields[0].shape[0]
    if leaving:
        outs = tuple(
            jax.ShapeDtypeStruct((2, 3, SIDE, SIDE), jnp.float32) for _ in range(lanes - 1)
        )
    else:
        outs = (jax.ShapeDtypeStruct((tile_count, SIDE, SIDE), jnp.float32),) * 3
    flat = [array for group in halos for array in group]
    block = pltpu.VMEM((NT, ROWS, SIDE), jnp.float32)
    strip = pltpu.VMEM((ROWS, SIDE), jnp.float32)
    history = pltpu.VMEM((STEPS + 1, ROWS, SIDE), jnp.float32)
    cells = (NT + 1) * ROWS * SIDE * STEPS
    return pl.pallas_call(
        functools.partial(advance_kernel, lanes, base, leaving),
        name="advance_leaving" if leaving else "advance_staying",
        out_shape=outs,
        in_specs=[pl.BlockSpec(memory_space=SMEM)]
        + [pl.BlockSpec(memory_space=ANY)] * (FIELDS + 3 * lanes),
        out_specs=tuple(pl.BlockSpec(memory_space=ANY) for _ in outs),
        scratch_shapes=[
            pltpu.VMEM((lanes,) + halos[0][0].shape, jnp.float32),
            pltpu.VMEM((lanes,) + halos[0][1].shape, jnp.float32),
            pltpu.VMEM((lanes,) + halos[0][2].shape, jnp.float32),
        ]
        + [block] * 7
        + [strip] * 7
        + [history] * 2
        + [
            pltpu.SemaphoreType.DMA((3 * lanes,)),
            pltpu.SemaphoreType.DMA((NT, FIELDS)),
            pltpu.SemaphoreType.DMA((NT, 3)),
        ],
        compiler_params=pltpu.CompilerParams(vmem_limit_bytes=32 * 1024 * 1024),
        cost_estimate=pl.CostEstimate(
            flops=60 * cells, bytes_accessed=8 * NT * SIDE * SIDE * 4, transcendentals=6 * cells
        ),
    )(table, *fields, *flat)


def place_kernel(lanes, *refs):
    table = refs[0]
    received = refs[1:lanes]
    outs = refs[lanes + 3 : lanes + 6]
    sem = refs[lanes + 6]

    def each(act):
        for k in range(1, lanes):
            for j in range(2):
                slot = table[RECEIVE + 2 * k + j]

                @pl.when(slot >= 0)
                def _():
                    for f in range(3):
                        act(
                            pltpu.make_async_copy(
                                received[k - 1].at[j, f], outs[f].at[slot], sem.at[k, j, f]
                            )
                        )

    each(lambda copy: copy.start())
    each(lambda copy: copy.wait())


def place(table, received, partial_outs):
    lanes = len(received) + 1
    return pl.pallas_call(
        functools.partial(place_kernel, lanes),
        name="place_arrivals",
        out_shape=tuple(jax.ShapeDtypeStruct(o.shape, o.dtype) for o in partial_outs),
        in_specs=[pl.BlockSpec(memory_space=SMEM)] + [pl.BlockSpec(memory_space=ANY)] * (lanes + 2),
        out_specs=tuple(pl.BlockSpec(memory_space=ANY) for _ in partial_outs),
        scratch_shapes=[pltpu.SemaphoreType.DMA((lanes, 2, 3))],
        input_output_aliases={lanes: 0, lanes + 1: 1, lanes + 2: 2},
    )(table, *received, *partial_outs)


def shift_lanes(array, col_shift, sub_shift):
    cols, subs = lax.axis_size("col"), lax.axis_size("sub")
    pairs = [
        (c * subs + s, ((c + col_shift) % cols) * subs + (s + sub_shift) % subs)
        for c in range(cols)
        for s in range(subs)
    ]
    return lax.ppermute(array, ("col", "sub"), pairs)


def spread(array):
    cols, subs = lax.axis_size("col"), lax.axis_size("sub")
    out = []
    for c in range(cols):
        part = array if c == 0 else shift_lanes(array, c, 0)
        out.append(part)
        for s in range(1, subs):
            out.append(shift_lanes(part, 0, s))
    return out


def shards(
    water_depth, flow_east, flow_south, bed_level, manning_n, placed_before, placed_after, wet_tiles
):
    cols, subs, rows = lax.axis_size("col"), lax.axis_size("sub"), lax.axis_size("row")
    tile_count = water_depth.shape[0]
    fields = (water_depth, flow_east, flow_south, bed_level, manning_n)
    position = jnp.stack([lax.axis_index("row"), lax.axis_index("col"), lax.axis_index("sub")])
    table = make_table(
        (cols, subs, tile_count, placed_before.shape[0]),
        position.astype(jnp.int32),
        placed_before,
        placed_after,
        wet_tiles,
    )
    columns, first, last = pack_edges(fields, tile_count)
    above = lax.ppermute(last, "row", [(i, i + 1) for i in range(rows - 1)])
    below = lax.ppermute(first, "row", [(i + 1, i) for i in range(rows - 1)])
    halos = list(zip(spread(columns), spread(above), spread(below)))
    leaving = advance(table, fields, halos, LEAVE, True)
    received = [
        shift_lanes(leaving[k - 1], k // subs, k % subs) for k in range(1, cols * subs)
    ]
    staying = advance(table, fields, halos, STAY, False)
    return place(table, received, staying)


def solution(mesh):
    tiles = P(("basin", "row", "col", "sub"), None, None)
    return jax.shard_map(
        shards,
        mesh=mesh,
        in_specs=(tiles,) * FIELDS + (P("basin"),) * 3,
        out_specs=(tiles,) * 3,
        check_vma=False,
    )
```

```python
import functools
import math

import jax
import jax.numpy as jnp
from jax import lax
from jax.experimental import pallas as pl
from jax.experimental.pallas import tpu as pltpu
from jax.sharding import PartitionSpec as P

STEPS = 6
GRAV = 9.81
STEP_TIME = 0.5
SPACING = 5.0
RATE = 0.1
DEPTH_FLOOR = 0.3

FIELDS = 5
HALO = STEPS
PAIR = 2 * HALO
PACK_ROWS = 32
SIDE = 128
TOP = 16
ROWS = SIDE + 32
LO = 8
HI = SIDE + 24
CHUNK = 24
NT = 4
GROUP = SIDE // NT
CLOSED = 1e30
POWER = -(7.0 / 3.0) / math.log(2.0)

ENTRY = 32
NEAR = {"w": 0, "e": 1, "n": 2, "s": 3, "nw": 4, "ne": 5, "sw": 6, "se": 7}
STEP_TO = ((0, -1), (0, 1), (-1, 0), (1, 0), (-1, -1), (-1, 1), (1, -1), (1, 1))
LEAVE, STAY, RECEIVE = 0, NT * ENTRY, 2 * NT * ENTRY

SMEM = pltpu.SMEM
VMEM = pltpu.VMEM
ANY = pl.ANY


def lane_index():
    return lax.broadcasted_iota(jnp.int32, (1, SIDE), 1)


def index_kernel(
    shape, pos_ref, before_ref, after_ref, wet_ref, table, inv_before, inv_after, count
):
    cols, subs, tile_count, total = shape
    lanes = cols * subs
    row_tiles = lanes * tile_count
    tile_rows = total // row_tiles
    my_row, my_col, my_sub = pos_ref[0], pos_ref[1], pos_ref[2]
    me = my_row * lanes + my_col * subs + my_sub

    def invert(s, carry):
        for u in range(8):
            inv_before[before_ref[s * 8 + u]] = s * 8 + u
            inv_after[after_ref[s * 8 + u]] = s * 8 + u
        return carry

    lax.fori_loop(0, total // 8, invert, 0)
    for i in range(2 * NT):
        table[i * ENTRY] = 0
    for i in range(lanes * 2):
        table[RECEIVE + i] = -1
    for i in range(lanes + 1):
        count[i] = 0

    def modulo(value, size):
        return lax.rem(value + size, size)

    def entry(base, tile, source, target):
        table[base] = 1
        table[base + 1] = jnp.where(wet_ref[tile] == 1, 1, 0)
        table[base + 2] = source
        table[base + 3] = target
        row, col = lax.div(tile, row_tiles), lax.rem(tile, row_tiles)
        for n, (dr, dc) in enumerate(STEP_TO):
            r, c = row + dr, col + dc
            there = (r >= 0) & (r < tile_rows) & (c >= 0) & (c < row_tiles)
            near = jnp.where(there, tile + (dr * row_tiles + dc), tile)
            at = inv_before[near]
            lane = lax.rem(lax.div(at, tile_count), lanes)
            rel = modulo(my_col - lax.div(lane, subs), cols) * subs + modulo(
                my_sub - lax.rem(lane, subs), subs
            )
            table[base + 4 + 3 * n] = jnp.where(there & (wet_ref[near] == 1), 1, 0)
            table[base + 5 + 3 * n] = rel
            table[base + 6 + 3 * n] = lax.rem(at, tile_count)

    def own(s, carry):
        tile = before_ref[me * tile_count + s]
        device = lax.div(inv_after[tile], tile_count)
        stays = device == me

        @pl.when(stays)
        def _():
            at = jnp.minimum(count[0], NT - 1)
            count[0] = at + 1
            entry(STAY + at * ENTRY, tile, s, s)

        @pl.when(jnp.logical_not(stays))
        def _():
            lane = lax.rem(device, lanes)
            rel = modulo(lax.div(lane, subs) - my_col, cols) * subs + modulo(
                lax.rem(lane, subs) - my_sub, subs
            )
            place = jnp.minimum(count[rel], 1)
            count[rel] = place + 1
            at = jnp.minimum(count[lanes], NT - 1)
            count[lanes] = at + 1
            entry(LEAVE + at * ENTRY, tile, s, rel * 2 + place)

        return carry

    lax.fori_loop(0, tile_count, own, 0)

    for rel in range(1, lanes):
        col = modulo(my_col - rel // subs, cols)
        sub = modulo(my_sub - rel % subs, subs)
        device = my_row * lanes + col * subs + sub

        def arriving(s, found):
            at = inv_after[before_ref[device * tile_count + s]]
            mine = lax.div(at, tile_count) == me

            @pl.when(mine)
            def _():
                table[RECEIVE + rel * 2 + jnp.minimum(found, 1)] = lax.rem(at, tile_count)

            return found + jnp.where(mine, 1, 0)

        lax.fori_loop(0, tile_count, arriving, jnp.int32(0))


def make_table(shape, position, before, after, wet):
    cols, subs, _, total = shape
    size = RECEIVE + 2 * cols * subs
    return pl.pallas_call(
        functools.partial(index_kernel, shape),
        name="index_table",
        out_shape=jax.ShapeDtypeStruct((size,), jnp.int32),
        in_specs=[pl.BlockSpec(memory_space=SMEM)] * 4,
        out_specs=pl.BlockSpec(memory_space=SMEM),
        scratch_shapes=[
            SMEM((total,), jnp.int32),
            SMEM((total,), jnp.int32),
            SMEM((cols * subs + 1,), jnp.int32),
        ],
    )(position, before, after, wet)


def in_vmem(array):
    return pltpu.with_memory_space_constraint(array, VMEM)


def vmem_specs(count):
    return [pl.BlockSpec(memory_space=VMEM)] * count


def pack_kernel(*refs):
    fields = refs[:FIELDS]
    columns, first, last = refs[FIELDS:]
    lane = lane_index()
    for t in range(fields[0].shape[0]):
        packed = jnp.zeros((SIDE, SIDE), jnp.float32) if t % 2 == 0 else packed
        for f in range(FIELDS):
            at = PAIR * (t % 2 * FIELDS + f)
            moved = pltpu.roll(fields[f][t], at + HALO, 1)
            packed = jnp.where((lane >= at) & (lane < at + PAIR), moved, packed)
            first[t, HALO * f : HALO * (f + 1), :] = fields[f][t, :HALO, :]
            last[t, 2 + HALO * f : 2 + HALO * (f + 1), :] = fields[f][t, SIDE - HALO :, :]
        first[t, FIELDS * HALO :, :] = jnp.zeros((2, SIDE), jnp.float32)
        last[t, :2, :] = jnp.zeros((2, SIDE), jnp.float32)
        if t % 2:
            columns[t // 2] = packed


def pack_edges(fields, tile_count):
    rows = VMEM((tile_count, PACK_ROWS, SIDE), jnp.float32)
    return pl.pallas_call(
        pack_kernel,
        name="pack_edges",
        out_shape=(VMEM((tile_count // 2, SIDE, SIDE), jnp.float32), rows, rows),
        in_specs=vmem_specs(FIELDS),
        out_specs=tuple(vmem_specs(3)),
    )(*fields)


def face(flow, level, level_next, ground, friction):
    wetted = jnp.maximum(level, level_next) - ground
    drive = (GRAV * STEP_TIME / SPACING) * jnp.maximum(wetted, 0.0) * (level_next - level)
    power = jnp.exp2(POWER * jnp.log(jnp.maximum(wetted, DEPTH_FLOOR)))
    return (flow - drive) / (1.0 + friction * jnp.abs(flow) * power)


def chunks():
    for r in range(LO, HI, CHUNK):
        yield r, min(CHUNK, HI - r)


def row_bands(r, rows, above, middle, below):
    row = r + lax.broadcasted_iota(jnp.int32, (rows, 1), 0)
    return jnp.where(row < TOP, above, jnp.where(row < TOP + SIDE, middle, below))


def assemble(table, base, i, slot, fields, stacks, block, strip):
    halo_cols, halo_above, halo_below = stacks
    lane = lane_index()
    at = GROUP * i

    def near(name):
        place = base + 5 + 3 * NEAR[name]
        return table[place], table[place + 1]

    def inside(lo, hi):
        return (lane >= at + lo) & (lane < at + hi)

    west, east = near("w"), near("e")
    for f in range(FIELDS):
        rows = pl.ds(HALO * f, 8)

        def ends(halo, middle, left, right, out):
            mid = halo[middle[0], middle[1], rows, :]
            block[f][i, out : out + 8, :] = mid
            lower = jnp.where(lane < SIDE // 2, mid, halo[left[0], left[1], rows, :])
            upper = jnp.where(lane < SIDE // 2, halo[right[0], right[1], rows, :], mid)
            value = jnp.where(
                inside(0, 16),
                pltpu.roll(lower, (at + 8) % SIDE, 1),
                pltpu.roll(upper, (at + 24) % SIDE, 1),
            )
            if i:
                value = jnp.where(inside(0, GROUP), value, strip[f][out : out + 8, :])
            strip[f][out : out + 8, :] = value

        ends(halo_above, near("n"), near("nw"), near("ne"), LO)
        ends(halo_below, near("s"), near("sw"), near("se"), TOP + SIDE)

        def shifted(place, goal):
            source = PAIR * (lax.rem(place[1], 2) * FIELDS + f)
            shift = lax.rem(goal - source + 2 * SIDE, SIDE)
            return pltpu.roll(halo_cols[place[0], lax.div(place[1], 2)], shift, 1)

        core = fields[f][slot]
        block[f][i, TOP : TOP + SIDE, :] = core
        value = shifted(west, at + 2)
        if i:
            value = jnp.where(inside(0, 8), value, strip[f][TOP : TOP + SIDE, :])
        value = jnp.where(inside(8, 16), pltpu.roll(core, (at + 8) % SIDE, 1), value)
        value = jnp.where(inside(16, 24), pltpu.roll(core, (at + 24) % SIDE, 1), value)
        value = jnp.where(inside(24, GROUP), shifted(east, at + 24 - HALO), value)
        strip[f][TOP : TOP + SIDE, :] = value


def prepare_strip(near_wet, strip, ground_x, ground_y):
    level, flow_x, flow_y, ground, friction = strip
    lane = lane_index()

    def lane_wet(center, left, right):
        value = jnp.zeros((1, SIDE), jnp.int32)
        for i in range(NT):
            at = GROUP * i
            middle = near_wet(i, center) if center else 1
            sides = jnp.where(
                lane < at + 8,
                near_wet(i, left),
                jnp.where(lane < at + 24, middle, near_wet(i, right)),
            )
            value = jnp.where((lane >= at) & (lane < at + GROUP), sides, value)
        return value

    bands = (lane_wet("n", "nw", "ne"), lane_wet(None, "w", "e"), lane_wet("s", "sw", "se"))
    for r, rows in chunks():
        at, south = pl.ds(r, rows), pl.ds(r + 1, rows)
        z = ground[at, :]
        here, next_row = row_bands(r, rows, *bands), row_bands(r + 1, rows, *bands)
        open_x = (here == 1) & (pltpu.roll(here, SIDE - 1, 1) == 1)
        open_y = (here == 1) & (next_row == 1)
        z_east = pltpu.roll(z, SIDE - 1, 1)
        ground_x[at, :] = jnp.where(open_x, jnp.maximum(z, z_east), CLOSED)
        ground_y[at, :] = jnp.where(open_y, jnp.maximum(z, ground[south, :]), CLOSED)
        flow_x[at, :] = jnp.where(open_x, flow_x[at, :], 0.0)
        flow_y[at, :] = jnp.where(open_y, flow_y[at, :], 0.0)
        friction[at, :] = (GRAV * STEP_TIME) * friction[at, :] * friction[at, :]
        level[at, :] = level[at, :] + z


def prepare_tile(near_wet, i, block, ground_x, ground_y, strip_ground):
    level, flow_x, flow_y, ground, friction = block
    lane = lane_index()
    last = lane == SIDE - 1
    n, e, s = near_wet(i, "n"), near_wet(i, "e"), near_wet(i, "s")
    bands = (
        jnp.where(last, n * near_wet(i, "ne"), n),
        jnp.where(last, e, 1),
        jnp.where(last, s * near_wet(i, "se"), s),
    )
    for r, rows in chunks():
        at, south = pl.ds(r, rows), pl.ds(r + 1, rows)
        z = ground[i, at, :]
        z_east = jnp.where(
            last, pltpu.roll(strip_ground[at, :], to_east(i), 1), pltpu.roll(z, SIDE - 1, 1)
        )
        open_x = row_bands(r, rows, *bands) == 1
        open_y = (row_bands(r + 1, rows, n, 1, s) == 1) & (row_bands(r, rows, n, 1, s) == 1)
        ground_x[i, at, :] = jnp.where(open_x, jnp.maximum(z, z_east), CLOSED)
        ground_y[i, at, :] = jnp.where(open_y, jnp.maximum(z, ground[i, south, :]), CLOSED)
        flow_x[i, at, :] = jnp.where(open_x, flow_x[i, at, :], 0.0)
        flow_y[i, at, :] = jnp.where(open_y, flow_y[i, at, :], 0.0)
        friction[i, at, :] = (GRAV * STEP_TIME) * friction[i, at, :] * friction[i, at, :]
        level[i, at, :] = level[i, at, :] + z


def to_east(i):
    return (SIDE - 1 - GROUP * i - 24) % SIDE


def to_west(i):
    return (SIDE - GROUP * i - 7) % SIDE


def advance_kernel(lanes, base, leaving, *refs):
    table = refs[0]
    fields = refs[1 : 1 + FIELDS]
    halos = refs[1 + FIELDS : 1 + FIELDS + 3 * lanes]
    n_out = lanes - 1 if leaving else 3
    outs = refs[1 + FIELDS + 3 * lanes : 1 + FIELDS + 3 * lanes + n_out]
    (
        halo_cols, halo_above, halo_below,
        level, flow_x, flow_y, ground, friction, ground_x, ground_y,
        s_level, s_flow_x, s_flow_y, s_ground, s_friction, s_ground_x, s_ground_y,
        sem_out,
    ) = refs[1 + FIELDS + 3 * lanes + n_out :]
    block = (level, flow_x, flow_y, ground, friction)
    strip = (s_level, s_flow_x, s_flow_y, s_ground, s_friction)
    stacks = (halo_cols, halo_above, halo_below)
    lane = lane_index()
    last, first = lane == SIDE - 1, lane == 0
    core = pl.ds(TOP, SIDE)

    def entry(i):
        at = base + i * ENTRY
        return table[at + 1], table[at + 2], table[at + 3]

    def near_wet(i, name):
        return table[base + i * ENTRY + 4 + 3 * NEAR[name]]

    for k in range(lanes):
        for n in range(3):
            stacks[n][k] = halos[3 * k + n][...]
    for i in range(NT):
        assemble(table, base + i * ENTRY, i, entry(i)[1], fields, stacks, block, strip)
    prepare_strip(near_wet, strip, s_ground_x, s_ground_y)
    for i in range(NT):
        prepare_tile(near_wet, i, block, ground_x, ground_y, s_ground)

    def step(_, carry):
        for r, rows in chunks():
            at, south = pl.ds(r, rows), pl.ds(r + 1, rows)
            e, c = s_level[at, :], s_friction[at, :]
            e_east = pltpu.roll(e, SIDE - 1, 1)
            s_flow_x[at, :] = face(s_flow_x[at, :], e, e_east, s_ground_x[at, :], c)
            s_flow_y[at, :] = face(s_flow_y[at, :], e, s_level[south, :], s_ground_y[at, :], c)
        for i in range(NT):
            for r, rows in chunks():
                at, south = pl.ds(r, rows), pl.ds(r + 1, rows)
                e, c = level[i, at, :], friction[i, at, :]
                e_east = jnp.where(
                    last, pltpu.roll(s_level[at, :], to_east(i), 1), pltpu.roll(e, SIDE - 1, 1)
                )
                flow_x[i, at, :] = face(flow_x[i, at, :], e, e_east, ground_x[i, at, :], c)
                flow_y[i, at, :] = face(
                    flow_y[i, at, :], e, level[i, south, :], ground_y[i, at, :], c
                )
        for r, rows in chunks():
            at, north = pl.ds(r, rows), pl.ds(r - 1, rows)
            qx = s_flow_x[at, :]
            s_level[at, :] = s_level[at, :] + RATE * (
                (pltpu.roll(qx, 1, 1) - qx) + (s_flow_y[north, :] - s_flow_y[at, :])
            )
        for i in range(NT):
            for r, rows in chunks():
                at, north = pl.ds(r, rows), pl.ds(r - 1, rows)
                qx = flow_x[i, at, :]
                qx_west = jnp.where(
                    first, pltpu.roll(s_flow_x[at, :], to_west(i), 1), pltpu.roll(qx, 1, 1)
                )
                level[i, at, :] = level[i, at, :] + RATE * (
                    (qx_west - qx) + (flow_y[i, north, :] - flow_y[i, at, :])
                )
        return carry

    lax.fori_loop(0, STEPS, step, 0)

    for i in range(NT):
        wet, slot, _ = entry(i)
        depth = level[i, core, :] - ground[i, core, :]
        level[i, core, :] = jnp.where(wet == 1, depth, fields[0][slot])
        flow_x[i, core, :] = jnp.where(wet == 1, flow_x[i, core, :], fields[1][slot])
        flow_y[i, core, :] = jnp.where(wet == 1, flow_y[i, core, :], fields[2][slot])

    results = (level, flow_x, flow_y)
    if leaving:
        for i in range(NT):
            target = entry(i)[2]
            for k in range(1, lanes):
                @pl.when(lax.div(target, 2) == k)
                def _():
                    for f in range(3):
                        outs[k - 1][lax.rem(target, 2), f] = results[f][i, core, :]

    else:
        copies = [
            pltpu.make_async_copy(
                results[f].at[i, core, :], outs[f].at[entry(i)[2]], sem_out.at[i, f]
            )
            for i in range(NT)
            for f in range(3)
        ]
        for copy in copies:
            copy.start()
        for copy in copies:
            copy.wait()


def advance(table, fields, halos, base, leaving):
    lanes = len(halos)
    if leaving:
        outs = (VMEM((2, 3, SIDE, SIDE), jnp.float32),) * (lanes - 1)
        out_specs = vmem_specs(lanes - 1)
    else:
        outs = (jax.ShapeDtypeStruct(fields[0].shape, jnp.float32),) * 3
        out_specs = [pl.BlockSpec(memory_space=ANY)] * 3
    flat = [array for group in halos for array in group]
    block = VMEM((NT, ROWS, SIDE), jnp.float32)
    strip = VMEM((ROWS, SIDE), jnp.float32)
    cells = (NT + 1) * ROWS * SIDE * STEPS
    return pl.pallas_call(
        functools.partial(advance_kernel, lanes, base, leaving),
        name="advance_leaving" if leaving else "advance_staying",
        out_shape=outs,
        in_specs=[pl.BlockSpec(memory_space=SMEM)] + vmem_specs(FIELDS + 3 * lanes),
        out_specs=tuple(out_specs),
        scratch_shapes=[VMEM((lanes,) + halos[0][n].shape, jnp.float32) for n in range(3)]
        + [block] * 7
        + [strip] * 7
        + [pltpu.SemaphoreType.DMA((NT, 3))],
        compiler_params=pltpu.CompilerParams(vmem_limit_bytes=16 * 1024 * 1024),
        cost_estimate=pl.CostEstimate(
            flops=60 * cells, bytes_accessed=8 * NT * SIDE * SIDE * 4, transcendentals=6 * cells
        ),
    )(table, *fields, *flat)


def place_kernel(lanes, *refs):
    table = refs[0]
    received = refs[1:lanes]
    outs = refs[lanes + 3 : lanes + 6]
    sem = refs[lanes + 6]

    def each(act):
        for k in range(1, lanes):
            for j in range(2):
                slot = table[RECEIVE + 2 * k + j]

                @pl.when(slot >= 0)
                def _():
                    for f in range(3):
                        act(
                            pltpu.make_async_copy(
                                received[k - 1].at[j, f], outs[f].at[slot], sem.at[k, j, f]
                            )
                        )

    each(lambda copy: copy.start())
    each(lambda copy: copy.wait())


def place(table, received, partial_outs):
    lanes = len(received) + 1
    return pl.pallas_call(
        functools.partial(place_kernel, lanes),
        name="place_arrivals",
        out_shape=tuple(jax.ShapeDtypeStruct(o.shape, o.dtype) for o in partial_outs),
        in_specs=[pl.BlockSpec(memory_space=SMEM)]
        + vmem_specs(lanes - 1)
        + [pl.BlockSpec(memory_space=ANY)] * 3,
        out_specs=tuple(pl.BlockSpec(memory_space=ANY) for _ in partial_outs),
        scratch_shapes=[pltpu.SemaphoreType.DMA((lanes, 2, 3))],
        input_output_aliases={lanes: 0, lanes + 1: 1, lanes + 2: 2},
    )(table, *received, *partial_outs)


def shift_lanes(array, col_shift, sub_shift):
    cols, subs = lax.axis_size("col"), lax.axis_size("sub")
    pairs = [
        (c * subs + s, ((c + col_shift) % cols) * subs + (s + sub_shift) % subs)
        for c in range(cols)
        for s in range(subs)
    ]
    return lax.ppermute(array, ("col", "sub"), pairs)


def spread(array):
    cols, subs = lax.axis_size("col"), lax.axis_size("sub")
    out = []
    for c in range(cols):
        part = array if c == 0 else shift_lanes(array, c, 0)
        out.append(part)
        for s in range(1, subs):
            out.append(shift_lanes(part, 0, s))
    return out


def shards(
    water_depth, flow_east, flow_south, bed_level, manning_n, placed_before, placed_after, wet_tiles
):
    cols, subs, rows = lax.axis_size("col"), lax.axis_size("sub"), lax.axis_size("row")
    tile_count = water_depth.shape[0]
    fields = [
        in_vmem(field) for field in (water_depth, flow_east, flow_south, bed_level, manning_n)
    ]
    position = jnp.stack([lax.axis_index("row"), lax.axis_index("col"), lax.axis_index("sub")])
    columns, first, last = pack_edges(fields, tile_count)
    above = lax.ppermute(last, "row", [(i, i + 1) for i in range(rows - 1)])
    below = lax.ppermute(first, "row", [(i + 1, i) for i in range(rows - 1)])
    table = make_table(
        (cols, subs, tile_count, placed_before.shape[0]),
        position.astype(jnp.int32),
        placed_before,
        placed_after,
        wet_tiles,
    )
    above, below, table = lax.optimization_barrier((above, below, table))
    halos = [
        tuple(in_vmem(part) for part in group)
        for group in zip(spread(columns), spread(above), spread(below))
    ]
    leaving = advance(table, fields, halos, LEAVE, True)
    received = [
        in_vmem(shift_lanes(leaving[k - 1], k // subs, k % subs)) for k in range(1, cols * subs)
    ]
    staying = advance(table, fields, halos, STAY, False)
    return place(table, received, staying)


def solution(mesh):
    tiles = P(("basin", "row", "col", "sub"), None, None)
    return jax.shard_map(
        shards,
        mesh=mesh,
        in_specs=(tiles,) * FIELDS + (P("basin"),) * 3,
        out_specs=(tiles,) * 3,
        check_vma=False,
    )
```

```python
import functools
import math

import jax
import jax.numpy as jnp
from jax import lax
from jax.experimental import pallas as pl
from jax.experimental.pallas import tpu as pltpu
from jax.sharding import PartitionSpec as P

STEPS = 6
GRAV = 9.81
STEP_TIME = 0.5
SPACING = 5.0
RATE = 0.1
DEPTH_FLOOR = 0.3

FIELDS = 5
HALO = STEPS
PAIR = 2 * HALO
PACK_ROWS = 32
SIDE = 128
TOP = 16
ROWS = SIDE + 32
LO = 8
HI = SIDE + 24
CHUNK = 24
NT = 4
GROUP = SIDE // NT
CLOSED = 1e30
POWER = -(7.0 / 3.0) / math.log(2.0)

ENTRY = 32
NEAR = {"w": 0, "e": 1, "n": 2, "s": 3, "nw": 4, "ne": 5, "sw": 6, "se": 7}
STEP_TO = ((0, -1), (0, 1), (-1, 0), (1, 0), (-1, -1), (-1, 1), (1, -1), (1, 1))
LEAVE, STAY, RECEIVE = 0, NT * ENTRY, 2 * NT * ENTRY

SMEM = pltpu.SMEM
VMEM = pltpu.VMEM
ANY = pl.ANY
SMALL = pltpu.CompilerParams(vmem_limit_bytes=2 * 1024 * 1024)


def lane_index():
    return lax.broadcasted_iota(jnp.int32, (1, SIDE), 1)


def divide(value, size):
    if size & (size - 1):
        return lax.div(value, size)
    return lax.shift_right_logical(value, size.bit_length() - 1)


def remainder(value, size):
    if size & (size - 1):
        return lax.rem(value, size)
    return value & (size - 1)


def index_kernel(shape, before_ref, after_ref, wet_ref, table, inv_before, inv_after, count):
    cols, subs, tile_count, total = shape
    lanes = cols * subs
    row_tiles = lanes * tile_count
    tile_rows = total // row_tiles
    my_row, my_col, my_sub = (lax.axis_index(name) for name in ("row", "col", "sub"))
    me = my_row * lanes + my_col * subs + my_sub
    spare = RECEIVE + 2 * lanes

    def invert(s, carry):
        for u in range(16):
            inv_before[before_ref[s * 16 + u]] = s * 16 + u
            inv_after[after_ref[s * 16 + u]] = s * 16 + u
        return carry

    lax.fori_loop(0, total // 16, invert, 0)
    for i in range(lanes * 2):
        table[RECEIVE + i] = -1
    for i in range(lanes + 1):
        count[i] = 0

    def relative(lane, sign):
        col = remainder(sign * (divide(lane, subs) - my_col) + cols, cols)
        sub = remainder(sign * (remainder(lane, subs) - my_sub) + subs, subs)
        return col * subs + sub

    def own(s, carry):
        tile = before_ref[me * tile_count + s]
        device = divide(inv_after[tile], tile_count)
        stays = device == me
        to = relative(remainder(device, lanes), 1)
        nth = count[to]
        count[to] = nth + 1
        left = count[lanes]
        count[lanes] = left + jnp.where(stays, 0, 1)
        base = jnp.where(
            stays,
            STAY + jnp.minimum(nth, NT - 1) * ENTRY,
            LEAVE + jnp.minimum(left, NT - 1) * ENTRY,
        )
        table[base + 1] = wet_ref[tile]
        table[base + 2] = s
        table[base + 3] = jnp.where(stays, s, to * 2 + jnp.minimum(nth, 1))
        row, col = divide(tile, row_tiles), remainder(tile, row_tiles)
        for n, (dr, dc) in enumerate(STEP_TO):
            r, c = row + dr, col + dc
            there = (r >= 0) & (r < tile_rows) & (c >= 0) & (c < row_tiles)
            near = jnp.where(there, tile + (dr * row_tiles + dc), tile)
            at = inv_before[near]
            table[base + 4 + 3 * n] = jnp.where(there, wet_ref[near], 0)
            table[base + 5 + 3 * n] = relative(remainder(divide(at, tile_count), lanes), -1)
            table[base + 6 + 3 * n] = remainder(at, tile_count)
        return carry

    lax.fori_loop(0, tile_count, own, 0)

    for rel in range(1, lanes):
        col = remainder(my_col + (cols - rel // subs), cols)
        sub = remainder(my_sub + (subs - rel % subs), subs)
        device = my_row * lanes + col * subs + sub
        found = jnp.int32(0)
        for s in range(tile_count):
            at = inv_after[before_ref[device * tile_count + s]]
            mine = divide(at, tile_count) == me
            place = RECEIVE + rel * 2 + jnp.minimum(found, 1)
            table[jnp.where(mine, place, spare)] = remainder(at, tile_count)
            found = found + jnp.where(mine, 1, 0)


def make_table(shape, before, after, wet):
    cols, subs, _, total = shape
    return pl.pallas_call(
        functools.partial(index_kernel, shape),
        name="index_table",
        out_shape=SMEM((RECEIVE + 2 * cols * subs + 1,), jnp.int32),
        in_specs=[pl.BlockSpec(memory_space=SMEM)] * 3,
        out_specs=pl.BlockSpec(memory_space=SMEM),
        scratch_shapes=[
            SMEM((total,), jnp.int32),
            SMEM((total,), jnp.int32),
            SMEM((cols * subs + 1,), jnp.int32),
        ],
        compiler_params=SMALL,
    )(before, after, wet)


def in_vmem(array):
    return pltpu.with_memory_space_constraint(array, VMEM)


def vmem_specs(count):
    return [pl.BlockSpec(memory_space=VMEM)] * count


def load_kernel(*refs):
    sources, refs = refs[:FIELDS], refs[FIELDS:]
    fields, (columns, first, last, sem) = refs[:FIELDS], refs[FIELDS:]
    lane = lane_index()
    copies = [
        pltpu.make_async_copy(sources[f], fields[f], sem.at[f]) for f in range(FIELDS)
    ]
    for copy in copies:
        copy.start()
    tile_count = fields[0].shape[0]
    for t in range(tile_count):
        first[t, FIELDS * HALO :, :] = jnp.zeros((2, SIDE), jnp.float32)
        last[t, :2, :] = jnp.zeros((2, SIDE), jnp.float32)
    for f in range(FIELDS):
        copies[f].wait()
        for t in range(0, tile_count, 2):
            packed = columns[t // 2] if f else jnp.zeros((SIDE, SIDE), jnp.float32)
            for u in range(2):
                at = PAIR * (u * FIELDS + f)
                moved = pltpu.roll(fields[f][t + u], at + HALO, 1)
                packed = jnp.where((lane >= at) & (lane < at + PAIR), moved, packed)
            columns[t // 2] = packed
        for t in range(tile_count):
            first[t, HALO * f : HALO * (f + 1), :] = fields[f][t, :HALO, :]
            last[t, 2 + HALO * f : 2 + HALO * (f + 1), :] = fields[f][t, SIDE - HALO :, :]


def load(arrays):
    tile_count = arrays[0].shape[0]
    rows = VMEM((tile_count, PACK_ROWS, SIDE), jnp.float32)
    outs = [VMEM(array.shape, array.dtype) for array in arrays]
    outs += [VMEM((tile_count // 2, SIDE, SIDE), jnp.float32), rows, rows]
    return pl.pallas_call(
        load_kernel,
        name="load_and_pack",
        out_shape=tuple(outs),
        in_specs=[pl.BlockSpec(memory_space=pltpu.HBM)] * FIELDS,
        out_specs=tuple(vmem_specs(len(outs))),
        scratch_shapes=[pltpu.SemaphoreType.DMA((FIELDS,))],
        compiler_params=SMALL,
    )(*[pltpu.with_memory_space_constraint(array, pltpu.HBM) for array in arrays])


def face(flow, level, level_next, ground, friction):
    wetted = jnp.maximum(level, level_next) - ground
    drive = (GRAV * STEP_TIME / SPACING) * jnp.maximum(wetted, 0.0) * (level_next - level)
    power = jnp.exp2(POWER * jnp.log(jnp.maximum(wetted, DEPTH_FLOOR)))
    return (flow - drive) / (1.0 + friction * jnp.abs(flow) * power)


def chunks():
    for r in range(LO, HI, CHUNK):
        yield r, min(CHUNK, HI - r)


def row_bands(r, rows, above, middle, below):
    row = r + lax.broadcasted_iota(jnp.int32, (rows, 1), 0)
    return jnp.where(row < TOP, above, jnp.where(row < TOP + SIDE, middle, below))


def assemble(table, base, i, slot, fields, stacks, block, strip):
    halo_cols, halo_above, halo_below = stacks
    lane = lane_index()
    at = GROUP * i

    def near(name):
        place = base + 5 + 3 * NEAR[name]
        return table[place], table[place + 1]

    def inside(lo, hi):
        return (lane >= at + lo) & (lane < at + hi)

    west, east = near("w"), near("e")
    for f in range(FIELDS):
        rows = pl.ds(HALO * f, 8)

        def ends(halo, middle, left, right, out):
            mid = halo[middle[0], middle[1], rows, :]
            block[f][i, out : out + 8, :] = mid
            lower = jnp.where(lane < SIDE // 2, mid, halo[left[0], left[1], rows, :])
            upper = jnp.where(lane < SIDE // 2, halo[right[0], right[1], rows, :], mid)
            value = jnp.where(
                inside(0, 16),
                pltpu.roll(lower, (at + 8) % SIDE, 1),
                pltpu.roll(upper, (at + 24) % SIDE, 1),
            )
            if i:
                value = jnp.where(inside(0, GROUP), value, strip[f][out : out + 8, :])
            strip[f][out : out + 8, :] = value

        ends(halo_above, near("n"), near("nw"), near("ne"), LO)
        ends(halo_below, near("s"), near("sw"), near("se"), TOP + SIDE)

        def shifted(place, goal):
            source = PAIR * (lax.rem(place[1], 2) * FIELDS + f)
            shift = lax.rem(goal - source + 2 * SIDE, SIDE)
            return pltpu.roll(halo_cols[place[0], lax.div(place[1], 2)], shift, 1)

        core = fields[f][slot]
        block[f][i, TOP : TOP + SIDE, :] = core
        value = shifted(west, at + 2)
        if i:
            value = jnp.where(inside(0, 8), value, strip[f][TOP : TOP + SIDE, :])
        value = jnp.where(inside(8, 16), pltpu.roll(core, (at + 8) % SIDE, 1), value)
        value = jnp.where(inside(16, 24), pltpu.roll(core, (at + 24) % SIDE, 1), value)
        value = jnp.where(inside(24, GROUP), shifted(east, at + 24 - HALO), value)
        strip[f][TOP : TOP + SIDE, :] = value


def prepare_strip(near_wet, strip, ground_x, ground_y):
    level, flow_x, flow_y, ground, friction = strip
    lane = lane_index()

    def lane_wet(center, left, right):
        value = jnp.zeros((1, SIDE), jnp.int32)
        for i in range(NT):
            at = GROUP * i
            middle = near_wet(i, center) if center else 1
            sides = jnp.where(
                lane < at + 8,
                near_wet(i, left),
                jnp.where(lane < at + 24, middle, near_wet(i, right)),
            )
            value = jnp.where((lane >= at) & (lane < at + GROUP), sides, value)
        return value

    bands = (lane_wet("n", "nw", "ne"), lane_wet(None, "w", "e"), lane_wet("s", "sw", "se"))
    for r, rows in chunks():
        at, south = pl.ds(r, rows), pl.ds(r + 1, rows)
        z = ground[at, :]
        here, next_row = row_bands(r, rows, *bands), row_bands(r + 1, rows, *bands)
        open_x = (here == 1) & (pltpu.roll(here, SIDE - 1, 1) == 1)
        open_y = (here == 1) & (next_row == 1)
        z_east = pltpu.roll(z, SIDE - 1, 1)
        ground_x[at, :] = jnp.where(open_x, jnp.maximum(z, z_east), CLOSED)
        ground_y[at, :] = jnp.where(open_y, jnp.maximum(z, ground[south, :]), CLOSED)
        flow_x[at, :] = jnp.where(open_x, flow_x[at, :], 0.0)
        flow_y[at, :] = jnp.where(open_y, flow_y[at, :], 0.0)
        friction[at, :] = (GRAV * STEP_TIME) * friction[at, :] * friction[at, :]
        level[at, :] = level[at, :] + z


def prepare_tile(near_wet, i, block, ground_x, ground_y, strip_ground):
    level, flow_x, flow_y, ground, friction = block
    lane = lane_index()
    last = lane == SIDE - 1
    n, e, s = near_wet(i, "n"), near_wet(i, "e"), near_wet(i, "s")
    bands = (
        jnp.where(last, n * near_wet(i, "ne"), n),
        jnp.where(last, e, 1),
        jnp.where(last, s * near_wet(i, "se"), s),
    )
    for r, rows in chunks():
        at, south = pl.ds(r, rows), pl.ds(r + 1, rows)
        z = ground[i, at, :]
        z_east = jnp.where(
            last, pltpu.roll(strip_ground[at, :], to_east(i), 1), pltpu.roll(z, SIDE - 1, 1)
        )
        open_x = row_bands(r, rows, *bands) == 1
        open_y = (row_bands(r + 1, rows, n, 1, s) == 1) & (row_bands(r, rows, n, 1, s) == 1)
        ground_x[i, at, :] = jnp.where(open_x, jnp.maximum(z, z_east), CLOSED)
        ground_y[i, at, :] = jnp.where(open_y, jnp.maximum(z, ground[i, south, :]), CLOSED)
        flow_x[i, at, :] = jnp.where(open_x, flow_x[i, at, :], 0.0)
        flow_y[i, at, :] = jnp.where(open_y, flow_y[i, at, :], 0.0)
        friction[i, at, :] = (GRAV * STEP_TIME) * friction[i, at, :] * friction[i, at, :]
        level[i, at, :] = level[i, at, :] + z


def to_east(i):
    return (SIDE - 1 - GROUP * i - 24) % SIDE


def to_west(i):
    return (SIDE - GROUP * i - 7) % SIDE


def advance_kernel(lanes, base, leaving, *refs):
    table = refs[0]
    fields = refs[1 : 1 + FIELDS]
    halos = refs[1 + FIELDS : 1 + FIELDS + 3 * lanes]
    n_out = lanes - 1 if leaving else 3
    outs = refs[1 + FIELDS + 3 * lanes : 1 + FIELDS + 3 * lanes + n_out]
    (
        halo_cols, halo_above, halo_below,
        level, flow_x, flow_y, ground, friction, ground_x, ground_y,
        s_level, s_flow_x, s_flow_y, s_ground, s_friction, s_ground_x, s_ground_y,
        sem_out,
    ) = refs[1 + FIELDS + 3 * lanes + n_out :]
    block = (level, flow_x, flow_y, ground, friction)
    strip = (s_level, s_flow_x, s_flow_y, s_ground, s_friction)
    stacks = (halo_cols, halo_above, halo_below)
    lane = lane_index()
    last, first = lane == SIDE - 1, lane == 0
    core = pl.ds(TOP, SIDE)

    def entry(i):
        at = base + i * ENTRY
        return table[at + 1], table[at + 2], table[at + 3]

    def near_wet(i, name):
        return table[base + i * ENTRY + 4 + 3 * NEAR[name]]

    for k in range(lanes):
        for n in range(3):
            stacks[n][k] = halos[3 * k + n][...]
    for i in range(NT):
        assemble(table, base + i * ENTRY, i, entry(i)[1], fields, stacks, block, strip)
    prepare_strip(near_wet, strip, s_ground_x, s_ground_y)
    for i in range(NT):
        prepare_tile(near_wet, i, block, ground_x, ground_y, s_ground)

    def step(_, carry):
        for r, rows in chunks():
            at, south = pl.ds(r, rows), pl.ds(r + 1, rows)
            e, c = s_level[at, :], s_friction[at, :]
            e_east = pltpu.roll(e, SIDE - 1, 1)
            s_flow_x[at, :] = face(s_flow_x[at, :], e, e_east, s_ground_x[at, :], c)
            s_flow_y[at, :] = face(s_flow_y[at, :], e, s_level[south, :], s_ground_y[at, :], c)
        for i in range(NT):
            for r, rows in chunks():
                at, south = pl.ds(r, rows), pl.ds(r + 1, rows)
                e, c = level[i, at, :], friction[i, at, :]
                e_east = jnp.where(
                    last, pltpu.roll(s_level[at, :], to_east(i), 1), pltpu.roll(e, SIDE - 1, 1)
                )
                flow_x[i, at, :] = face(flow_x[i, at, :], e, e_east, ground_x[i, at, :], c)
                flow_y[i, at, :] = face(
                    flow_y[i, at, :], e, level[i, south, :], ground_y[i, at, :], c
                )
        for r, rows in chunks():
            at, north = pl.ds(r, rows), pl.ds(r - 1, rows)
            qx = s_flow_x[at, :]
            s_level[at, :] = s_level[at, :] + RATE * (
                (pltpu.roll(qx, 1, 1) - qx) + (s_flow_y[north, :] - s_flow_y[at, :])
            )
        for i in range(NT):
            for r, rows in chunks():
                at, north = pl.ds(r, rows), pl.ds(r - 1, rows)
                qx = flow_x[i, at, :]
                qx_west = jnp.where(
                    first, pltpu.roll(s_flow_x[at, :], to_west(i), 1), pltpu.roll(qx, 1, 1)
                )
                level[i, at, :] = level[i, at, :] + RATE * (
                    (qx_west - qx) + (flow_y[i, north, :] - flow_y[i, at, :])
                )
        return carry

    lax.fori_loop(0, STEPS, step, 0)

    for i in range(NT):
        wet, slot, _ = entry(i)
        depth = level[i, core, :] - ground[i, core, :]
        level[i, core, :] = jnp.where(wet == 1, depth, fields[0][slot])
        flow_x[i, core, :] = jnp.where(wet == 1, flow_x[i, core, :], fields[1][slot])
        flow_y[i, core, :] = jnp.where(wet == 1, flow_y[i, core, :], fields[2][slot])

    results = (level, flow_x, flow_y)
    if leaving:
        for i in range(NT):
            target = entry(i)[2]
            for k in range(1, lanes):
                @pl.when(lax.div(target, 2) == k)
                def _():
                    for f in range(3):
                        outs[k - 1][lax.rem(target, 2), f] = results[f][i, core, :]

    else:
        copies = [
            pltpu.make_async_copy(
                results[f].at[i, core, :], outs[f].at[entry(i)[2]], sem_out.at[i, f]
            )
            for i in range(NT)
            for f in range(3)
        ]
        for copy in copies:
            copy.start()
        for copy in copies:
            copy.wait()


def advance(table, fields, halos, base, leaving):
    lanes = len(halos)
    if leaving:
        outs = (VMEM((2, 3, SIDE, SIDE), jnp.float32),) * (lanes - 1)
        out_specs = vmem_specs(lanes - 1)
    else:
        outs = (jax.ShapeDtypeStruct(fields[0].shape, jnp.float32),) * 3
        out_specs = [pl.BlockSpec(memory_space=ANY)] * 3
    flat = [array for group in halos for array in group]
    block = VMEM((NT, ROWS, SIDE), jnp.float32)
    strip = VMEM((ROWS, SIDE), jnp.float32)
    cells = (NT + 1) * ROWS * SIDE * STEPS
    return pl.pallas_call(
        functools.partial(advance_kernel, lanes, base, leaving),
        name="advance_leaving" if leaving else "advance_staying",
        out_shape=outs,
        in_specs=[pl.BlockSpec(memory_space=SMEM)] + vmem_specs(FIELDS + 3 * lanes),
        out_specs=tuple(out_specs),
        scratch_shapes=[VMEM((lanes,) + halos[0][n].shape, jnp.float32) for n in range(3)]
        + [block] * 7
        + [strip] * 7
        + [pltpu.SemaphoreType.DMA((NT, 3))],
        compiler_params=pltpu.CompilerParams(vmem_limit_bytes=12 * 1024 * 1024),
        cost_estimate=pl.CostEstimate(
            flops=60 * cells, bytes_accessed=8 * NT * SIDE * SIDE * 4, transcendentals=6 * cells
        ),
    )(table, *fields, *flat)


def place_kernel(lanes, *refs):
    table = refs[0]
    received = refs[1:lanes]
    outs = refs[lanes + 3 : lanes + 6]
    sem = refs[lanes + 6]

    def each(act):
        for k in range(1, lanes):
            for j in range(2):
                slot = table[RECEIVE + 2 * k + j]

                @pl.when(slot >= 0)
                def _():
                    for f in range(3):
                        act(
                            pltpu.make_async_copy(
                                received[k - 1].at[j, f], outs[f].at[slot], sem.at[k, j, f]
                            )
                        )

    each(lambda copy: copy.start())
    each(lambda copy: copy.wait())


def place(table, received, partial_outs):
    lanes = len(received) + 1
    return pl.pallas_call(
        functools.partial(place_kernel, lanes),
        name="place_arrivals",
        out_shape=tuple(jax.ShapeDtypeStruct(o.shape, o.dtype) for o in partial_outs),
        in_specs=[pl.BlockSpec(memory_space=SMEM)]
        + vmem_specs(lanes - 1)
        + [pl.BlockSpec(memory_space=ANY)] * 3,
        out_specs=tuple(pl.BlockSpec(memory_space=ANY) for _ in partial_outs),
        scratch_shapes=[pltpu.SemaphoreType.DMA((lanes, 2, 3))],
        input_output_aliases={lanes: 0, lanes + 1: 1, lanes + 2: 2},
        compiler_params=SMALL,
    )(table, *received, *partial_outs)


def shift_lanes(array, col_shift, sub_shift):
    cols, subs = lax.axis_size("col"), lax.axis_size("sub")
    pairs = [
        (c * subs + s, ((c + col_shift) % cols) * subs + (s + sub_shift) % subs)
        for c in range(cols)
        for s in range(subs)
    ]
    return lax.ppermute(array, ("col", "sub"), pairs)


def over_cols(array):
    return [array] + [shift_lanes(array, c, 0) for c in range(1, lax.axis_size("col"))]


def over_subs(parts):
    subs = lax.axis_size("sub")
    return [
        in_vmem(part if s == 0 else shift_lanes(part, 0, s)) for part in parts for s in range(subs)
    ]


def shards(
    water_depth, flow_east, flow_south, bed_level, manning_n, placed_before, placed_after, wet_tiles
):
    cols, subs, rows = lax.axis_size("col"), lax.axis_size("sub"), lax.axis_size("row")
    tile_count = water_depth.shape[0]
    *fields, columns, first, last = load(
        (water_depth, flow_east, flow_south, bed_level, manning_n)
    )
    fields = [in_vmem(field) for field in fields]
    columns = over_cols(columns)
    above = over_cols(lax.ppermute(last, "row", [(i, i + 1) for i in range(rows - 1)]))
    below = over_cols(lax.ppermute(first, "row", [(i + 1, i) for i in range(rows - 1)]))
    table = make_table(
        (cols, subs, tile_count, placed_before.shape[0]), placed_before, placed_after, wet_tiles
    )
    above[1:], below[1:], table = lax.optimization_barrier((above[1:], below[1:], table))
    table = pltpu.with_memory_space_constraint(table, SMEM)
    halos = list(zip(over_subs(columns), over_subs(above), over_subs(below)))
    leaving = advance(table, fields, halos, LEAVE, True)
    received = [
        in_vmem(shift_lanes(leaving[k - 1], k // subs, k % subs)) for k in range(1, cols * subs)
    ]
    staying = advance(table, fields, halos, STAY, False)
    return place(table, received, staying)


def solution(mesh):
    tiles = P(("basin", "row", "col", "sub"), None, None)
    return jax.shard_map(
        shards,
        mesh=mesh,
        in_specs=(tiles,) * FIELDS + (P("basin"),) * 3,
        out_specs=(tiles,) * 3,
        check_vma=False,
    )
```

```python
import functools
import math

import jax
import jax.numpy as jnp
from jax import lax
from jax.experimental import pallas as pl
from jax.experimental.pallas import tpu as pltpu
from jax.sharding import PartitionSpec as P

STEPS = 6
GRAV = 9.81
STEP_TIME = 0.5
SPACING = 5.0
RATE = 0.1
DEPTH_FLOOR = 0.3

FIELDS = 5
HALO = STEPS
PAIR = 2 * HALO
PACK_ROWS = 32
SIDE = 128
TOP = 16
ROWS = SIDE + 32
LO = 8
HI = SIDE + 24
CHUNK = 24
NT = 4
GROUP = SIDE // NT
CLOSED = 1e30
POWER = -(7.0 / 3.0) / math.log(2.0)

ENTRY = 32
NEAR = {"w": 0, "e": 1, "n": 2, "s": 3, "nw": 4, "ne": 5, "sw": 6, "se": 7}
STEP_TO = ((0, -1), (0, 1), (-1, 0), (1, 0), (-1, -1), (-1, 1), (1, -1), (1, 1))
LEAVE, STAY, RECEIVE = 0, NT * ENTRY, 2 * NT * ENTRY

SMEM = pltpu.SMEM
VMEM = pltpu.VMEM
ANY = pl.ANY
SMALL = pltpu.CompilerParams(vmem_limit_bytes=2 * 1024 * 1024)


def lane_index():
    return lax.broadcasted_iota(jnp.int32, (1, SIDE), 1)


def divide(value, size):
    if size & (size - 1):
        return lax.div(value, size)
    return lax.shift_right_logical(value, size.bit_length() - 1)


def remainder(value, size):
    if size & (size - 1):
        return lax.rem(value, size)
    return value & (size - 1)


def index_kernel(shape, before_ref, after_ref, wet_ref, table, inv_before, inv_after, count):
    cols, subs, tile_count, total = shape
    lanes = cols * subs
    row_tiles = lanes * tile_count
    tile_rows = total // row_tiles
    my_row, my_col, my_sub = (lax.axis_index(name) for name in ("row", "col", "sub"))
    me = my_row * lanes + my_col * subs + my_sub
    spare = RECEIVE + 2 * lanes

    def invert(s, carry):
        for u in range(16):
            inv_before[before_ref[s * 16 + u]] = s * 16 + u
            inv_after[after_ref[s * 16 + u]] = s * 16 + u
        return carry

    lax.fori_loop(0, total // 16, invert, 0)
    for i in range(lanes * 2):
        table[RECEIVE + i] = -1
    for i in range(lanes + 1):
        count[i] = 0

    def relative(lane, sign):
        col = remainder(sign * (divide(lane, subs) - my_col) + cols, cols)
        sub = remainder(sign * (remainder(lane, subs) - my_sub) + subs, subs)
        return col * subs + sub

    def own(s, carry):
        tile = before_ref[me * tile_count + s]
        device = divide(inv_after[tile], tile_count)
        stays = device == me
        to = relative(remainder(device, lanes), 1)
        nth = count[to]
        count[to] = nth + 1
        left = count[lanes]
        count[lanes] = left + jnp.where(stays, 0, 1)
        base = jnp.where(
            stays,
            STAY + jnp.minimum(nth, NT - 1) * ENTRY,
            LEAVE + jnp.minimum(left, NT - 1) * ENTRY,
        )
        table[base + 1] = wet_ref[tile]
        table[base + 2] = s
        table[base + 3] = jnp.where(stays, s, to * 2 + jnp.minimum(nth, 1))
        row, col = divide(tile, row_tiles), remainder(tile, row_tiles)
        for n, (dr, dc) in enumerate(STEP_TO):
            r, c = row + dr, col + dc
            there = (r >= 0) & (r < tile_rows) & (c >= 0) & (c < row_tiles)
            near = jnp.where(there, tile + (dr * row_tiles + dc), tile)
            at = inv_before[near]
            table[base + 4 + 3 * n] = jnp.where(there, wet_ref[near], 0)
            table[base + 5 + 3 * n] = relative(remainder(divide(at, tile_count), lanes), -1)
            table[base + 6 + 3 * n] = remainder(at, tile_count)
        return carry

    lax.fori_loop(0, tile_count, own, 0)

    for rel in range(1, lanes):
        col = remainder(my_col + (cols - rel // subs), cols)
        sub = remainder(my_sub + (subs - rel % subs), subs)
        device = my_row * lanes + col * subs + sub
        found = jnp.int32(0)
        for s in range(tile_count):
            at = inv_after[before_ref[device * tile_count + s]]
            mine = divide(at, tile_count) == me
            place = RECEIVE + rel * 2 + jnp.minimum(found, 1)
            table[jnp.where(mine, place, spare)] = remainder(at, tile_count)
            found = found + jnp.where(mine, 1, 0)


def make_table(shape, before, after, wet):
    cols, subs, _, total = shape
    return pl.pallas_call(
        functools.partial(index_kernel, shape),
        name="index_table",
        out_shape=SMEM((RECEIVE + 2 * cols * subs + 1,), jnp.int32),
        in_specs=[pl.BlockSpec(memory_space=SMEM)] * 3,
        out_specs=pl.BlockSpec(memory_space=SMEM),
        scratch_shapes=[
            SMEM((total,), jnp.int32),
            SMEM((total,), jnp.int32),
            SMEM((cols * subs + 1,), jnp.int32),
        ],
        compiler_params=SMALL,
    )(before, after, wet)


def in_vmem(array):
    return pltpu.with_memory_space_constraint(array, VMEM)


def vmem_specs(count):
    return [pl.BlockSpec(memory_space=VMEM)] * count


def load_kernel(*refs):
    sources, refs = refs[:FIELDS], refs[FIELDS:]
    fields, (columns, first, last, sem) = refs[:FIELDS], refs[FIELDS:]
    lane = lane_index()
    copies = [
        pltpu.make_async_copy(sources[f], fields[f], sem.at[f]) for f in range(FIELDS)
    ]
    for copy in copies:
        copy.start()
    tile_count = fields[0].shape[0]
    for t in range(tile_count):
        first[t, FIELDS * HALO :, :] = jnp.zeros((2, SIDE), jnp.float32)
        last[t, :2, :] = jnp.zeros((2, SIDE), jnp.float32)
    for f in range(FIELDS):
        copies[f].wait()
        for t in range(0, tile_count, 2):
            packed = columns[t // 2] if f else jnp.zeros((SIDE, SIDE), jnp.float32)
            for u in range(2):
                at = PAIR * (u * FIELDS + f)
                moved = pltpu.roll(fields[f][t + u], at + HALO, 1)
                packed = jnp.where((lane >= at) & (lane < at + PAIR), moved, packed)
            columns[t // 2] = packed
        for t in range(tile_count):
            first[t, HALO * f : HALO * (f + 1), :] = fields[f][t, :HALO, :]
            last[t, 2 + HALO * f : 2 + HALO * (f + 1), :] = fields[f][t, SIDE - HALO :, :]


def load(arrays):
    tile_count = arrays[0].shape[0]
    rows = VMEM((tile_count, PACK_ROWS, SIDE), jnp.float32)
    outs = [VMEM(array.shape, array.dtype) for array in arrays]
    outs += [VMEM((tile_count // 2, SIDE, SIDE), jnp.float32), rows, rows]
    return pl.pallas_call(
        load_kernel,
        name="load_and_pack",
        out_shape=tuple(outs),
        in_specs=[pl.BlockSpec(memory_space=pltpu.HBM)] * FIELDS,
        out_specs=tuple(vmem_specs(len(outs))),
        scratch_shapes=[pltpu.SemaphoreType.DMA((FIELDS,))],
        compiler_params=SMALL,
    )(*[pltpu.with_memory_space_constraint(array, pltpu.HBM) for array in arrays])


def face(flow, level, level_next, ground, friction):
    wetted = jnp.maximum(level, level_next) - ground
    drive = (GRAV * STEP_TIME / SPACING) * jnp.maximum(wetted, 0.0) * (level_next - level)
    power = jnp.exp2(POWER * jnp.log(jnp.maximum(wetted, DEPTH_FLOOR)))
    return (flow - drive) / (1.0 + friction * jnp.abs(flow) * power)


class Part:
    def __init__(self, name, base, computed, own, halo_rows, sent):
        self.name = name
        self.base = base
        self.computed = computed
        self.own = own
        self.halo_rows = halo_rows
        self.sent = sent

    def chunks(self):
        for start, count in self.computed:
            for r in range(start, start + count, CHUNK):
                yield r, min(CHUNK, start + count - r)


def row_span(span):
    return pl.ds(span[0], span[1])


EDGE = 8
BAND = 24
EARLY = Part("leaving_middle", LEAVE, ((TOP, SIDE),), ((0, SIDE),), False, ((EDGE, SIDE - 2 * EDGE),))
LATE = Part(
    "leaving_edges",
    LEAVE,
    ((LO, BAND), (HI - BAND, BAND)),
    ((0, BAND - 8), (SIDE - BAND + 8, BAND - 8)),
    True,
    ((0, EDGE), (SIDE - EDGE, EDGE)),
)
WHOLE = Part("staying", STAY, ((LO, HI - LO),), ((0, SIDE),), True, ((0, SIDE),))


def row_bands(r, rows, above, middle, below):
    row = r + lax.broadcasted_iota(jnp.int32, (rows, 1), 0)
    return jnp.where(row < TOP, above, jnp.where(row < TOP + SIDE, middle, below))


def assemble(part, table, base, i, slot, fields, stacks, block, strip):
    halo_cols = stacks[0]
    lane = lane_index()
    at = GROUP * i

    def near(name):
        place = base + 5 + 3 * NEAR[name]
        return table[place], table[place + 1]

    def inside(lo, hi):
        return (lane >= at + lo) & (lane < at + hi)

    west, east = near("w"), near("e")
    for f in range(FIELDS):
        rows = pl.ds(HALO * f, 8)

        def ends(halo, middle, left, right, out):
            mid = halo[middle[0], middle[1], rows, :]
            block[f][i, out : out + 8, :] = mid
            lower = jnp.where(lane < SIDE // 2, mid, halo[left[0], left[1], rows, :])
            upper = jnp.where(lane < SIDE // 2, halo[right[0], right[1], rows, :], mid)
            value = jnp.where(
                inside(0, 16),
                pltpu.roll(lower, (at + 8) % SIDE, 1),
                pltpu.roll(upper, (at + 24) % SIDE, 1),
            )
            if i:
                value = jnp.where(inside(0, GROUP), value, strip[f][out : out + 8, :])
            strip[f][out : out + 8, :] = value

        if part.halo_rows:
            ends(stacks[1], near("n"), near("nw"), near("ne"), LO)
            ends(stacks[2], near("s"), near("sw"), near("se"), TOP + SIDE)

        for start, count in part.own:
            own, out = pl.ds(start, count), pl.ds(TOP + start, count)

            def shifted(place, goal):
                source = PAIR * (remainder(place[1], 2) * FIELDS + f)
                shift = remainder(goal - source + 2 * SIDE, SIDE)
                return pltpu.roll(halo_cols[place[0], divide(place[1], 2), own, :], shift, 1)

            core = fields[f][slot, own, :]
            block[f][i, out, :] = core
            value = shifted(west, at + 2)
            if i:
                value = jnp.where(inside(0, 8), value, strip[f][out, :])
            value = jnp.where(inside(8, 16), pltpu.roll(core, (at + 8) % SIDE, 1), value)
            value = jnp.where(inside(16, 24), pltpu.roll(core, (at + 24) % SIDE, 1), value)
            value = jnp.where(inside(24, GROUP), shifted(east, at + 24 - HALO), value)
            strip[f][out, :] = value


def prepare_strip(part, near_wet, strip, ground_x, ground_y):
    level, flow_x, flow_y, ground, friction = strip
    lane = lane_index()

    def lane_wet(center, left, right):
        value = jnp.zeros((1, SIDE), jnp.int32)
        for i in range(NT):
            at = GROUP * i
            middle = near_wet(i, center) if center else 1
            sides = jnp.where(
                lane < at + 8,
                near_wet(i, left),
                jnp.where(lane < at + 24, middle, near_wet(i, right)),
            )
            value = jnp.where((lane >= at) & (lane < at + GROUP), sides, value)
        return value

    bands = (lane_wet("n", "nw", "ne"), lane_wet(None, "w", "e"), lane_wet("s", "sw", "se"))
    for r, rows in part.chunks():
        at, south = pl.ds(r, rows), pl.ds(r + 1, rows)
        z = ground[at, :]
        here, next_row = row_bands(r, rows, *bands), row_bands(r + 1, rows, *bands)
        open_x = (here == 1) & (pltpu.roll(here, SIDE - 1, 1) == 1)
        open_y = (here == 1) & (next_row == 1)
        z_east = pltpu.roll(z, SIDE - 1, 1)
        ground_x[at, :] = jnp.where(open_x, jnp.maximum(z, z_east), CLOSED)
        ground_y[at, :] = jnp.where(open_y, jnp.maximum(z, ground[south, :]), CLOSED)
        flow_x[at, :] = jnp.where(open_x, flow_x[at, :], 0.0)
        flow_y[at, :] = jnp.where(open_y, flow_y[at, :], 0.0)
        friction[at, :] = (GRAV * STEP_TIME) * friction[at, :] * friction[at, :]
        level[at, :] = level[at, :] + z


def prepare_tile(part, near_wet, i, block, ground_x, ground_y, strip_ground):
    level, flow_x, flow_y, ground, friction = block
    lane = lane_index()
    last = lane == SIDE - 1
    n, e, s = near_wet(i, "n"), near_wet(i, "e"), near_wet(i, "s")
    bands = (
        jnp.where(last, n * near_wet(i, "ne"), n),
        jnp.where(last, e, 1),
        jnp.where(last, s * near_wet(i, "se"), s),
    )
    for r, rows in part.chunks():
        at, south = pl.ds(r, rows), pl.ds(r + 1, rows)
        z = ground[i, at, :]
        z_east = jnp.where(
            last, pltpu.roll(strip_ground[at, :], to_east(i), 1), pltpu.roll(z, SIDE - 1, 1)
        )
        open_x = row_bands(r, rows, *bands) == 1
        open_y = (row_bands(r + 1, rows, n, 1, s) == 1) & (row_bands(r, rows, n, 1, s) == 1)
        ground_x[i, at, :] = jnp.where(open_x, jnp.maximum(z, z_east), CLOSED)
        ground_y[i, at, :] = jnp.where(open_y, jnp.maximum(z, ground[i, south, :]), CLOSED)
        flow_x[i, at, :] = jnp.where(open_x, flow_x[i, at, :], 0.0)
        flow_y[i, at, :] = jnp.where(open_y, flow_y[i, at, :], 0.0)
        friction[i, at, :] = (GRAV * STEP_TIME) * friction[i, at, :] * friction[i, at, :]
        level[i, at, :] = level[i, at, :] + z


def to_east(i):
    return (SIDE - 1 - GROUP * i - 24) % SIDE


def to_west(i):
    return (SIDE - GROUP * i - 7) % SIDE


def advance_kernel(part, lanes, *refs):
    table = refs[0]
    fields = refs[1 : 1 + FIELDS]
    kinds = 3 if part.halo_rows else 1
    halos, refs = refs[1 + FIELDS : 1 + FIELDS + kinds * lanes], refs[1 + FIELDS + kinds * lanes :]
    n_out = 3 if part is WHOLE else lanes - 1
    outs, stacks, refs = refs[:n_out], refs[n_out : n_out + kinds], refs[n_out + kinds :]
    (
        level, flow_x, flow_y, ground, friction, ground_x, ground_y,
        s_level, s_flow_x, s_flow_y, s_ground, s_friction, s_ground_x, s_ground_y,
        sem_out,
    ) = refs
    block = (level, flow_x, flow_y, ground, friction)
    strip = (s_level, s_flow_x, s_flow_y, s_ground, s_friction)
    lane = lane_index()
    last, first = lane == SIDE - 1, lane == 0

    def entry(i):
        at = part.base + i * ENTRY
        return table[at + 1], table[at + 2], table[at + 3]

    def near_wet(i, name):
        return table[part.base + i * ENTRY + 4 + 3 * NEAR[name]]

    for k in range(lanes):
        for n in range(kinds):
            if n:
                stacks[n][k] = halos[kinds * k + n][...]
            else:
                for span in part.own:
                    stacks[0][k, :, row_span(span), :] = halos[kinds * k][:, row_span(span), :]
    for i in range(NT):
        base = part.base + i * ENTRY
        assemble(part, table, base, i, entry(i)[1], fields, stacks, block, strip)
    prepare_strip(part, near_wet, strip, s_ground_x, s_ground_y)
    for i in range(NT):
        prepare_tile(part, near_wet, i, block, ground_x, ground_y, s_ground)

    def step(_, carry):
        for r, rows in part.chunks():
            at, south = pl.ds(r, rows), pl.ds(r + 1, rows)
            e, c = s_level[at, :], s_friction[at, :]
            e_east = pltpu.roll(e, SIDE - 1, 1)
            s_flow_x[at, :] = face(s_flow_x[at, :], e, e_east, s_ground_x[at, :], c)
            s_flow_y[at, :] = face(s_flow_y[at, :], e, s_level[south, :], s_ground_y[at, :], c)
        for i in range(NT):
            for r, rows in part.chunks():
                at, south = pl.ds(r, rows), pl.ds(r + 1, rows)
                e, c = level[i, at, :], friction[i, at, :]
                e_east = jnp.where(
                    last, pltpu.roll(s_level[at, :], to_east(i), 1), pltpu.roll(e, SIDE - 1, 1)
                )
                flow_x[i, at, :] = face(flow_x[i, at, :], e, e_east, ground_x[i, at, :], c)
                flow_y[i, at, :] = face(
                    flow_y[i, at, :], e, level[i, south, :], ground_y[i, at, :], c
                )
        for r, rows in part.chunks():
            at, north = pl.ds(r, rows), pl.ds(r - 1, rows)
            qx = s_flow_x[at, :]
            s_level[at, :] = s_level[at, :] + RATE * (
                (pltpu.roll(qx, 1, 1) - qx) + (s_flow_y[north, :] - s_flow_y[at, :])
            )
        for i in range(NT):
            for r, rows in part.chunks():
                at, north = pl.ds(r, rows), pl.ds(r - 1, rows)
                qx = flow_x[i, at, :]
                qx_west = jnp.where(
                    first, pltpu.roll(s_flow_x[at, :], to_west(i), 1), pltpu.roll(qx, 1, 1)
                )
                level[i, at, :] = level[i, at, :] + RATE * (
                    (qx_west - qx) + (flow_y[i, north, :] - flow_y[i, at, :])
                )
        return carry

    lax.fori_loop(0, STEPS, step, 0)

    results = (level, flow_x, flow_y)
    for i in range(NT):
        wet, slot, _ = entry(i)
        for start, count in part.sent:
            own, at = pl.ds(start, count), pl.ds(TOP + start, count)
            level[i, at, :] = level[i, at, :] - ground[i, at, :]
            for f in range(3):
                results[f][i, at, :] = jnp.where(
                    wet == 1, results[f][i, at, :], fields[f][slot, own, :]
                )

    if part is not WHOLE:
        for i in range(NT):
            target = entry(i)[2]
            for k in range(1, lanes):
                @pl.when(divide(target, 2) == k)
                def _():
                    out = 0
                    for start, count in part.sent:
                        for f in range(3):
                            value = results[f][i, pl.ds(TOP + start, count), :]
                            outs[k - 1][remainder(target, 2), f, out : out + count, :] = value
                        out += count

    else:
        copies = [
            pltpu.make_async_copy(
                results[f].at[i, pl.ds(TOP, SIDE), :], outs[f].at[entry(i)[2]], sem_out.at[i, f]
            )
            for i in range(NT)
            for f in range(3)
        ]
        for copy in copies:
            copy.start()
        for copy in copies:
            copy.wait()


def advance(part, table, fields, halos):
    lanes = len(halos)
    sent = sum(count for _, count in part.sent)
    if part is WHOLE:
        outs = (jax.ShapeDtypeStruct(fields[0].shape, jnp.float32),) * 3
        out_specs = [pl.BlockSpec(memory_space=ANY)] * 3
    else:
        outs = (VMEM((2, 3, sent, SIDE), jnp.float32),) * (lanes - 1)
        out_specs = vmem_specs(lanes - 1)
    if not part.halo_rows:
        halos = [group[:1] for group in halos]
    flat = [array for group in halos for array in group]
    block = VMEM((NT, ROWS, SIDE), jnp.float32)
    strip = VMEM((ROWS, SIDE), jnp.float32)
    cells = (NT + 1) * sum(count for _, count in part.computed) * SIDE * STEPS
    return pl.pallas_call(
        functools.partial(advance_kernel, part, lanes),
        name="advance_" + part.name,
        out_shape=outs,
        in_specs=[pl.BlockSpec(memory_space=SMEM)] + vmem_specs(FIELDS + len(flat)),
        out_specs=tuple(out_specs),
        scratch_shapes=[VMEM((lanes,) + array.shape, jnp.float32) for array in halos[0]]
        + [block] * 7
        + [strip] * 7
        + [pltpu.SemaphoreType.DMA((NT, 3))],
        compiler_params=pltpu.CompilerParams(vmem_limit_bytes=12 * 1024 * 1024),
        cost_estimate=pl.CostEstimate(
            flops=60 * cells, bytes_accessed=8 * NT * sent * SIDE * 4, transcendentals=6 * cells
        ),
    )(table, *fields, *flat)


def place_kernel(spans, lanes, *refs):
    table = refs[0]
    received = refs[1:lanes]
    outs = refs[lanes + 3 : lanes + 6]
    sem = refs[lanes + 6]

    def each(act):
        for k in range(1, lanes):
            for j in range(2):
                slot = table[RECEIVE + 2 * k + j]

                @pl.when(slot >= 0)
                def _():
                    at = 0
                    for n, (start, count) in enumerate(spans):
                        for f in range(3):
                            act(
                                pltpu.make_async_copy(
                                    received[k - 1].at[j, f, pl.ds(at, count), :],
                                    outs[f].at[slot, pl.ds(start, count), :],
                                    sem.at[k, j, f, n],
                                )
                            )
                        at += count

    each(lambda copy: copy.start())
    each(lambda copy: copy.wait())


def place(part, table, received, partial_outs):
    lanes = len(received) + 1
    return pl.pallas_call(
        functools.partial(place_kernel, part.sent, lanes),
        name="place_" + part.name,
        out_shape=tuple(jax.ShapeDtypeStruct(o.shape, o.dtype) for o in partial_outs),
        in_specs=[pl.BlockSpec(memory_space=SMEM)]
        + vmem_specs(lanes - 1)
        + [pl.BlockSpec(memory_space=ANY)] * 3,
        out_specs=tuple(pl.BlockSpec(memory_space=ANY) for _ in partial_outs),
        scratch_shapes=[pltpu.SemaphoreType.DMA((lanes, 2, 3, len(part.sent)))],
        input_output_aliases={lanes: 0, lanes + 1: 1, lanes + 2: 2},
        compiler_params=SMALL,
    )(table, *received, *partial_outs)


def shift_lanes(array, col_shift, sub_shift):
    cols, subs = lax.axis_size("col"), lax.axis_size("sub")
    pairs = [
        (c * subs + s, ((c + col_shift) % cols) * subs + (s + sub_shift) % subs)
        for c in range(cols)
        for s in range(subs)
    ]
    return lax.ppermute(array, ("col", "sub"), pairs)


def over_cols(array):
    return [array] + [shift_lanes(array, c, 0) for c in range(1, lax.axis_size("col"))]


def over_subs(parts):
    subs = lax.axis_size("sub")
    return [
        in_vmem(part if s == 0 else shift_lanes(part, 0, s)) for part in parts for s in range(subs)
    ]


def shards(
    water_depth, flow_east, flow_south, bed_level, manning_n, placed_before, placed_after, wet_tiles
):
    cols, subs, rows = lax.axis_size("col"), lax.axis_size("sub"), lax.axis_size("row")
    tile_count = water_depth.shape[0]
    *fields, columns, first, last = load(
        (water_depth, flow_east, flow_south, bed_level, manning_n)
    )
    fields = [in_vmem(field) for field in fields]
    columns = over_cols(columns)
    above = over_cols(lax.ppermute(last, "row", [(i, i + 1) for i in range(rows - 1)]))
    below = over_cols(lax.ppermute(first, "row", [(i + 1, i) for i in range(rows - 1)]))
    table = make_table(
        (cols, subs, tile_count, placed_before.shape[0]), placed_before, placed_after, wet_tiles
    )
    columns[1:], table = lax.optimization_barrier((columns[1:], table))
    table = pltpu.with_memory_space_constraint(table, SMEM)
    columns = over_subs(columns)

    def send(parts):
        return [
            in_vmem(shift_lanes(parts[k - 1], k // subs, k % subs)) for k in range(1, cols * subs)
        ]

    middle = send(advance(EARLY, table, fields, [(part,) for part in columns]))
    halos = list(zip(columns, over_subs(above), over_subs(below)))
    edges = send(advance(LATE, table, fields, halos))
    outs = advance(WHOLE, table, fields, halos)
    outs = place(EARLY, table, middle, outs)
    return place(LATE, table, edges, outs)


def solution(mesh):
    tiles = P(("basin", "row", "col", "sub"), None, None)
    return jax.shard_map(
        shards,
        mesh=mesh,
        in_specs=(tiles,) * FIELDS + (P("basin"),) * 3,
        out_specs=(tiles,) * 3,
        check_vma=False,
    )
```

```python
import functools
import math

import jax
import jax.numpy as jnp
from jax import lax
from jax.experimental import pallas as pl
from jax.experimental.pallas import tpu as pltpu
from jax.sharding import PartitionSpec as P

STEPS = 6
GRAV = 9.81
STEP_TIME = 0.5
SPACING = 5.0
RATE = 0.1
DEPTH_FLOOR = 0.3

FIELDS = 5
HALO = STEPS
PAIR = 2 * HALO
PACK_ROWS = 32
SIDE = 128
TOP = 16
ROWS = SIDE + 32
LO = 8
HI = SIDE + 24
CHUNK = 24
NT = 4
GROUP = SIDE // NT
CLOSED = 1e30
POWER = -(7.0 / 3.0) / math.log(2.0)

ENTRY = 32
NEAR = {"w": 0, "e": 1, "n": 2, "s": 3, "nw": 4, "ne": 5, "sw": 6, "se": 7}
STEP_TO = ((0, -1), (0, 1), (-1, 0), (1, 0), (-1, -1), (-1, 1), (1, -1), (1, 1))
LEAVE, STAY, RECEIVE = 0, NT * ENTRY, 2 * NT * ENTRY

SMEM = pltpu.SMEM
VMEM = pltpu.VMEM
ANY = pl.ANY
SMALL = pltpu.CompilerParams(vmem_limit_bytes=2 * 1024 * 1024)


def lane_index():
    return lax.broadcasted_iota(jnp.int32, (1, SIDE), 1)


def divide(value, size):
    if size & (size - 1):
        return lax.div(value, size)
    return lax.shift_right_logical(value, size.bit_length() - 1)


def remainder(value, size):
    if size & (size - 1):
        return lax.rem(value, size)
    return value & (size - 1)


def index_kernel(shape, before_ref, after_ref, wet_ref, table, inv_before, inv_after, count):
    cols, subs, tile_count, total = shape
    lanes = cols * subs
    row_tiles = lanes * tile_count
    tile_rows = total // row_tiles
    my_row, my_col, my_sub = (lax.axis_index(name) for name in ("row", "col", "sub"))
    me = my_row * lanes + my_col * subs + my_sub
    spare = RECEIVE + 2 * lanes

    def invert(s, carry):
        for u in range(16):
            inv_before[before_ref[s * 16 + u]] = s * 16 + u
            inv_after[after_ref[s * 16 + u]] = s * 16 + u
        return carry

    lax.fori_loop(0, total // 16, invert, 0)
    for i in range(lanes * 2):
        table[RECEIVE + i] = -1
    for i in range(lanes + 1):
        count[i] = 0

    def relative(lane, sign):
        col = remainder(sign * (divide(lane, subs) - my_col) + cols, cols)
        sub = remainder(sign * (remainder(lane, subs) - my_sub) + subs, subs)
        return col * subs + sub

    def own(s, carry):
        tile = before_ref[me * tile_count + s]
        device = divide(inv_after[tile], tile_count)
        stays = device == me
        to = relative(remainder(device, lanes), 1)
        nth = count[to]
        count[to] = nth + 1
        left = count[lanes]
        count[lanes] = left + jnp.where(stays, 0, 1)
        base = jnp.where(
            stays,
            STAY + jnp.minimum(nth, NT - 1) * ENTRY,
            LEAVE + jnp.minimum(left, NT - 1) * ENTRY,
        )
        table[base + 1] = wet_ref[tile]
        table[base + 2] = s
        table[base + 3] = jnp.where(stays, s, to * 2 + jnp.minimum(nth, 1))
        row, col = divide(tile, row_tiles), remainder(tile, row_tiles)
        for n, (dr, dc) in enumerate(STEP_TO):
            r, c = row + dr, col + dc
            there = (r >= 0) & (r < tile_rows) & (c >= 0) & (c < row_tiles)
            near = jnp.where(there, tile + (dr * row_tiles + dc), tile)
            at = inv_before[near]
            table[base + 4 + 3 * n] = jnp.where(there, wet_ref[near], 0)
            table[base + 5 + 3 * n] = relative(remainder(divide(at, tile_count), lanes), -1)
            table[base + 6 + 3 * n] = remainder(at, tile_count)
        return carry

    lax.fori_loop(0, tile_count, own, 0)

    for rel in range(1, lanes):
        col = remainder(my_col + (cols - rel // subs), cols)
        sub = remainder(my_sub + (subs - rel % subs), subs)
        device = my_row * lanes + col * subs + sub
        found = jnp.int32(0)
        for s in range(tile_count):
            at = inv_after[before_ref[device * tile_count + s]]
            mine = divide(at, tile_count) == me
            place = RECEIVE + rel * 2 + jnp.minimum(found, 1)
            table[jnp.where(mine, place, spare)] = remainder(at, tile_count)
            found = found + jnp.where(mine, 1, 0)


def make_table(shape, before, after, wet):
    cols, subs, _, total = shape
    return pl.pallas_call(
        functools.partial(index_kernel, shape),
        name="index_table",
        out_shape=SMEM((RECEIVE + 2 * cols * subs + 1,), jnp.int32),
        in_specs=[pl.BlockSpec(memory_space=SMEM)] * 3,
        out_specs=pl.BlockSpec(memory_space=SMEM),
        scratch_shapes=[
            SMEM((total,), jnp.int32),
            SMEM((total,), jnp.int32),
            SMEM((cols * subs + 1,), jnp.int32),
        ],
        compiler_params=SMALL,
    )(before, after, wet)


def in_vmem(array):
    return pltpu.with_memory_space_constraint(array, VMEM)


def vmem_specs(count):
    return [pl.BlockSpec(memory_space=VMEM)] * count


def load_kernel(*refs):
    sources, refs = refs[:FIELDS], refs[FIELDS:]
    fields, (columns, pair_even, pair_odd, first, last, sem) = refs[:FIELDS], refs[FIELDS:]
    lane = lane_index()
    odd = remainder(lax.axis_index("row"), 2) == 1
    copies = [
        pltpu.make_async_copy(sources[f], fields[f], sem.at[f]) for f in range(FIELDS)
    ]
    for copy in copies:
        copy.start()
    tile_count = fields[0].shape[0]
    for t in range(tile_count):
        first[t, FIELDS * HALO :, :] = jnp.zeros((2, SIDE), jnp.float32)
        last[t, :2, :] = jnp.zeros((2, SIDE), jnp.float32)
    for f in range(FIELDS):
        copies[f].wait()
        for t in range(0, tile_count, 2):
            packed = columns[t // 2] if f else jnp.zeros((SIDE, SIDE), jnp.float32)
            for u in range(2):
                at = PAIR * (u * FIELDS + f)
                moved = pltpu.roll(fields[f][t + u], at + HALO, 1)
                packed = jnp.where((lane >= at) & (lane < at + PAIR), moved, packed)
            columns[t // 2] = packed
        for t in range(tile_count):
            first[t, HALO * f : HALO * (f + 1), :] = fields[f][t, :HALO, :]
            last[t, 2 + HALO * f : 2 + HALO * (f + 1), :] = fields[f][t, SIDE - HALO :, :]
    pair_even[...] = jnp.where(odd, first[...], last[...])
    pair_odd[...] = jnp.where(odd, last[...], first[...])


def load(arrays):
    tile_count = arrays[0].shape[0]
    rows = VMEM((tile_count, PACK_ROWS, SIDE), jnp.float32)
    outs = [VMEM(array.shape, array.dtype) for array in arrays]
    outs += [VMEM((tile_count // 2, SIDE, SIDE), jnp.float32), rows, rows]
    return pl.pallas_call(
        load_kernel,
        name="load_and_pack",
        out_shape=tuple(outs),
        in_specs=[pl.BlockSpec(memory_space=pltpu.HBM)] * FIELDS,
        out_specs=tuple(vmem_specs(len(outs))),
        scratch_shapes=[rows, rows, pltpu.SemaphoreType.DMA((FIELDS,))],
        compiler_params=SMALL,
    )(*[pltpu.with_memory_space_constraint(array, pltpu.HBM) for array in arrays])


def join_kernel(met_even, met_odd, joined):
    odd = remainder(lax.axis_index("row"), 2) == 1
    joined[0] = jnp.where(odd, met_even[...], met_odd[...])
    joined[1] = jnp.where(odd, met_odd[...], met_even[...])


def join(met_even, met_odd):
    return pl.pallas_call(
        join_kernel,
        name="join_row_halos",
        out_shape=VMEM((2,) + met_even.shape, met_even.dtype),
        in_specs=vmem_specs(2),
        out_specs=pl.BlockSpec(memory_space=VMEM),
        compiler_params=SMALL,
    )(in_vmem(met_even), in_vmem(met_odd))


def face(flow, level, level_next, ground, friction):
    wetted = jnp.maximum(level, level_next) - ground
    drive = (GRAV * STEP_TIME / SPACING) * jnp.maximum(wetted, 0.0) * (level_next - level)
    power = jnp.exp2(POWER * jnp.log(jnp.maximum(wetted, DEPTH_FLOOR)))
    return (flow - drive) / (1.0 + friction * jnp.abs(flow) * power)


class Part:
    def __init__(self, name, base, computed, own, halo_rows, sent):
        self.name = name
        self.base = base
        self.computed = computed
        self.own = own
        self.halo_rows = halo_rows
        self.sent = sent

    def chunks(self):
        for start, count in self.computed:
            for r in range(start, start + count, CHUNK):
                yield r, min(CHUNK, start + count - r)


def row_span(span):
    return pl.ds(span[0], span[1])


EDGE = 8
BAND = 24
EARLY = Part("leaving_middle", LEAVE, ((TOP, SIDE),), ((0, SIDE),), False, ((EDGE, SIDE - 2 * EDGE),))
LATE = Part(
    "leaving_edges",
    LEAVE,
    ((LO, BAND), (HI - BAND, BAND)),
    ((0, BAND - 8), (SIDE - BAND + 8, BAND - 8)),
    True,
    ((0, EDGE), (SIDE - EDGE, EDGE)),
)
WHOLE = Part("staying", STAY, ((LO, HI - LO),), ((0, SIDE),), True, ((0, SIDE),))


def row_bands(r, rows, above, middle, below):
    row = r + lax.broadcasted_iota(jnp.int32, (rows, 1), 0)
    return jnp.where(row < TOP, above, jnp.where(row < TOP + SIDE, middle, below))


def assemble(part, table, base, i, slot, fields, stacks, block, strip):
    halo_cols = stacks[0]
    lane = lane_index()
    at = GROUP * i

    def near(name):
        place = base + 5 + 3 * NEAR[name]
        return table[place], table[place + 1]

    def inside(lo, hi):
        return (lane >= at + lo) & (lane < at + hi)

    west, east = near("w"), near("e")
    for f in range(FIELDS):
        rows = pl.ds(HALO * f, 8)

        def ends(side, middle, left, right, out):
            mid, left_end, right_end = (
                stacks[1][place[0], side, place[1], rows, :] for place in (middle, left, right)
            )
            block[f][i, out : out + 8, :] = mid
            lower = jnp.where(lane < SIDE // 2, mid, left_end)
            upper = jnp.where(lane < SIDE // 2, right_end, mid)
            value = jnp.where(
                inside(0, 16),
                pltpu.roll(lower, (at + 8) % SIDE, 1),
                pltpu.roll(upper, (at + 24) % SIDE, 1),
            )
            if i:
                value = jnp.where(inside(0, GROUP), value, strip[f][out : out + 8, :])
            strip[f][out : out + 8, :] = value

        if part.halo_rows:
            ends(0, near("n"), near("nw"), near("ne"), LO)
            ends(1, near("s"), near("sw"), near("se"), TOP + SIDE)

        for start, count in part.own:
            own, out = pl.ds(start, count), pl.ds(TOP + start, count)

            def shifted(place, goal):
                source = PAIR * (remainder(place[1], 2) * FIELDS + f)
                shift = remainder(goal - source + 2 * SIDE, SIDE)
                return pltpu.roll(halo_cols[place[0], divide(place[1], 2), own, :], shift, 1)

            core = fields[f][slot, own, :]
            block[f][i, out, :] = core
            value = shifted(west, at + 2)
            if i:
                value = jnp.where(inside(0, 8), value, strip[f][out, :])
            value = jnp.where(inside(8, 16), pltpu.roll(core, (at + 8) % SIDE, 1), value)
            value = jnp.where(inside(16, 24), pltpu.roll(core, (at + 24) % SIDE, 1), value)
            value = jnp.where(inside(24, GROUP), shifted(east, at + 24 - HALO), value)
            strip[f][out, :] = value


def prepare_strip(part, near_wet, strip, ground_x, ground_y):
    level, flow_x, flow_y, ground, friction = strip
    lane = lane_index()

    def lane_wet(center, left, right):
        value = jnp.zeros((1, SIDE), jnp.int32)
        for i in range(NT):
            at = GROUP * i
            middle = near_wet(i, center) if center else 1
            sides = jnp.where(
                lane < at + 8,
                near_wet(i, left),
                jnp.where(lane < at + 24, middle, near_wet(i, right)),
            )
            value = jnp.where((lane >= at) & (lane < at + GROUP), sides, value)
        return value

    bands = (lane_wet("n", "nw", "ne"), lane_wet(None, "w", "e"), lane_wet("s", "sw", "se"))
    for r, rows in part.chunks():
        at, south = pl.ds(r, rows), pl.ds(r + 1, rows)
        z = ground[at, :]
        here, next_row = row_bands(r, rows, *bands), row_bands(r + 1, rows, *bands)
        open_x = (here == 1) & (pltpu.roll(here, SIDE - 1, 1) == 1)
        open_y = (here == 1) & (next_row == 1)
        z_east = pltpu.roll(z, SIDE - 1, 1)
        ground_x[at, :] = jnp.where(open_x, jnp.maximum(z, z_east), CLOSED)
        ground_y[at, :] = jnp.where(open_y, jnp.maximum(z, ground[south, :]), CLOSED)
        flow_x[at, :] = jnp.where(open_x, flow_x[at, :], 0.0)
        flow_y[at, :] = jnp.where(open_y, flow_y[at, :], 0.0)
        friction[at, :] = (GRAV * STEP_TIME) * friction[at, :] * friction[at, :]
        level[at, :] = level[at, :] + z


def prepare_tile(part, near_wet, i, block, ground_x, ground_y, strip_ground):
    level, flow_x, flow_y, ground, friction = block
    lane = lane_index()
    last = lane == SIDE - 1
    n, e, s = near_wet(i, "n"), near_wet(i, "e"), near_wet(i, "s")
    bands = (
        jnp.where(last, n * near_wet(i, "ne"), n),
        jnp.where(last, e, 1),
        jnp.where(last, s * near_wet(i, "se"), s),
    )
    for r, rows in part.chunks():
        at, south = pl.ds(r, rows), pl.ds(r + 1, rows)
        z = ground[i, at, :]
        z_east = jnp.where(
            last, pltpu.roll(strip_ground[at, :], to_east(i), 1), pltpu.roll(z, SIDE - 1, 1)
        )
        open_x = row_bands(r, rows, *bands) == 1
        open_y = (row_bands(r + 1, rows, n, 1, s) == 1) & (row_bands(r, rows, n, 1, s) == 1)
        ground_x[i, at, :] = jnp.where(open_x, jnp.maximum(z, z_east), CLOSED)
        ground_y[i, at, :] = jnp.where(open_y, jnp.maximum(z, ground[i, south, :]), CLOSED)
        flow_x[i, at, :] = jnp.where(open_x, flow_x[i, at, :], 0.0)
        flow_y[i, at, :] = jnp.where(open_y, flow_y[i, at, :], 0.0)
        friction[i, at, :] = (GRAV * STEP_TIME) * friction[i, at, :] * friction[i, at, :]
        level[i, at, :] = level[i, at, :] + z


def to_east(i):
    return (SIDE - 1 - GROUP * i - 24) % SIDE


def to_west(i):
    return (SIDE - GROUP * i - 7) % SIDE


def advance_kernel(part, lanes, *refs):
    table = refs[0]
    fields = refs[1 : 1 + FIELDS]
    kinds = 2 if part.halo_rows else 1
    halos, refs = refs[1 + FIELDS : 1 + FIELDS + kinds * lanes], refs[1 + FIELDS + kinds * lanes :]
    n_out = 3 if part is WHOLE else lanes - 1
    outs, stacks, refs = refs[:n_out], refs[n_out : n_out + kinds], refs[n_out + kinds :]
    (
        level, flow_x, flow_y, ground, friction, ground_x, ground_y,
        s_level, s_flow_x, s_flow_y, s_ground, s_friction, s_ground_x, s_ground_y,
        sem_out,
    ) = refs
    block = (level, flow_x, flow_y, ground, friction)
    strip = (s_level, s_flow_x, s_flow_y, s_ground, s_friction)
    lane = lane_index()
    last, first = lane == SIDE - 1, lane == 0

    def entry(i):
        at = part.base + i * ENTRY
        return table[at + 1], table[at + 2], table[at + 3]

    def near_wet(i, name):
        return table[part.base + i * ENTRY + 4 + 3 * NEAR[name]]

    for k in range(lanes):
        for n in range(kinds):
            if n:
                stacks[n][k] = halos[kinds * k + n][...]
            else:
                for span in part.own:
                    stacks[0][k, :, row_span(span), :] = halos[kinds * k][:, row_span(span), :]
    for i in range(NT):
        base = part.base + i * ENTRY
        assemble(part, table, base, i, entry(i)[1], fields, stacks, block, strip)
    prepare_strip(part, near_wet, strip, s_ground_x, s_ground_y)
    for i in range(NT):
        prepare_tile(part, near_wet, i, block, ground_x, ground_y, s_ground)

    def step(_, carry):
        for r, rows in part.chunks():
            at, south = pl.ds(r, rows), pl.ds(r + 1, rows)
            e, c = s_level[at, :], s_friction[at, :]
            e_east = pltpu.roll(e, SIDE - 1, 1)
            s_flow_x[at, :] = face(s_flow_x[at, :], e, e_east, s_ground_x[at, :], c)
            s_flow_y[at, :] = face(s_flow_y[at, :], e, s_level[south, :], s_ground_y[at, :], c)
        for i in range(NT):
            for r, rows in part.chunks():
                at, south = pl.ds(r, rows), pl.ds(r + 1, rows)
                e, c = level[i, at, :], friction[i, at, :]
                e_east = jnp.where(
                    last, pltpu.roll(s_level[at, :], to_east(i), 1), pltpu.roll(e, SIDE - 1, 1)
                )
                flow_x[i, at, :] = face(flow_x[i, at, :], e, e_east, ground_x[i, at, :], c)
                flow_y[i, at, :] = face(
                    flow_y[i, at, :], e, level[i, south, :], ground_y[i, at, :], c
                )
        for r, rows in part.chunks():
            at, north = pl.ds(r, rows), pl.ds(r - 1, rows)
            qx = s_flow_x[at, :]
            s_level[at, :] = s_level[at, :] + RATE * (
                (pltpu.roll(qx, 1, 1) - qx) + (s_flow_y[north, :] - s_flow_y[at, :])
            )
        for i in range(NT):
            for r, rows in part.chunks():
                at, north = pl.ds(r, rows), pl.ds(r - 1, rows)
                qx = flow_x[i, at, :]
                qx_west = jnp.where(
                    first, pltpu.roll(s_flow_x[at, :], to_west(i), 1), pltpu.roll(qx, 1, 1)
                )
                level[i, at, :] = level[i, at, :] + RATE * (
                    (qx_west - qx) + (flow_y[i, north, :] - flow_y[i, at, :])
                )
        return carry

    lax.fori_loop(0, STEPS, step, 0)

    results = (level, flow_x, flow_y)
    for i in range(NT):
        wet, slot, _ = entry(i)
        for start, count in part.sent:
            own, at = pl.ds(start, count), pl.ds(TOP + start, count)
            level[i, at, :] = level[i, at, :] - ground[i, at, :]
            for f in range(3):
                results[f][i, at, :] = jnp.where(
                    wet == 1, results[f][i, at, :], fields[f][slot, own, :]
                )

    if part is not WHOLE:
        for i in range(NT):
            target = entry(i)[2]
            for k in range(1, lanes):
                @pl.when(divide(target, 2) == k)
                def _():
                    out = 0
                    for start, count in part.sent:
                        for f in range(3):
                            value = results[f][i, pl.ds(TOP + start, count), :]
                            outs[k - 1][remainder(target, 2), f, out : out + count, :] = value
                        out += count

    else:
        copies = [
            pltpu.make_async_copy(
                results[f].at[i, pl.ds(TOP, SIDE), :], outs[f].at[entry(i)[2]], sem_out.at[i, f]
            )
            for i in range(NT)
            for f in range(3)
        ]
        for copy in copies:
            copy.start()
        for copy in copies:
            copy.wait()


def advance(part, table, fields, halos):
    lanes = len(halos)
    sent = sum(count for _, count in part.sent)
    if part is WHOLE:
        outs = (jax.ShapeDtypeStruct(fields[0].shape, jnp.float32),) * 3
        out_specs = [pl.BlockSpec(memory_space=ANY)] * 3
    else:
        outs = (VMEM((2, 3, sent, SIDE), jnp.float32),) * (lanes - 1)
        out_specs = vmem_specs(lanes - 1)
    if not part.halo_rows:
        halos = [group[:1] for group in halos]
    flat = [array for group in halos for array in group]
    block = VMEM((NT, ROWS, SIDE), jnp.float32)
    strip = VMEM((ROWS, SIDE), jnp.float32)
    cells = (NT + 1) * sum(count for _, count in part.computed) * SIDE * STEPS
    return pl.pallas_call(
        functools.partial(advance_kernel, part, lanes),
        name="advance_" + part.name,
        out_shape=outs,
        in_specs=[pl.BlockSpec(memory_space=SMEM)] + vmem_specs(FIELDS + len(flat)),
        out_specs=tuple(out_specs),
        scratch_shapes=[VMEM((lanes,) + array.shape, jnp.float32) for array in halos[0]]
        + [block] * 7
        + [strip] * 7
        + [pltpu.SemaphoreType.DMA((NT, 3))],
        compiler_params=pltpu.CompilerParams(vmem_limit_bytes=12 * 1024 * 1024),
        cost_estimate=pl.CostEstimate(
            flops=60 * cells, bytes_accessed=8 * NT * sent * SIDE * 4, transcendentals=6 * cells
        ),
    )(table, *fields, *flat)


def place_kernel(spans, lanes, *refs):
    table = refs[0]
    received = refs[1:lanes]
    outs = refs[lanes + 3 : lanes + 6]
    sem = refs[lanes + 6]

    def each(act):
        for k in range(1, lanes):
            for j in range(2):
                slot = table[RECEIVE + 2 * k + j]

                @pl.when(slot >= 0)
                def _():
                    at = 0
                    for n, (start, count) in enumerate(spans):
                        for f in range(3):
                            act(
                                pltpu.make_async_copy(
                                    received[k - 1].at[j, f, pl.ds(at, count), :],
                                    outs[f].at[slot, pl.ds(start, count), :],
                                    sem.at[k, j, f, n],
                                )
                            )
                        at += count

    each(lambda copy: copy.start())
    each(lambda copy: copy.wait())


def place(part, table, received, partial_outs):
    lanes = len(received) + 1
    return pl.pallas_call(
        functools.partial(place_kernel, part.sent, lanes),
        name="place_" + part.name,
        out_shape=tuple(jax.ShapeDtypeStruct(o.shape, o.dtype) for o in partial_outs),
        in_specs=[pl.BlockSpec(memory_space=SMEM)]
        + vmem_specs(lanes - 1)
        + [pl.BlockSpec(memory_space=ANY)] * 3,
        out_specs=tuple(pl.BlockSpec(memory_space=ANY) for _ in partial_outs),
        scratch_shapes=[pltpu.SemaphoreType.DMA((lanes, 2, 3, len(part.sent)))],
        input_output_aliases={lanes: 0, lanes + 1: 1, lanes + 2: 2},
        compiler_params=SMALL,
    )(table, *received, *partial_outs)


def shift_lanes(array, col_shift, sub_shift):
    cols, subs = lax.axis_size("col"), lax.axis_size("sub")
    pairs = [
        (c * subs + s, ((c + col_shift) % cols) * subs + (s + sub_shift) % subs)
        for c in range(cols)
        for s in range(subs)
    ]
    return lax.ppermute(array, ("col", "sub"), pairs)


def over_cols(array):
    return [array] + [shift_lanes(array, c, 0) for c in range(1, lax.axis_size("col"))]


def over_subs(parts):
    subs = lax.axis_size("sub")
    return [
        in_vmem(part if s == 0 else shift_lanes(part, 0, s)) for part in parts for s in range(subs)
    ]


def meet_rows(array, parity):
    rows, subs = lax.axis_size("row"), lax.axis_size("sub")
    pairs = []
    for r in range(rows):
        other = r + 1 if r % 2 == parity else r - 1
        for s in range(subs):
            if 0 <= other < rows:
                pairs.append((r * subs + s, other * subs + s))
            else:
                pairs.append((r * subs + s, r * subs + (s + 1) % subs))
    return lax.ppermute(array, ("row", "sub"), pairs)


def shards(
    water_depth, flow_east, flow_south, bed_level, manning_n, placed_before, placed_after, wet_tiles
):
    cols, subs = lax.axis_size("col"), lax.axis_size("sub")
    tile_count = water_depth.shape[0]
    *fields, columns, pair_even, pair_odd = load(
        (water_depth, flow_east, flow_south, bed_level, manning_n)
    )
    fields = [in_vmem(field) for field in fields]
    columns = over_cols(columns)
    met_even, met_odd = meet_rows(pair_even, 0), meet_rows(pair_odd, 1)
    table = make_table(
        (cols, subs, tile_count, placed_before.shape[0]), placed_before, placed_after, wet_tiles
    )
    columns[1:], met_even, met_odd, table = lax.optimization_barrier(
        (columns[1:], met_even, met_odd, table)
    )
    table = pltpu.with_memory_space_constraint(table, SMEM)
    near_rows = over_subs(over_cols(join(met_even, met_odd)))
    columns = over_subs(columns)

    def send(parts):
        return [
            in_vmem(shift_lanes(parts[k - 1], k // subs, k % subs)) for k in range(1, cols * subs)
        ]

    middle = send(advance(EARLY, table, fields, [(part,) for part in columns]))
    halos = list(zip(columns, near_rows))
    edges = send(advance(LATE, table, fields, halos))
    outs = advance(WHOLE, table, fields, halos)
    outs = place(EARLY, table, middle, outs)
    return place(LATE, table, edges, outs)


def solution(mesh):
    tiles = P(("basin", "row", "col", "sub"), None, None)
    return jax.shard_map(
        shards,
        mesh=mesh,
        in_specs=(tiles,) * FIELDS + (P("basin"),) * 3,
        out_specs=(tiles,) * 3,
        check_vma=False,
    )
```

```python
import functools
import math

import jax
import jax.numpy as jnp
from jax import lax
from jax.experimental import pallas as pl
from jax.experimental.pallas import tpu as pltpu
from jax.sharding import PartitionSpec as P

STEPS = 6
GRAV = 9.81
STEP_TIME = 0.5
SPACING = 5.0
RATE = 0.1
DEPTH_FLOOR = 0.3

FIELDS = 5
HALO = STEPS
LAST_COLS = (HALO, HALO, HALO - 1, HALO, HALO)
FIRST_COLS = (HALO, HALO - 1, HALO - 1, HALO, HALO - 1)
LAST_ROWS = (HALO, HALO - 1, HALO, HALO, HALO)
FIRST_ROWS = (HALO, HALO - 1, HALO - 1, HALO, HALO - 1)


def starts(counts):
    return [sum(counts[:f]) for f in range(len(counts))]


BOTH_COLS = tuple(a + b for a, b in zip(LAST_COLS, FIRST_COLS))
TILE_LANES = sum(BOTH_COLS)
TILE_ROWS = max(sum(LAST_ROWS), sum(FIRST_ROWS))
COL_AT, LAST_AT, FIRST_AT = starts(BOTH_COLS), starts(LAST_ROWS), starts(FIRST_ROWS)
SIDE = 128
TOP = 16
ROWS = SIDE + 32
LO = 8
HI = SIDE + 24
CHUNK = 24
SPARE = 2
NT = 4
GROUP = SIDE // NT
CLOSED = 1e30
POWER = -(7.0 / 3.0) / math.log(2.0)

ENTRY = 32
NEAR = {"w": 0, "e": 1, "n": 2, "s": 3, "nw": 4, "ne": 5, "sw": 6, "se": 7}
STEP_TO = ((0, -1), (0, 1), (-1, 0), (1, 0), (-1, -1), (-1, 1), (1, -1), (1, 1))
LEAVE, STAY, RECEIVE = 0, NT * ENTRY, 2 * NT * ENTRY

SMEM = pltpu.SMEM
VMEM = pltpu.VMEM
ANY = pl.ANY
SMALL = pltpu.CompilerParams(vmem_limit_bytes=2 * 1024 * 1024)


def lane_index():
    return lax.broadcasted_iota(jnp.int32, (1, SIDE), 1)


def divide(value, size):
    if size & (size - 1):
        return lax.div(value, size)
    return lax.shift_right_logical(value, size.bit_length() - 1)


def remainder(value, size):
    if size & (size - 1):
        return lax.rem(value, size)
    return value & (size - 1)


def index_kernel(shape, before_ref, after_ref, wet_ref, table, inv_before, inv_after, count):
    cols, subs, tile_count, total = shape
    lanes = cols * subs
    row_tiles = lanes * tile_count
    tile_rows = total // row_tiles
    my_row, my_col, my_sub = (lax.axis_index(name) for name in ("row", "col", "sub"))
    me = my_row * lanes + my_col * subs + my_sub
    spare = RECEIVE + 2 * lanes

    def invert(s, carry):
        for u in range(16):
            inv_before[before_ref[s * 16 + u]] = s * 16 + u
            inv_after[after_ref[s * 16 + u]] = s * 16 + u
        return carry

    lax.fori_loop(0, total // 16, invert, 0)
    for i in range(lanes * 2):
        table[RECEIVE + i] = -1
    for i in range(lanes + 1):
        count[i] = 0

    def relative(lane, sign):
        col = remainder(sign * (divide(lane, subs) - my_col) + cols, cols)
        sub = remainder(sign * (remainder(lane, subs) - my_sub) + subs, subs)
        return col * subs + sub

    def own(s, carry):
        tile = before_ref[me * tile_count + s]
        device = divide(inv_after[tile], tile_count)
        stays = device == me
        to = relative(remainder(device, lanes), 1)
        nth = count[to]
        count[to] = nth + 1
        left = count[lanes]
        count[lanes] = left + jnp.where(stays, 0, 1)
        base = jnp.where(
            stays,
            STAY + jnp.minimum(nth, NT - 1) * ENTRY,
            LEAVE + jnp.minimum(left, NT - 1) * ENTRY,
        )
        table[base + 1] = wet_ref[tile]
        table[base + 2] = s
        table[base + 3] = jnp.where(stays, s, to * 2 + jnp.minimum(nth, 1))
        row, col = divide(tile, row_tiles), remainder(tile, row_tiles)
        for n, (dr, dc) in enumerate(STEP_TO):
            r, c = row + dr, col + dc
            there = (r >= 0) & (r < tile_rows) & (c >= 0) & (c < row_tiles)
            near = jnp.where(there, tile + (dr * row_tiles + dc), tile)
            at = inv_before[near]
            table[base + 4 + 3 * n] = jnp.where(there, wet_ref[near], 0)
            table[base + 5 + 3 * n] = relative(remainder(divide(at, tile_count), lanes), -1)
            table[base + 6 + 3 * n] = remainder(at, tile_count)
        return carry

    lax.fori_loop(0, tile_count, own, 0)

    for rel in range(1, lanes):
        col = remainder(my_col + (cols - rel // subs), cols)
        sub = remainder(my_sub + (subs - rel % subs), subs)
        device = my_row * lanes + col * subs + sub
        found = jnp.int32(0)
        for s in range(tile_count):
            at = inv_after[before_ref[device * tile_count + s]]
            mine = divide(at, tile_count) == me
            place = RECEIVE + rel * 2 + jnp.minimum(found, 1)
            table[jnp.where(mine, place, spare)] = remainder(at, tile_count)
            found = found + jnp.where(mine, 1, 0)


def make_table(shape, before, after, wet):
    cols, subs, _, total = shape
    return pl.pallas_call(
        functools.partial(index_kernel, shape),
        name="index_table",
        out_shape=SMEM((RECEIVE + 2 * cols * subs + 1,), jnp.int32),
        in_specs=[pl.BlockSpec(memory_space=SMEM)] * 3,
        out_specs=pl.BlockSpec(memory_space=SMEM),
        scratch_shapes=[
            SMEM((total,), jnp.int32),
            SMEM((total,), jnp.int32),
            SMEM((cols * subs + 1,), jnp.int32),
        ],
        compiler_params=SMALL,
    )(before, after, wet)


def in_vmem(array):
    return pltpu.with_memory_space_constraint(array, VMEM)


def vmem_specs(count):
    return [pl.BlockSpec(memory_space=VMEM)] * count


def load_kernel(*refs):
    sources, refs = refs[:FIELDS], refs[FIELDS:]
    fields, (columns, pair_even, pair_odd, first, last, sem, _) = refs[:FIELDS], refs[FIELDS:]
    spill = refs[-1]
    lane = lane_index()
    odd = remainder(lax.axis_index("row"), 2) == 1
    copies = [
        pltpu.make_async_copy(sources[f], fields[f], sem.at[f]) for f in range(FIELDS)
    ]
    for copy in copies:
        copy.start()
    tile_count = fields[0].shape[0]
    blocks = tile_count * TILE_LANES // SIDE
    for f in range(FIELDS):
        copies[f].wait()
        for b in range(blocks + 1):
            target, place = (columns, pl.ds(b * SIDE, SIDE)) if b < blocks else (spill, slice(None))
            packed = target[place, :]
            for t in range(tile_count):
                at = TILE_LANES * t + COL_AT[f] - b * SIDE
                if at < SIDE and at + BOTH_COLS[f] > 0:
                    moved = pltpu.roll(fields[f][t], (at + LAST_COLS[f]) % SIDE, 1)
                    packed = jnp.where((lane >= at) & (lane < at + BOTH_COLS[f]), moved, packed)
            target[place, :] = packed
        for t in range(tile_count):
            at, count = TILE_ROWS * t + FIRST_AT[f], FIRST_ROWS[f]
            first[at : at + count, :] = fields[f][t, :count, :]
            at, count = TILE_ROWS * t + LAST_AT[f], LAST_ROWS[f]
            last[at : at + count, :] = fields[f][t, SIDE - count :, :]
    half = SIDE // 2
    columns[blocks * SIDE :, :] = jnp.where(
        lane < half, spill[:half, :], pltpu.roll(spill[half:, :], half, 1)
    )
    pair_even[...] = jnp.where(odd, first[...], last[...])
    pair_odd[...] = jnp.where(odd, last[...], first[...])


def load(arrays):
    tile_count = arrays[0].shape[0]
    rows = VMEM((tile_count * TILE_ROWS, SIDE), jnp.float32)
    outs = [VMEM(array.shape, array.dtype) for array in arrays]
    outs += [VMEM((tile_count * TILE_LANES, SIDE), jnp.float32), rows, rows]
    return pl.pallas_call(
        load_kernel,
        name="load_and_pack",
        out_shape=tuple(outs),
        in_specs=[pl.BlockSpec(memory_space=pltpu.HBM)] * FIELDS,
        out_specs=tuple(vmem_specs(len(outs))),
        scratch_shapes=[
            rows,
            rows,
            pltpu.SemaphoreType.DMA((FIELDS,)),
            VMEM((SIDE, SIDE), jnp.float32),
        ],
        compiler_params=SMALL,
    )(*[pltpu.with_memory_space_constraint(array, pltpu.HBM) for array in arrays])


def join_kernel(met_even, met_odd, joined):
    odd = remainder(lax.axis_index("row"), 2) == 1
    joined[0] = jnp.where(odd, met_even[...], met_odd[...])
    joined[1] = jnp.where(odd, met_odd[...], met_even[...])


def join(met_even, met_odd):
    return pl.pallas_call(
        join_kernel,
        name="join_row_halos",
        out_shape=VMEM((2,) + met_even.shape, met_even.dtype),
        in_specs=vmem_specs(2),
        out_specs=pl.BlockSpec(memory_space=VMEM),
        compiler_params=SMALL,
    )(in_vmem(met_even), in_vmem(met_odd))


def face(flow, level, level_next, ground, friction):
    wetted = jnp.maximum(level, level_next) - ground
    drive = (GRAV * STEP_TIME / SPACING) * jnp.maximum(wetted, 0.0) * (level_next - level)
    power = jnp.exp2(POWER * jnp.log(jnp.maximum(wetted, DEPTH_FLOOR)))
    return (flow - drive) / (1.0 + friction * jnp.abs(flow) * power)


class Part:
    def __init__(self, name, base, computed, own, halo_rows, sent):
        self.name = name
        self.base = base
        self.computed = computed
        self.own = own
        self.halo_rows = halo_rows
        self.sent = sent

    def chunks(self):
        for start, count in self.computed:
            for r in range(start, start + count, CHUNK):
                yield r, min(CHUNK, start + count - r)


def row_span(span):
    return pl.ds(span[0], span[1])


EDGE = 8
BAND = 24
EARLY = Part("leaving_middle", LEAVE, ((TOP, SIDE),), ((0, SIDE),), False, ((EDGE, SIDE - 2 * EDGE),))
LATE = Part(
    "leaving_edges",
    LEAVE,
    ((LO, BAND), (HI - BAND, BAND)),
    ((0, BAND - 8), (SIDE - BAND + 8, BAND - 8)),
    True,
    ((0, EDGE), (SIDE - EDGE, EDGE)),
)
WHOLE = Part("staying", STAY, ((LO, HI - LO),), ((0, SIDE),), True, ((0, SIDE),))


def row_bands(r, rows, above, middle, below):
    row = r + lax.broadcasted_iota(jnp.int32, (rows, 1), 0)
    return jnp.where(row < TOP, above, jnp.where(row < TOP + SIDE, middle, below))


def assemble(part, table, base, i, slot, fields, stacks, block, strip):
    halo_cols = stacks[0]
    lane = lane_index()
    at = GROUP * i

    def near(name):
        place = base + 5 + 3 * NEAR[name]
        return table[place], table[place + 1]

    def inside(lo, hi):
        return (lane >= at + lo) & (lane < at + hi)

    west, east = near("w"), near("e")
    for f in range(FIELDS):

        def ends(side, start, middle, left, right, out):
            rows = pl.ds(start, 8)
            mid, left_end, right_end = (
                stacks[1][place[0], side, place[1], rows, :] for place in (middle, left, right)
            )
            block[f][i, out : out + 8, :] = mid
            lower = jnp.where(lane < SIDE // 2, mid, left_end)
            upper = jnp.where(lane < SIDE // 2, right_end, mid)
            value = jnp.where(
                inside(0, 16),
                pltpu.roll(lower, (at + 8) % SIDE, 1),
                pltpu.roll(upper, (at + 24) % SIDE, 1),
            )
            if i:
                value = jnp.where(inside(0, GROUP), value, strip[f][out : out + 8, :])
            strip[f][out : out + 8, :] = value

        if part.halo_rows:
            start = SPARE + LAST_AT[f] + LAST_ROWS[f] - 8
            ends(0, start, near("n"), near("nw"), near("ne"), LO)
            ends(1, SPARE + FIRST_AT[f], near("s"), near("sw"), near("se"), TOP + SIDE)

        for start, count in part.own:
            own, out = pl.ds(start, count), pl.ds(TOP + start, count)

            def shifted(place, offset, goal):
                lanes_at = TILE_LANES * place[1] + (COL_AT[f] + offset)
                b, source = divide(lanes_at, SIDE), remainder(lanes_at, SIDE)
                beyond = jnp.minimum(b + 1, halo_cols.shape[1] - 1)
                value = jnp.where(
                    lane >= source, halo_cols[place[0], b, own, :], halo_cols[place[0], beyond, own, :]
                )
                return pltpu.roll(value, remainder(goal - source + SIDE, SIDE), 1)

            core = fields[f][slot, own, :]
            block[f][i, out, :] = core
            value = shifted(west, 0, at + 8 - LAST_COLS[f])
            if i:
                value = jnp.where(inside(0, 8), value, strip[f][out, :])
            value = jnp.where(inside(8, 16), pltpu.roll(core, (at + 8) % SIDE, 1), value)
            value = jnp.where(inside(16, 24), pltpu.roll(core, (at + 24) % SIDE, 1), value)
            value = jnp.where(inside(24, GROUP), shifted(east, LAST_COLS[f], at + 24), value)
            strip[f][out, :] = value


def prepare_strip(part, near_wet, strip, ground_x, ground_y):
    level, flow_x, flow_y, ground, friction = strip
    lane = lane_index()

    def lane_wet(center, left, right):
        value = jnp.zeros((1, SIDE), jnp.int32)
        for i in range(NT):
            at = GROUP * i
            middle = near_wet(i, center) if center else 1
            sides = jnp.where(
                lane < at + 8,
                near_wet(i, left),
                jnp.where(lane < at + 24, middle, near_wet(i, right)),
            )
            value = jnp.where((lane >= at) & (lane < at + GROUP), sides, value)
        return value

    bands = (lane_wet("n", "nw", "ne"), lane_wet(None, "w", "e"), lane_wet("s", "sw", "se"))
    for r, rows in part.chunks():
        at, south = pl.ds(r, rows), pl.ds(r + 1, rows)
        z = ground[at, :]
        here, next_row = row_bands(r, rows, *bands), row_bands(r + 1, rows, *bands)
        open_x = (here == 1) & (pltpu.roll(here, SIDE - 1, 1) == 1)
        open_y = (here == 1) & (next_row == 1)
        z_east = pltpu.roll(z, SIDE - 1, 1)
        ground_x[at, :] = jnp.where(open_x, jnp.maximum(z, z_east), CLOSED)
        ground_y[at, :] = jnp.where(open_y, jnp.maximum(z, ground[south, :]), CLOSED)
        flow_x[at, :] = jnp.where(open_x, flow_x[at, :], 0.0)
        flow_y[at, :] = jnp.where(open_y, flow_y[at, :], 0.0)
        friction[at, :] = (GRAV * STEP_TIME) * friction[at, :] * friction[at, :]
        level[at, :] = level[at, :] + z


def prepare_tile(part, near_wet, i, block, ground_x, ground_y, strip_ground):
    level, flow_x, flow_y, ground, friction = block
    lane = lane_index()
    last = lane == SIDE - 1
    n, e, s = near_wet(i, "n"), near_wet(i, "e"), near_wet(i, "s")
    bands = (
        jnp.where(last, n * near_wet(i, "ne"), n),
        jnp.where(last, e, 1),
        jnp.where(last, s * near_wet(i, "se"), s),
    )
    for r, rows in part.chunks():
        at, south = pl.ds(r, rows), pl.ds(r + 1, rows)
        z = ground[i, at, :]
        z_east = jnp.where(
            last, pltpu.roll(strip_ground[at, :], to_east(i), 1), pltpu.roll(z, SIDE - 1, 1)
        )
        open_x = row_bands(r, rows, *bands) == 1
        open_y = (row_bands(r + 1, rows, n, 1, s) == 1) & (row_bands(r, rows, n, 1, s) == 1)
        ground_x[i, at, :] = jnp.where(open_x, jnp.maximum(z, z_east), CLOSED)
        ground_y[i, at, :] = jnp.where(open_y, jnp.maximum(z, ground[i, south, :]), CLOSED)
        flow_x[i, at, :] = jnp.where(open_x, flow_x[i, at, :], 0.0)
        flow_y[i, at, :] = jnp.where(open_y, flow_y[i, at, :], 0.0)
        friction[i, at, :] = (GRAV * STEP_TIME) * friction[i, at, :] * friction[i, at, :]
        level[i, at, :] = level[i, at, :] + z


def to_east(i):
    return (SIDE - 1 - GROUP * i - 24) % SIDE


def to_west(i):
    return (SIDE - GROUP * i - 7) % SIDE


def unpack_columns(part, packed, out):
    blocks, half = out.shape[0] - 1, SIDE // 2
    for start, count in part.own:
        rows = pl.ds(start, count)
        for b in range(blocks):
            out[b, rows, :] = packed[b * SIDE + start : b * SIDE + start + count, :]
        if start < half:
            n = min(count, half - start)
            out[blocks, start : start + n, :] = packed[
                blocks * SIDE + start : blocks * SIDE + start + n, :
            ]
        if start + count > half:
            low, high = max(start, half), start + count
            lower = packed[blocks * SIDE + low - half : blocks * SIDE + high - half, :]
            out[blocks, low:high, :] = pltpu.roll(lower, half, 1)


def advance_kernel(part, lanes, *refs):
    table = refs[0]
    fields = refs[1 : 1 + FIELDS]
    kinds = 2 if part.halo_rows else 1
    halos, refs = refs[1 + FIELDS : 1 + FIELDS + kinds * lanes], refs[1 + FIELDS + kinds * lanes :]
    n_out = 3 if part is WHOLE else lanes - 1
    outs, stacks, refs = refs[:n_out], refs[n_out : n_out + kinds], refs[n_out + kinds :]
    (
        level, flow_x, flow_y, ground, friction, ground_x, ground_y,
        s_level, s_flow_x, s_flow_y, s_ground, s_friction, s_ground_x, s_ground_y,
        sem_out,
    ) = refs
    block = (level, flow_x, flow_y, ground, friction)
    strip = (s_level, s_flow_x, s_flow_y, s_ground, s_friction)
    lane = lane_index()
    last, first = lane == SIDE - 1, lane == 0

    def entry(i):
        at = part.base + i * ENTRY
        return table[at + 1], table[at + 2], table[at + 3]

    def near_wet(i, name):
        return table[part.base + i * ENTRY + 4 + 3 * NEAR[name]]

    for k in range(lanes):
        for n in range(kinds):
            if n:
                for side in range(2):
                    for t in range(fields[0].shape[0]):
                        stacks[1][k, side, t, SPARE : SPARE + TILE_ROWS, :] = halos[kinds * k + 1][
                            side, TILE_ROWS * t : TILE_ROWS * (t + 1), :
                        ]
            else:
                unpack_columns(part, halos[kinds * k], stacks[0].at[k])
    for i in range(NT):
        base = part.base + i * ENTRY
        assemble(part, table, base, i, entry(i)[1], fields, stacks, block, strip)
    prepare_strip(part, near_wet, strip, s_ground_x, s_ground_y)
    for i in range(NT):
        prepare_tile(part, near_wet, i, block, ground_x, ground_y, s_ground)

    def step(_, carry):
        for r, rows in part.chunks():
            at, south = pl.ds(r, rows), pl.ds(r + 1, rows)
            e, c = s_level[at, :], s_friction[at, :]
            e_east = pltpu.roll(e, SIDE - 1, 1)
            s_flow_x[at, :] = face(s_flow_x[at, :], e, e_east, s_ground_x[at, :], c)
            s_flow_y[at, :] = face(s_flow_y[at, :], e, s_level[south, :], s_ground_y[at, :], c)
        for i in range(NT):
            for r, rows in part.chunks():
                at, south = pl.ds(r, rows), pl.ds(r + 1, rows)
                e, c = level[i, at, :], friction[i, at, :]
                e_east = jnp.where(
                    last, pltpu.roll(s_level[at, :], to_east(i), 1), pltpu.roll(e, SIDE - 1, 1)
                )
                flow_x[i, at, :] = face(flow_x[i, at, :], e, e_east, ground_x[i, at, :], c)
                flow_y[i, at, :] = face(
                    flow_y[i, at, :], e, level[i, south, :], ground_y[i, at, :], c
                )
        for r, rows in part.chunks():
            at, north = pl.ds(r, rows), pl.ds(r - 1, rows)
            qx = s_flow_x[at, :]
            s_level[at, :] = s_level[at, :] + RATE * (
                (pltpu.roll(qx, 1, 1) - qx) + (s_flow_y[north, :] - s_flow_y[at, :])
            )
        for i in range(NT):
            for r, rows in part.chunks():
                at, north = pl.ds(r, rows), pl.ds(r - 1, rows)
                qx = flow_x[i, at, :]
                qx_west = jnp.where(
                    first, pltpu.roll(s_flow_x[at, :], to_west(i), 1), pltpu.roll(qx, 1, 1)
                )
                level[i, at, :] = level[i, at, :] + RATE * (
                    (qx_west - qx) + (flow_y[i, north, :] - flow_y[i, at, :])
                )
        return carry

    lax.fori_loop(0, STEPS, step, 0)

    results = (level, flow_x, flow_y)
    for i in range(NT):
        wet, slot, _ = entry(i)
        for start, count in part.sent:
            own, at = pl.ds(start, count), pl.ds(TOP + start, count)
            level[i, at, :] = level[i, at, :] - ground[i, at, :]
            for f in range(3):
                results[f][i, at, :] = jnp.where(
                    wet == 1, results[f][i, at, :], fields[f][slot, own, :]
                )

    if part is not WHOLE:
        for i in range(NT):
            target = entry(i)[2]
            for k in range(1, lanes):
                @pl.when(divide(target, 2) == k)
                def _():
                    out = 0
                    for start, count in part.sent:
                        for f in range(3):
                            value = results[f][i, pl.ds(TOP + start, count), :]
                            outs[k - 1][remainder(target, 2), f, out : out + count, :] = value
                        out += count

    else:
        copies = [
            pltpu.make_async_copy(
                results[f].at[i, pl.ds(TOP, SIDE), :], outs[f].at[entry(i)[2]], sem_out.at[i, f]
            )
            for i in range(NT)
            for f in range(3)
        ]
        for copy in copies:
            copy.start()
        for copy in copies:
            copy.wait()


def advance(part, table, fields, halos):
    lanes = len(halos)
    sent = sum(count for _, count in part.sent)
    if part is WHOLE:
        outs = (jax.ShapeDtypeStruct(fields[0].shape, jnp.float32),) * 3
        out_specs = [pl.BlockSpec(memory_space=ANY)] * 3
    else:
        outs = (VMEM((2, 3, sent, SIDE), jnp.float32),) * (lanes - 1)
        out_specs = vmem_specs(lanes - 1)
    if not part.halo_rows:
        halos = [group[:1] for group in halos]
    flat = [array for group in halos for array in group]
    tile_count = fields[0].shape[0]
    stacks = [VMEM((lanes, -(-tile_count * TILE_LANES // SIDE), SIDE, SIDE), jnp.float32)]
    if part.halo_rows:
        stacks.append(VMEM((lanes, 2, tile_count, SPARE + TILE_ROWS + 1, SIDE), jnp.float32))
    block = VMEM((NT, ROWS, SIDE), jnp.float32)
    strip = VMEM((ROWS, SIDE), jnp.float32)
    cells = (NT + 1) * sum(count for _, count in part.computed) * SIDE * STEPS
    return pl.pallas_call(
        functools.partial(advance_kernel, part, lanes),
        name="advance_" + part.name,
        out_shape=outs,
        in_specs=[pl.BlockSpec(memory_space=SMEM)] + vmem_specs(FIELDS + len(flat)),
        out_specs=tuple(out_specs),
        scratch_shapes=stacks
        + [block] * 7
        + [strip] * 7
        + [pltpu.SemaphoreType.DMA((NT, 3))],
        compiler_params=pltpu.CompilerParams(vmem_limit_bytes=12 * 1024 * 1024),
        cost_estimate=pl.CostEstimate(
            flops=60 * cells, bytes_accessed=8 * NT * sent * SIDE * 4, transcendentals=6 * cells
        ),
    )(table, *fields, *flat)


def place_kernel(spans, lanes, *refs):
    table = refs[0]
    received = refs[1:lanes]
    outs = refs[lanes + 3 : lanes + 6]
    sem = refs[lanes + 6]

    def each(act):
        for k in range(1, lanes):
            for j in range(2):
                slot = table[RECEIVE + 2 * k + j]

                @pl.when(slot >= 0)
                def _():
                    at = 0
                    for n, (start, count) in enumerate(spans):
                        for f in range(3):
                            act(
                                pltpu.make_async_copy(
                                    received[k - 1].at[j, f, pl.ds(at, count), :],
                                    outs[f].at[slot, pl.ds(start, count), :],
                                    sem.at[k, j, f, n],
                                )
                            )
                        at += count

    each(lambda copy: copy.start())
    each(lambda copy: copy.wait())


def place(part, table, received, partial_outs):
    lanes = len(received) + 1
    return pl.pallas_call(
        functools.partial(place_kernel, part.sent, lanes),
        name="place_" + part.name,
        out_shape=tuple(jax.ShapeDtypeStruct(o.shape, o.dtype) for o in partial_outs),
        in_specs=[pl.BlockSpec(memory_space=SMEM)]
        + vmem_specs(lanes - 1)
        + [pl.BlockSpec(memory_space=ANY)] * 3,
        out_specs=tuple(pl.BlockSpec(memory_space=ANY) for _ in partial_outs),
        scratch_shapes=[pltpu.SemaphoreType.DMA((lanes, 2, 3, len(part.sent)))],
        input_output_aliases={lanes: 0, lanes + 1: 1, lanes + 2: 2},
        compiler_params=SMALL,
    )(table, *received, *partial_outs)


def shift_lanes(array, col_shift, sub_shift):
    cols, subs = lax.axis_size("col"), lax.axis_size("sub")
    pairs = [
        (c * subs + s, ((c + col_shift) % cols) * subs + (s + sub_shift) % subs)
        for c in range(cols)
        for s in range(subs)
    ]
    return lax.ppermute(array, ("col", "sub"), pairs)


def over_cols(array):
    return [array] + [shift_lanes(array, c, 0) for c in range(1, lax.axis_size("col"))]


def over_subs(parts):
    subs = lax.axis_size("sub")
    return [
        in_vmem(part if s == 0 else shift_lanes(part, 0, s)) for part in parts for s in range(subs)
    ]


def meet_rows(array, parity):
    rows, subs = lax.axis_size("row"), lax.axis_size("sub")
    pairs = []
    for r in range(rows):
        other = r + 1 if r % 2 == parity else r - 1
        for s in range(subs):
            if 0 <= other < rows:
                pairs.append((r * subs + s, other * subs + s))
            else:
                pairs.append((r * subs + s, r * subs + (s + 1) % subs))
    return lax.ppermute(array, ("row", "sub"), pairs)


def shards(
    water_depth, flow_east, flow_south, bed_level, manning_n, placed_before, placed_after, wet_tiles
):
    cols, subs = lax.axis_size("col"), lax.axis_size("sub")
    tile_count = water_depth.shape[0]
    *fields, columns, pair_even, pair_odd = load(
        (water_depth, flow_east, flow_south, bed_level, manning_n)
    )
    fields = [in_vmem(field) for field in fields]
    columns = over_cols(columns)
    met_even, met_odd = meet_rows(pair_even, 0), meet_rows(pair_odd, 1)
    table = make_table(
        (cols, subs, tile_count, placed_before.shape[0]), placed_before, placed_after, wet_tiles
    )
    joined = join(met_even, met_odd)
    near_rows = over_cols(joined)
    columns[1:], joined, table = lax.optimization_barrier((columns[1:], joined, table))
    near_rows[0] = joined
    table = pltpu.with_memory_space_constraint(table, SMEM)
    near_rows = over_subs(near_rows)
    columns = over_subs(columns)

    def send(parts):
        return [
            in_vmem(shift_lanes(parts[k - 1], k // subs, k % subs)) for k in range(1, cols * subs)
        ]

    middle = send(advance(EARLY, table, fields, [(part,) for part in columns]))
    halos = list(zip(columns, near_rows))
    edges = send(advance(LATE, table, fields, halos))
    outs = advance(WHOLE, table, fields, halos)
    outs = place(EARLY, table, middle, outs)
    return place(LATE, table, edges, outs)


def solution(mesh):
    tiles = P(("basin", "row", "col", "sub"), None, None)
    return jax.shard_map(
        shards,
        mesh=mesh,
        in_specs=(tiles,) * FIELDS + (P("basin"),) * 3,
        out_specs=(tiles,) * 3,
        check_vma=False,
    )
```

```python
import functools
import math

import jax
import jax.numpy as jnp
from jax import lax
from jax.experimental import pallas as pl
from jax.experimental.pallas import tpu as pltpu
from jax.sharding import PartitionSpec as P

STEPS = 6
GRAV = 9.81
STEP_TIME = 0.5
SPACING = 5.0
RATE = 0.1
DEPTH_FLOOR = 0.3

FIELDS = 5
HALO = STEPS
LAST_COLS = (HALO, HALO, HALO - 1, HALO, HALO)
FIRST_COLS = (HALO, HALO - 1, HALO - 1, HALO, HALO - 1)
LAST_ROWS = (HALO, HALO - 1, HALO, HALO, HALO)
FIRST_ROWS = (HALO, HALO - 1, HALO - 1, HALO, HALO - 1)


def starts(counts):
    return [sum(counts[:f]) for f in range(len(counts))]


BOTH_COLS = tuple(a + b for a, b in zip(LAST_COLS, FIRST_COLS))
TILE_LANES = sum(BOTH_COLS)
TILE_ROWS = max(sum(LAST_ROWS), sum(FIRST_ROWS))
COL_AT, LAST_AT, FIRST_AT = starts(BOTH_COLS), starts(LAST_ROWS), starts(FIRST_ROWS)
SIDE = 128
TOP = 16
ROWS = SIDE + 32
LO = 8
HI = SIDE + 24
CHUNK = 24
SPARE = 2
NT = 4
GROUP = SIDE // NT
CLOSED = 1e30
POWER = -(7.0 / 3.0) / math.log(2.0)

ENTRY = 32
NEAR = {"w": 0, "e": 1, "n": 2, "s": 3, "nw": 4, "ne": 5, "sw": 6, "se": 7}
STEP_TO = ((0, -1), (0, 1), (-1, 0), (1, 0), (-1, -1), (-1, 1), (1, -1), (1, 1))
LEAVE, STAY, RECEIVE = 0, NT * ENTRY, 2 * NT * ENTRY

SMEM = pltpu.SMEM
VMEM = pltpu.VMEM
ANY = pl.ANY
SMALL = pltpu.CompilerParams(vmem_limit_bytes=2 * 1024 * 1024)


def lane_index():
    return lax.broadcasted_iota(jnp.int32, (1, SIDE), 1)


def divide(value, size):
    if size & (size - 1):
        return lax.div(value, size)
    return lax.shift_right_logical(value, size.bit_length() - 1)


def remainder(value, size):
    if size & (size - 1):
        return lax.rem(value, size)
    return value & (size - 1)


def index_kernel(shape, before_ref, after_ref, wet_ref, table, inv_before, inv_after, count):
    cols, subs, tile_count, total = shape
    lanes = cols * subs
    row_tiles = lanes * tile_count
    tile_rows = total // row_tiles
    my_row, my_col, my_sub = (lax.axis_index(name) for name in ("row", "col", "sub"))
    me = my_row * lanes + my_col * subs + my_sub
    spare = RECEIVE + 2 * lanes

    def invert(s, carry):
        for u in range(16):
            inv_before[before_ref[s * 16 + u]] = s * 16 + u
            inv_after[after_ref[s * 16 + u]] = s * 16 + u
        return carry

    lax.fori_loop(0, total // 16, invert, 0)
    for i in range(lanes * 2):
        table[RECEIVE + i] = -1
    for i in range(lanes + 1):
        count[i] = 0

    def relative(lane, sign):
        col = remainder(sign * (divide(lane, subs) - my_col) + cols, cols)
        sub = remainder(sign * (remainder(lane, subs) - my_sub) + subs, subs)
        return col * subs + sub

    def own(s, carry):
        tile = before_ref[me * tile_count + s]
        device = divide(inv_after[tile], tile_count)
        stays = device == me
        to = relative(remainder(device, lanes), 1)
        nth = count[to]
        count[to] = nth + 1
        other = jnp.where(stays | (to == subs), 0, 1)
        left = count[lanes]
        count[lanes] = left + other
        place = jnp.minimum(jnp.where(other == 1, NT - 1 - left, nth), NT - 1)
        base = jnp.where(stays, STAY, LEAVE) + jnp.maximum(place, 0) * ENTRY
        table[base + 1] = wet_ref[tile]
        table[base + 2] = s
        table[base + 3] = jnp.where(stays, s, to * 2 + jnp.minimum(nth, 1))
        row, col = divide(tile, row_tiles), remainder(tile, row_tiles)
        for n, (dr, dc) in enumerate(STEP_TO):
            r, c = row + dr, col + dc
            there = (r >= 0) & (r < tile_rows) & (c >= 0) & (c < row_tiles)
            near = jnp.where(there, tile + (dr * row_tiles + dc), tile)
            at = inv_before[near]
            table[base + 4 + 3 * n] = jnp.where(there, wet_ref[near], 0)
            table[base + 5 + 3 * n] = relative(remainder(divide(at, tile_count), lanes), -1)
            table[base + 6 + 3 * n] = remainder(at, tile_count)
        return carry

    lax.fori_loop(0, tile_count, own, 0)

    for rel in range(1, lanes):
        col = remainder(my_col + (cols - rel // subs), cols)
        sub = remainder(my_sub + (subs - rel % subs), subs)
        device = my_row * lanes + col * subs + sub
        found = jnp.int32(0)
        for s in range(tile_count):
            at = inv_after[before_ref[device * tile_count + s]]
            mine = divide(at, tile_count) == me
            place = RECEIVE + rel * 2 + jnp.minimum(found, 1)
            table[jnp.where(mine, place, spare)] = remainder(at, tile_count)
            found = found + jnp.where(mine, 1, 0)


def make_table(shape, before, after, wet):
    cols, subs, _, total = shape
    return pl.pallas_call(
        functools.partial(index_kernel, shape),
        name="index_table",
        out_shape=SMEM((RECEIVE + 2 * cols * subs + 1,), jnp.int32),
        in_specs=[pl.BlockSpec(memory_space=SMEM)] * 3,
        out_specs=pl.BlockSpec(memory_space=SMEM),
        scratch_shapes=[
            SMEM((total,), jnp.int32),
            SMEM((total,), jnp.int32),
            SMEM((cols * subs + 1,), jnp.int32),
        ],
        compiler_params=SMALL,
    )(before, after, wet)


def in_vmem(array):
    return pltpu.with_memory_space_constraint(array, VMEM)


def vmem_specs(count):
    return [pl.BlockSpec(memory_space=VMEM)] * count


def load_kernel(*refs):
    sources, refs = refs[:FIELDS], refs[FIELDS:]
    fields, (columns, pair_even, pair_odd, first, last, sem, _) = refs[:FIELDS], refs[FIELDS:]
    spill = refs[-1]
    lane = lane_index()
    odd = remainder(lax.axis_index("row"), 2) == 1
    copies = [
        pltpu.make_async_copy(sources[f], fields[f], sem.at[f]) for f in range(FIELDS)
    ]
    for copy in copies:
        copy.start()
    tile_count = fields[0].shape[0]
    blocks = tile_count * TILE_LANES // SIDE
    for f in range(FIELDS):
        copies[f].wait()
        for b in range(blocks + 1):
            target, place = (columns, pl.ds(b * SIDE, SIDE)) if b < blocks else (spill, slice(None))
            packed = target[place, :]
            for t in range(tile_count):
                at = TILE_LANES * t + COL_AT[f] - b * SIDE
                if at < SIDE and at + BOTH_COLS[f] > 0:
                    moved = pltpu.roll(fields[f][t], (at + LAST_COLS[f]) % SIDE, 1)
                    packed = jnp.where((lane >= at) & (lane < at + BOTH_COLS[f]), moved, packed)
            target[place, :] = packed
        for t in range(tile_count):
            at, count = TILE_ROWS * t + FIRST_AT[f], FIRST_ROWS[f]
            first[at : at + count, :] = fields[f][t, :count, :]
            at, count = TILE_ROWS * t + LAST_AT[f], LAST_ROWS[f]
            last[at : at + count, :] = fields[f][t, SIDE - count :, :]
    half = SIDE // 2
    columns[blocks * SIDE :, :] = jnp.where(
        lane < half, spill[:half, :], pltpu.roll(spill[half:, :], half, 1)
    )
    pair_even[...] = jnp.where(odd, first[...], last[...])
    pair_odd[...] = jnp.where(odd, last[...], first[...])


def load(arrays):
    tile_count = arrays[0].shape[0]
    rows = VMEM((tile_count * TILE_ROWS, SIDE), jnp.float32)
    outs = [VMEM(array.shape, array.dtype) for array in arrays]
    outs += [VMEM((tile_count * TILE_LANES, SIDE), jnp.float32), rows, rows]
    return pl.pallas_call(
        load_kernel,
        name="load_and_pack",
        out_shape=tuple(outs),
        in_specs=[pl.BlockSpec(memory_space=pltpu.HBM)] * FIELDS,
        out_specs=tuple(vmem_specs(len(outs))),
        scratch_shapes=[
            rows,
            rows,
            pltpu.SemaphoreType.DMA((FIELDS,)),
            VMEM((SIDE, SIDE), jnp.float32),
        ],
        compiler_params=SMALL,
    )(*[pltpu.with_memory_space_constraint(array, pltpu.HBM) for array in arrays])


def join_kernel(met_even, met_odd, joined):
    odd = remainder(lax.axis_index("row"), 2) == 1
    joined[0] = jnp.where(odd, met_even[...], met_odd[...])
    joined[1] = jnp.where(odd, met_odd[...], met_even[...])


def join(met_even, met_odd):
    return pl.pallas_call(
        join_kernel,
        name="join_row_halos",
        out_shape=VMEM((2,) + met_even.shape, met_even.dtype),
        in_specs=vmem_specs(2),
        out_specs=pl.BlockSpec(memory_space=VMEM),
        compiler_params=SMALL,
    )(in_vmem(met_even), in_vmem(met_odd))


def face(flow, level, level_next, ground, friction):
    wetted = jnp.maximum(level, level_next) - ground
    drive = (GRAV * STEP_TIME / SPACING) * jnp.maximum(wetted, 0.0) * (level_next - level)
    power = jnp.exp2(POWER * jnp.log(jnp.maximum(wetted, DEPTH_FLOOR)))
    return (flow - drive) / (1.0 + friction * jnp.abs(flow) * power)


class Part:
    def __init__(self, name, base, tiles, computed, own, halo_rows, sent):
        self.name = name
        self.base = base
        self.tiles = tiles
        self.computed = computed
        self.own = own
        self.halo_rows = halo_rows
        self.sent = sent

    def chunks(self):
        for start, count in self.computed:
            for r in range(start, start + count, CHUNK):
                yield r, min(CHUNK, start + count - r)


def row_span(span):
    return pl.ds(span[0], span[1])


EDGE = 8
BAND = 24
MIDDLE = (EDGE, SIDE - 2 * EDGE)
EARLY = (
    Part("leaving_first", LEAVE, 2, ((TOP, SIDE),), ((0, SIDE),), False, (MIDDLE,)),
    Part("leaving_second", LEAVE + 2 * ENTRY, 2, ((TOP, SIDE),), ((0, SIDE),), False, (MIDDLE,)),
)
LATE = Part(
    "leaving_edges",
    LEAVE,
    NT,
    ((LO, BAND), (HI - BAND, BAND)),
    ((0, BAND - 8), (SIDE - BAND + 8, BAND - 8)),
    True,
    ((0, EDGE), (SIDE - EDGE, EDGE)),
)
WHOLE = Part("staying", STAY, NT, ((LO, HI - LO),), ((0, SIDE),), True, ((0, SIDE),))


def row_bands(r, rows, above, middle, below):
    row = r + lax.broadcasted_iota(jnp.int32, (rows, 1), 0)
    return jnp.where(row < TOP, above, jnp.where(row < TOP + SIDE, middle, below))


def assemble(part, table, base, i, slot, fields, stacks, block, strip):
    halo_cols = stacks[0]
    lane = lane_index()
    at = GROUP * i

    def near(name):
        place = base + 5 + 3 * NEAR[name]
        return table[place], table[place + 1]

    def inside(lo, hi):
        return (lane >= at + lo) & (lane < at + hi)

    west, east = near("w"), near("e")
    for f in range(FIELDS):

        def ends(side, start, middle, left, right, out):
            rows = pl.ds(start, 8)
            mid, left_end, right_end = (
                stacks[1][place[0], side, place[1], rows, :] for place in (middle, left, right)
            )
            block[f][i, out : out + 8, :] = mid
            lower = jnp.where(lane < SIDE // 2, mid, left_end)
            upper = jnp.where(lane < SIDE // 2, right_end, mid)
            value = jnp.where(
                inside(0, 16),
                pltpu.roll(lower, (at + 8) % SIDE, 1),
                pltpu.roll(upper, (at + 24) % SIDE, 1),
            )
            if i:
                value = jnp.where(inside(0, GROUP), value, strip[f][out : out + 8, :])
            strip[f][out : out + 8, :] = value

        if part.halo_rows:
            start = SPARE + LAST_AT[f] + LAST_ROWS[f] - 8
            ends(0, start, near("n"), near("nw"), near("ne"), LO)
            ends(1, SPARE + FIRST_AT[f], near("s"), near("sw"), near("se"), TOP + SIDE)

        for start, count in part.own:
            own, out = pl.ds(start, count), pl.ds(TOP + start, count)

            def shifted(place, offset, goal):
                lanes_at = TILE_LANES * place[1] + (COL_AT[f] + offset)
                b, source = divide(lanes_at, SIDE), remainder(lanes_at, SIDE)
                beyond = jnp.minimum(b + 1, halo_cols.shape[1] - 1)
                value = jnp.where(
                    lane >= source, halo_cols[place[0], b, own, :], halo_cols[place[0], beyond, own, :]
                )
                return pltpu.roll(value, remainder(goal - source + SIDE, SIDE), 1)

            core = fields[f][slot, own, :]
            block[f][i, out, :] = core
            value = shifted(west, 0, at + 8 - LAST_COLS[f])
            if i:
                value = jnp.where(inside(0, 8), value, strip[f][out, :])
            value = jnp.where(inside(8, 16), pltpu.roll(core, (at + 8) % SIDE, 1), value)
            value = jnp.where(inside(16, 24), pltpu.roll(core, (at + 24) % SIDE, 1), value)
            value = jnp.where(inside(24, GROUP), shifted(east, LAST_COLS[f], at + 24), value)
            strip[f][out, :] = value


def prepare_strip(part, near_wet, strip, ground_x, ground_y):
    level, flow_x, flow_y, ground, friction = strip
    lane = lane_index()

    def lane_wet(center, left, right):
        value = jnp.zeros((1, SIDE), jnp.int32)
        for i in range(part.tiles):
            at = GROUP * i
            middle = near_wet(i, center) if center else 1
            sides = jnp.where(
                lane < at + 8,
                near_wet(i, left),
                jnp.where(lane < at + 24, middle, near_wet(i, right)),
            )
            value = jnp.where((lane >= at) & (lane < at + GROUP), sides, value)
        return value

    bands = (lane_wet("n", "nw", "ne"), lane_wet(None, "w", "e"), lane_wet("s", "sw", "se"))
    for r, rows in part.chunks():
        at, south = pl.ds(r, rows), pl.ds(r + 1, rows)
        z = ground[at, :]
        here, next_row = row_bands(r, rows, *bands), row_bands(r + 1, rows, *bands)
        open_x = (here == 1) & (pltpu.roll(here, SIDE - 1, 1) == 1)
        open_y = (here == 1) & (next_row == 1)
        z_east = pltpu.roll(z, SIDE - 1, 1)
        ground_x[at, :] = jnp.where(open_x, jnp.maximum(z, z_east), CLOSED)
        ground_y[at, :] = jnp.where(open_y, jnp.maximum(z, ground[south, :]), CLOSED)
        flow_x[at, :] = jnp.where(open_x, flow_x[at, :], 0.0)
        flow_y[at, :] = jnp.where(open_y, flow_y[at, :], 0.0)
        friction[at, :] = (GRAV * STEP_TIME) * friction[at, :] * friction[at, :]
        level[at, :] = level[at, :] + z


def prepare_tile(part, near_wet, i, block, ground_x, ground_y, strip_ground):
    level, flow_x, flow_y, ground, friction = block
    lane = lane_index()
    last = lane == SIDE - 1
    n, e, s = near_wet(i, "n"), near_wet(i, "e"), near_wet(i, "s")
    bands = (
        jnp.where(last, n * near_wet(i, "ne"), n),
        jnp.where(last, e, 1),
        jnp.where(last, s * near_wet(i, "se"), s),
    )
    for r, rows in part.chunks():
        at, south = pl.ds(r, rows), pl.ds(r + 1, rows)
        z = ground[i, at, :]
        z_east = jnp.where(
            last, pltpu.roll(strip_ground[at, :], to_east(i), 1), pltpu.roll(z, SIDE - 1, 1)
        )
        open_x = row_bands(r, rows, *bands) == 1
        open_y = (row_bands(r + 1, rows, n, 1, s) == 1) & (row_bands(r, rows, n, 1, s) == 1)
        ground_x[i, at, :] = jnp.where(open_x, jnp.maximum(z, z_east), CLOSED)
        ground_y[i, at, :] = jnp.where(open_y, jnp.maximum(z, ground[i, south, :]), CLOSED)
        flow_x[i, at, :] = jnp.where(open_x, flow_x[i, at, :], 0.0)
        flow_y[i, at, :] = jnp.where(open_y, flow_y[i, at, :], 0.0)
        friction[i, at, :] = (GRAV * STEP_TIME) * friction[i, at, :] * friction[i, at, :]
        level[i, at, :] = level[i, at, :] + z


def to_east(i):
    return (SIDE - 1 - GROUP * i - 24) % SIDE


def to_west(i):
    return (SIDE - GROUP * i - 7) % SIDE


def unpack_columns(part, packed, out):
    blocks, half = out.shape[0] - 1, SIDE // 2
    for start, count in part.own:
        rows = pl.ds(start, count)
        for b in range(blocks):
            out[b, rows, :] = packed[b * SIDE + start : b * SIDE + start + count, :]
        if start < half:
            n = min(count, half - start)
            out[blocks, start : start + n, :] = packed[
                blocks * SIDE + start : blocks * SIDE + start + n, :
            ]
        if start + count > half:
            low, high = max(start, half), start + count
            lower = packed[blocks * SIDE + low - half : blocks * SIDE + high - half, :]
            out[blocks, low:high, :] = pltpu.roll(lower, half, 1)


def advance_kernel(part, lanes, units, given, *refs):
    table = refs[0]
    fields = refs[1 : 1 + FIELDS]
    kinds = 2 if part.halo_rows else 1
    halos, refs = refs[1 + FIELDS : 1 + FIELDS + kinds * lanes], refs[1 + FIELDS + kinds * lanes :]
    refs = refs[given:]
    n_out = 3 if part is WHOLE else len(units)
    outs, stacks, refs = refs[:n_out], refs[n_out : n_out + kinds], refs[n_out + kinds :]
    (
        level, flow_x, flow_y, ground, friction, ground_x, ground_y,
        s_level, s_flow_x, s_flow_y, s_ground, s_friction, s_ground_x, s_ground_y,
        sem_out,
    ) = refs
    block = (level, flow_x, flow_y, ground, friction)
    strip = (s_level, s_flow_x, s_flow_y, s_ground, s_friction)
    lane = lane_index()
    last, first = lane == SIDE - 1, lane == 0

    def entry(i):
        at = part.base + i * ENTRY
        return table[at + 1], table[at + 2], table[at + 3]

    def near_wet(i, name):
        return table[part.base + i * ENTRY + 4 + 3 * NEAR[name]]

    for k in range(lanes):
        for n in range(kinds):
            if n:
                for side in range(2):
                    for t in range(fields[0].shape[0]):
                        stacks[1][k, side, t, SPARE : SPARE + TILE_ROWS, :] = halos[kinds * k + 1][
                            side, TILE_ROWS * t : TILE_ROWS * (t + 1), :
                        ]
            else:
                unpack_columns(part, halos[kinds * k], stacks[0].at[k])
    for i in range(part.tiles):
        base = part.base + i * ENTRY
        assemble(part, table, base, i, entry(i)[1], fields, stacks, block, strip)
    prepare_strip(part, near_wet, strip, s_ground_x, s_ground_y)
    for i in range(part.tiles):
        prepare_tile(part, near_wet, i, block, ground_x, ground_y, s_ground)

    def step(_, carry):
        for r, rows in part.chunks():
            at, south = pl.ds(r, rows), pl.ds(r + 1, rows)
            e, c = s_level[at, :], s_friction[at, :]
            e_east = pltpu.roll(e, SIDE - 1, 1)
            s_flow_x[at, :] = face(s_flow_x[at, :], e, e_east, s_ground_x[at, :], c)
            s_flow_y[at, :] = face(s_flow_y[at, :], e, s_level[south, :], s_ground_y[at, :], c)
        for i in range(part.tiles):
            for r, rows in part.chunks():
                at, south = pl.ds(r, rows), pl.ds(r + 1, rows)
                e, c = level[i, at, :], friction[i, at, :]
                e_east = jnp.where(
                    last, pltpu.roll(s_level[at, :], to_east(i), 1), pltpu.roll(e, SIDE - 1, 1)
                )
                flow_x[i, at, :] = face(flow_x[i, at, :], e, e_east, ground_x[i, at, :], c)
                flow_y[i, at, :] = face(
                    flow_y[i, at, :], e, level[i, south, :], ground_y[i, at, :], c
                )
        for r, rows in part.chunks():
            at, north = pl.ds(r, rows), pl.ds(r - 1, rows)
            qx = s_flow_x[at, :]
            s_level[at, :] = s_level[at, :] + RATE * (
                (pltpu.roll(qx, 1, 1) - qx) + (s_flow_y[north, :] - s_flow_y[at, :])
            )
        for i in range(part.tiles):
            for r, rows in part.chunks():
                at, north = pl.ds(r, rows), pl.ds(r - 1, rows)
                qx = flow_x[i, at, :]
                qx_west = jnp.where(
                    first, pltpu.roll(s_flow_x[at, :], to_west(i), 1), pltpu.roll(qx, 1, 1)
                )
                level[i, at, :] = level[i, at, :] + RATE * (
                    (qx_west - qx) + (flow_y[i, north, :] - flow_y[i, at, :])
                )
        return carry

    lax.fori_loop(0, STEPS, step, 0)

    results = (level, flow_x, flow_y)
    for i in range(part.tiles):
        wet, slot, _ = entry(i)
        for start, count in part.sent:
            own, at = pl.ds(start, count), pl.ds(TOP + start, count)
            level[i, at, :] = level[i, at, :] - ground[i, at, :]
            for f in range(3):
                results[f][i, at, :] = jnp.where(
                    wet == 1, results[f][i, at, :], fields[f][slot, own, :]
                )

    if part is not WHOLE:
        for i in range(part.tiles):
            target = entry(i)[2]
            for out_ref, k in zip(outs, units):
                @pl.when(divide(target, 2) == k)
                def _():
                    out = 0
                    for start, count in part.sent:
                        for f in range(3):
                            value = results[f][i, pl.ds(TOP + start, count), :]
                            out_ref[remainder(target, 2), f, out : out + count, :] = value
                        out += count

    else:
        copies = [
            pltpu.make_async_copy(
                results[f].at[i, pl.ds(TOP, SIDE), :], outs[f].at[entry(i)[2]], sem_out.at[i, f]
            )
            for i in range(part.tiles)
            for f in range(3)
        ]
        for copy in copies:
            copy.start()
        for copy in copies:
            copy.wait()


def advance(part, table, fields, halos, units=(), partial=()):
    lanes = len(halos)
    sent = sum(count for _, count in part.sent)
    if part is WHOLE:
        outs = (jax.ShapeDtypeStruct(fields[0].shape, jnp.float32),) * 3
        out_specs = [pl.BlockSpec(memory_space=ANY)] * 3
    else:
        outs = (VMEM((2, 3, sent, SIDE), jnp.float32),) * len(units)
        out_specs = vmem_specs(len(units))
    if not part.halo_rows:
        halos = [group[:1] for group in halos]
    flat = [array for group in halos for array in group]
    tile_count = fields[0].shape[0]
    stacks = [VMEM((lanes, -(-tile_count * TILE_LANES // SIDE), SIDE, SIDE), jnp.float32)]
    if part.halo_rows:
        stacks.append(VMEM((lanes, 2, tile_count, SPARE + TILE_ROWS + 1, SIDE), jnp.float32))
    block = VMEM((part.tiles, ROWS, SIDE), jnp.float32)
    strip = VMEM((ROWS, SIDE), jnp.float32)
    cells = (part.tiles + 1) * sum(count for _, count in part.computed) * SIDE * STEPS
    return pl.pallas_call(
        functools.partial(advance_kernel, part, lanes, units, len(partial)),
        name="advance_" + part.name,
        out_shape=outs,
        in_specs=[pl.BlockSpec(memory_space=SMEM)]
        + vmem_specs(FIELDS + len(flat) + len(partial)),
        input_output_aliases={1 + FIELDS + len(flat) + n: n for n in range(len(partial))},
        out_specs=tuple(out_specs),
        scratch_shapes=stacks
        + [block] * 7
        + [strip] * 7
        + [pltpu.SemaphoreType.DMA((part.tiles, 3))],
        compiler_params=pltpu.CompilerParams(vmem_limit_bytes=12 * 1024 * 1024),
        cost_estimate=pl.CostEstimate(
            flops=60 * cells, bytes_accessed=8 * part.tiles * sent * SIDE * 4, transcendentals=6 * cells
        ),
    )(table, *fields, *flat, *partial)


def place_kernel(spans, lanes, *refs):
    table = refs[0]
    received = refs[1:lanes]
    outs = refs[lanes + 3 : lanes + 6]
    sem = refs[lanes + 6]

    def each(act):
        for k in range(1, lanes):
            for j in range(2):
                slot = table[RECEIVE + 2 * k + j]

                @pl.when(slot >= 0)
                def _():
                    at = 0
                    for n, (start, count) in enumerate(spans):
                        for f in range(3):
                            act(
                                pltpu.make_async_copy(
                                    received[k - 1].at[j, f, pl.ds(at, count), :],
                                    outs[f].at[slot, pl.ds(start, count), :],
                                    sem.at[k, j, f, n],
                                )
                            )
                        at += count

    each(lambda copy: copy.start())
    each(lambda copy: copy.wait())


def place(name, spans, table, received, partial_outs):
    lanes = len(received) + 1
    return pl.pallas_call(
        functools.partial(place_kernel, spans, lanes),
        name="place_" + name,
        out_shape=tuple(jax.ShapeDtypeStruct(o.shape, o.dtype) for o in partial_outs),
        in_specs=[pl.BlockSpec(memory_space=SMEM)]
        + vmem_specs(lanes - 1)
        + [pl.BlockSpec(memory_space=ANY)] * 3,
        out_specs=tuple(pl.BlockSpec(memory_space=ANY) for _ in partial_outs),
        scratch_shapes=[pltpu.SemaphoreType.DMA((lanes, 2, 3, len(spans)))],
        input_output_aliases={lanes: 0, lanes + 1: 1, lanes + 2: 2},
        compiler_params=SMALL,
    )(table, *received, *partial_outs)


def shift_lanes(array, col_shift, sub_shift):
    cols, subs = lax.axis_size("col"), lax.axis_size("sub")
    pairs = [
        (c * subs + s, ((c + col_shift) % cols) * subs + (s + sub_shift) % subs)
        for c in range(cols)
        for s in range(subs)
    ]
    return lax.ppermute(array, ("col", "sub"), pairs)


def over_cols(array):
    return [array] + [shift_lanes(array, c, 0) for c in range(1, lax.axis_size("col"))]


def over_subs(parts):
    subs = lax.axis_size("sub")
    return [
        in_vmem(part if s == 0 else shift_lanes(part, 0, s)) for part in parts for s in range(subs)
    ]


def meet_rows(array, parity):
    rows, subs = lax.axis_size("row"), lax.axis_size("sub")
    pairs = []
    for r in range(rows):
        other = r + 1 if r % 2 == parity else r - 1
        for s in range(subs):
            if 0 <= other < rows:
                pairs.append((r * subs + s, other * subs + s))
            else:
                pairs.append((r * subs + s, r * subs + (s + 1) % subs))
    return lax.ppermute(array, ("row", "sub"), pairs)


def shards(
    water_depth, flow_east, flow_south, bed_level, manning_n, placed_before, placed_after, wet_tiles
):
    cols, subs = lax.axis_size("col"), lax.axis_size("sub")
    tile_count = water_depth.shape[0]
    *fields, columns, pair_even, pair_odd = load(
        (water_depth, flow_east, flow_south, bed_level, manning_n)
    )
    fields = [in_vmem(field) for field in fields]
    columns = over_cols(columns)
    met_even, met_odd = meet_rows(pair_even, 0), meet_rows(pair_odd, 1)
    table = make_table(
        (cols, subs, tile_count, placed_before.shape[0]), placed_before, placed_after, wet_tiles
    )
    joined = join(met_even, met_odd)
    near_rows = over_cols(joined)
    columns[1:], joined, table = lax.optimization_barrier((columns[1:], joined, table))
    near_rows[0] = joined
    table = pltpu.with_memory_space_constraint(table, SMEM)
    near_rows = over_subs(near_rows)
    columns = over_subs(columns)

    def send(part, k):
        return in_vmem(shift_lanes(part, k // subs, k % subs))

    units = tuple(range(1, cols * subs))
    ahead, others = subs, tuple(k for k in units if k != subs)
    alone = [(part,) for part in columns]
    first, *rest = advance(EARLY[0], table, fields, alone, (ahead,) + others)
    rest = advance(EARLY[1], table, fields, alone, others, [in_vmem(part) for part in rest])
    middle = {ahead: send(first, ahead)}
    middle.update((k, send(part, k)) for k, part in zip(others, rest))
    halos = list(zip(columns, near_rows))
    edges = advance(LATE, table, fields, halos, units)
    middle[ahead], edges = lax.optimization_barrier((middle[ahead], edges))
    middle[ahead] = in_vmem(middle[ahead])
    edges = [send(part, k) for k, part in zip(units, edges)]
    outs = advance(WHOLE, table, fields, halos)
    outs = place("middle", EARLY[0].sent, table, [middle[k] for k in units], outs)
    return place("edges", LATE.sent, table, edges, outs)


def solution(mesh):
    tiles = P(("basin", "row", "col", "sub"), None, None)
    return jax.shard_map(
        shards,
        mesh=mesh,
        in_specs=(tiles,) * FIELDS + (P("basin"),) * 3,
        out_specs=(tiles,) * 3,
        check_vma=False,
    )
```

```python
import functools
import math

import jax
import jax.numpy as jnp
from jax import lax
from jax.experimental import pallas as pl
from jax.experimental.pallas import tpu as pltpu
from jax.sharding import PartitionSpec as P

STEPS = 6
GRAV = 9.81
STEP_TIME = 0.5
SPACING = 5.0
RATE = 0.1
DEPTH_FLOOR = 0.3

FIELDS = 5
HALO = STEPS
LAST_COLS = (HALO, HALO, HALO - 1, HALO, HALO)
FIRST_COLS = (HALO, HALO - 1, HALO - 1, HALO, HALO - 1)
LAST_ROWS = (HALO, HALO - 1, HALO, HALO, HALO)
FIRST_ROWS = (HALO, HALO - 1, HALO - 1, HALO, HALO - 1)


def starts(counts):
    return [sum(counts[:f]) for f in range(len(counts))]


BOTH_COLS = tuple(a + b for a, b in zip(LAST_COLS, FIRST_COLS))
TILE_LANES = sum(BOTH_COLS)
TILE_ROWS = max(sum(LAST_ROWS), sum(FIRST_ROWS))
COL_AT, LAST_AT, FIRST_AT = starts(BOTH_COLS), starts(LAST_ROWS), starts(FIRST_ROWS)
SIDE = 128
TOP = 16
ROWS = SIDE + 32
LO = 8
HI = SIDE + 24
CHUNK = 24
SPARE = 2
NT = 4
GROUP = SIDE // NT
CLOSED = 1e30
POWER = -(7.0 / 3.0) / math.log(2.0)

ENTRY = 32
NEAR = {"w": 0, "e": 1, "n": 2, "s": 3, "nw": 4, "ne": 5, "sw": 6, "se": 7}
STEP_TO = ((0, -1), (0, 1), (-1, 0), (1, 0), (-1, -1), (-1, 1), (1, -1), (1, 1))
LEAVE, STAY, RECEIVE = 0, NT * ENTRY, 2 * NT * ENTRY

SMEM = pltpu.SMEM
VMEM = pltpu.VMEM
ANY = pl.ANY
SMALL = pltpu.CompilerParams(vmem_limit_bytes=2 * 1024 * 1024)


def lane_index():
    return lax.broadcasted_iota(jnp.int32, (1, SIDE), 1)


def divide(value, size):
    if size & (size - 1):
        return lax.div(value, size)
    return lax.shift_right_logical(value, size.bit_length() - 1)


def remainder(value, size):
    if size & (size - 1):
        return lax.rem(value, size)
    return value & (size - 1)


def index_kernel(shape, before_ref, after_ref, wet_ref, table, inv_before, inv_after, count):
    cols, subs, tile_count, total = shape
    lanes = cols * subs
    row_tiles = lanes * tile_count
    tile_rows = total // row_tiles
    my_row, my_col, my_sub = (lax.axis_index(name) for name in ("row", "col", "sub"))
    me = my_row * lanes + my_col * subs + my_sub
    spare = RECEIVE + 2 * lanes

    def invert(s, carry):
        for u in range(16):
            inv_before[before_ref[s * 16 + u]] = s * 16 + u
            inv_after[after_ref[s * 16 + u]] = s * 16 + u
        return carry

    lax.fori_loop(0, total // 16, invert, 0)
    for i in range(lanes * 2):
        table[RECEIVE + i] = -1
    for i in range(lanes + 1):
        count[i] = 0

    def relative(lane, sign):
        col = remainder(sign * (divide(lane, subs) - my_col) + cols, cols)
        sub = remainder(sign * (remainder(lane, subs) - my_sub) + subs, subs)
        return col * subs + sub

    def own(s, carry):
        tile = before_ref[me * tile_count + s]
        device = divide(inv_after[tile], tile_count)
        stays = device == me
        to = relative(remainder(device, lanes), 1)
        nth = count[to]
        count[to] = nth + 1
        other = jnp.where(stays | (to == subs), 0, 1)
        left = count[lanes]
        count[lanes] = left + other
        place = jnp.minimum(jnp.where(other == 1, NT - 1 - left, nth), NT - 1)
        base = jnp.where(stays, STAY, LEAVE) + jnp.maximum(place, 0) * ENTRY
        table[base + 1] = wet_ref[tile]
        table[base + 2] = s
        table[base + 3] = jnp.where(stays, s, to * 2 + jnp.minimum(nth, 1))
        row, col = divide(tile, row_tiles), remainder(tile, row_tiles)
        for n, (dr, dc) in enumerate(STEP_TO):
            r, c = row + dr, col + dc
            there = (r >= 0) & (r < tile_rows) & (c >= 0) & (c < row_tiles)
            near = jnp.where(there, tile + (dr * row_tiles + dc), tile)
            at = inv_before[near]
            table[base + 4 + 3 * n] = jnp.where(there, wet_ref[near], 0)
            table[base + 5 + 3 * n] = relative(remainder(divide(at, tile_count), lanes), -1)
            table[base + 6 + 3 * n] = remainder(at, tile_count)
        return carry

    lax.fori_loop(0, tile_count, own, 0)

    for rel in range(1, lanes):
        col = remainder(my_col + (cols - rel // subs), cols)
        sub = remainder(my_sub + (subs - rel % subs), subs)
        device = my_row * lanes + col * subs + sub
        found = jnp.int32(0)
        for s in range(tile_count):
            at = inv_after[before_ref[device * tile_count + s]]
            mine = divide(at, tile_count) == me
            place = RECEIVE + rel * 2 + jnp.minimum(found, 1)
            table[jnp.where(mine, place, spare)] = remainder(at, tile_count)
            found = found + jnp.where(mine, 1, 0)


def make_table(shape, before, after, wet):
    cols, subs, _, total = shape
    return pl.pallas_call(
        functools.partial(index_kernel, shape),
        name="index_table",
        out_shape=SMEM((RECEIVE + 2 * cols * subs + 1,), jnp.int32),
        in_specs=[pl.BlockSpec(memory_space=SMEM)] * 3,
        out_specs=pl.BlockSpec(memory_space=SMEM),
        scratch_shapes=[
            SMEM((total,), jnp.int32),
            SMEM((total,), jnp.int32),
            SMEM((cols * subs + 1,), jnp.int32),
        ],
        compiler_params=SMALL,
    )(before, after, wet)


def in_vmem(array):
    return pltpu.with_memory_space_constraint(array, VMEM)


def vmem_specs(count):
    return [pl.BlockSpec(memory_space=VMEM)] * count


def load_kernel(*refs):
    sources, refs = refs[:FIELDS], refs[FIELDS:]
    fields, (columns, pair_even, pair_odd, first, last, sem, _) = refs[:FIELDS], refs[FIELDS:]
    spill = refs[-1]
    lane = lane_index()
    odd = remainder(lax.axis_index("row"), 2) == 1
    copies = [
        pltpu.make_async_copy(sources[f], fields[f], sem.at[f]) for f in range(FIELDS)
    ]
    for copy in copies:
        copy.start()
    tile_count = fields[0].shape[0]
    blocks = tile_count * TILE_LANES // SIDE
    for f in range(FIELDS):
        copies[f].wait()
        for b in range(blocks + 1):
            target, place = (columns, pl.ds(b * SIDE, SIDE)) if b < blocks else (spill, slice(None))
            packed = target[place, :]
            for t in range(tile_count):
                at = TILE_LANES * t + COL_AT[f] - b * SIDE
                if at < SIDE and at + BOTH_COLS[f] > 0:
                    moved = pltpu.roll(fields[f][t], (at + LAST_COLS[f]) % SIDE, 1)
                    packed = jnp.where((lane >= at) & (lane < at + BOTH_COLS[f]), moved, packed)
            target[place, :] = packed
        for t in range(tile_count):
            at, count = TILE_ROWS * t + FIRST_AT[f], FIRST_ROWS[f]
            first[at : at + count, :] = fields[f][t, :count, :]
            at, count = TILE_ROWS * t + LAST_AT[f], LAST_ROWS[f]
            last[at : at + count, :] = fields[f][t, SIDE - count :, :]
    half = SIDE // 2
    columns[blocks * SIDE :, :] = jnp.where(
        lane < half, spill[:half, :], pltpu.roll(spill[half:, :], half, 1)
    )
    pair_even[...] = jnp.where(odd, first[...], last[...])
    pair_odd[...] = jnp.where(odd, last[...], first[...])


def load(arrays):
    tile_count = arrays[0].shape[0]
    rows = VMEM((tile_count * TILE_ROWS, SIDE), jnp.float32)
    outs = [VMEM(array.shape, array.dtype) for array in arrays]
    outs += [VMEM((tile_count * TILE_LANES, SIDE), jnp.float32), rows, rows]
    return pl.pallas_call(
        load_kernel,
        name="load_and_pack",
        out_shape=tuple(outs),
        in_specs=[pl.BlockSpec(memory_space=pltpu.HBM)] * FIELDS,
        out_specs=tuple(vmem_specs(len(outs))),
        scratch_shapes=[
            rows,
            rows,
            pltpu.SemaphoreType.DMA((FIELDS,)),
            VMEM((SIDE, SIDE), jnp.float32),
        ],
        compiler_params=SMALL,
    )(*[pltpu.with_memory_space_constraint(array, pltpu.HBM) for array in arrays])


def join_kernel(met_even, met_odd, joined):
    odd = remainder(lax.axis_index("row"), 2) == 1
    joined[0] = jnp.where(odd, met_even[...], met_odd[...])
    joined[1] = jnp.where(odd, met_odd[...], met_even[...])


def join(met_even, met_odd):
    return pl.pallas_call(
        join_kernel,
        name="join_row_halos",
        out_shape=VMEM((2,) + met_even.shape, met_even.dtype),
        in_specs=vmem_specs(2),
        out_specs=pl.BlockSpec(memory_space=VMEM),
        compiler_params=SMALL,
    )(in_vmem(met_even), in_vmem(met_odd))


def arrivals(table, units, received, spans, outs, sem):
    def each(act):
        for n, k in enumerate(units):
            for j in range(2):
                slot = table[RECEIVE + 2 * k + j]

                @pl.when(slot >= 0)
                def _():
                    at = 0
                    for m, (start, count) in enumerate(spans):
                        for f in range(3):
                            act(
                                pltpu.make_async_copy(
                                    received[n].at[j, f, pl.ds(at, count), :],
                                    outs[f].at[slot, pl.ds(start, count), :],
                                    sem.at[n, j, f, m],
                                )
                            )
                        at += count

    return each


def place_kernel(groups, *refs):
    table, received, refs = refs[0], refs[1 : 1 + len(groups)], refs[1 + len(groups) :]
    outs, sem = refs[3:6], refs[6]
    copies = [
        arrivals(table, (k,), (array,), spans, outs, sem.at[pl.ds(n, 1)])
        for n, ((k, spans), array) in enumerate(zip(groups, received))
    ]
    for each in copies:
        each(lambda copy: copy.start())
    for each in copies:
        each(lambda copy: copy.wait())


def place(groups, table, received, partial_outs):
    count = len(received)
    return pl.pallas_call(
        functools.partial(place_kernel, groups),
        name="place_arrivals",
        out_shape=tuple(jax.ShapeDtypeStruct(o.shape, o.dtype) for o in partial_outs),
        in_specs=[pl.BlockSpec(memory_space=SMEM)]
        + vmem_specs(count)
        + [pl.BlockSpec(memory_space=ANY)] * 3,
        out_specs=tuple(pl.BlockSpec(memory_space=ANY) for _ in partial_outs),
        scratch_shapes=[pltpu.SemaphoreType.DMA((count, 2, 3, 2))],
        input_output_aliases={1 + count + f: f for f in range(3)},
        compiler_params=SMALL,
    )(table, *received, *partial_outs)


def face(flow, level, level_next, ground, friction):
    wetted = jnp.maximum(level, level_next) - ground
    drive = (GRAV * STEP_TIME / SPACING) * jnp.maximum(wetted, 0.0) * (level_next - level)
    power = jnp.exp2(POWER * jnp.log(jnp.maximum(wetted, DEPTH_FLOOR)))
    return (flow - drive) / (1.0 + friction * jnp.abs(flow) * power)


class Part:
    def __init__(self, name, base, tiles, computed, own, halo_rows, sent):
        self.name = name
        self.base = base
        self.tiles = tiles
        self.computed = computed
        self.own = own
        self.halo_rows = halo_rows
        self.sent = sent

    def chunks(self):
        for start, count in self.computed:
            for r in range(start, start + count, CHUNK):
                yield r, min(CHUNK, start + count - r)


def row_span(span):
    return pl.ds(span[0], span[1])


EDGE = 8
BAND = 24
MIDDLE = (EDGE, SIDE - 2 * EDGE)
EARLY = (
    Part("leaving_first", LEAVE, 2, ((TOP, SIDE),), ((0, SIDE),), False, (MIDDLE,)),
    Part("leaving_second", LEAVE + 2 * ENTRY, 2, ((TOP, SIDE),), ((0, SIDE),), False, (MIDDLE,)),
)
LATE = Part(
    "leaving_edges",
    LEAVE,
    NT,
    ((LO, BAND), (HI - BAND, BAND)),
    ((0, BAND - 8), (SIDE - BAND + 8, BAND - 8)),
    True,
    ((0, EDGE), (SIDE - EDGE, EDGE)),
)
WHOLE = Part("staying", STAY, NT, ((LO, HI - LO),), ((0, SIDE),), True, ((0, SIDE),))


def row_bands(r, rows, above, middle, below):
    row = r + lax.broadcasted_iota(jnp.int32, (rows, 1), 0)
    return jnp.where(row < TOP, above, jnp.where(row < TOP + SIDE, middle, below))


def assemble(part, table, base, i, slot, fields, stacks, block, strip):
    halo_cols = stacks[0]
    lane = lane_index()
    at = GROUP * i

    def near(name):
        place = base + 5 + 3 * NEAR[name]
        return table[place], table[place + 1]

    def inside(lo, hi):
        return (lane >= at + lo) & (lane < at + hi)

    west, east = near("w"), near("e")
    for f in range(FIELDS):

        def ends(side, start, middle, left, right, out):
            rows = pl.ds(start, 8)
            mid, left_end, right_end = (
                stacks[1][place[0], side, place[1], rows, :] for place in (middle, left, right)
            )
            block[f][i, out : out + 8, :] = mid
            lower = jnp.where(lane < SIDE // 2, mid, left_end)
            upper = jnp.where(lane < SIDE // 2, right_end, mid)
            value = jnp.where(
                inside(0, 16),
                pltpu.roll(lower, (at + 8) % SIDE, 1),
                pltpu.roll(upper, (at + 24) % SIDE, 1),
            )
            if i:
                value = jnp.where(inside(0, GROUP), value, strip[f][out : out + 8, :])
            strip[f][out : out + 8, :] = value

        if part.halo_rows:
            start = SPARE + LAST_AT[f] + LAST_ROWS[f] - 8
            ends(0, start, near("n"), near("nw"), near("ne"), LO)
            ends(1, SPARE + FIRST_AT[f], near("s"), near("sw"), near("se"), TOP + SIDE)

        for start, count in part.own:
            own, out = pl.ds(start, count), pl.ds(TOP + start, count)

            def shifted(place, offset, goal):
                lanes_at = TILE_LANES * place[1] + (COL_AT[f] + offset)
                b, source = divide(lanes_at, SIDE), remainder(lanes_at, SIDE)
                beyond = jnp.minimum(b + 1, halo_cols.shape[1] - 1)
                value = jnp.where(
                    lane >= source, halo_cols[place[0], b, own, :], halo_cols[place[0], beyond, own, :]
                )
                return pltpu.roll(value, remainder(goal - source + SIDE, SIDE), 1)

            core = fields[f][slot, own, :]
            block[f][i, out, :] = core
            value = shifted(west, 0, at + 8 - LAST_COLS[f])
            if i:
                value = jnp.where(inside(0, 8), value, strip[f][out, :])
            value = jnp.where(inside(8, 16), pltpu.roll(core, (at + 8) % SIDE, 1), value)
            value = jnp.where(inside(16, 24), pltpu.roll(core, (at + 24) % SIDE, 1), value)
            value = jnp.where(inside(24, GROUP), shifted(east, LAST_COLS[f], at + 24), value)
            strip[f][out, :] = value


def prepare_strip(part, near_wet, strip, ground_x, ground_y):
    level, flow_x, flow_y, ground, friction = strip
    lane = lane_index()

    def lane_wet(center, left, right):
        value = jnp.zeros((1, SIDE), jnp.int32)
        for i in range(part.tiles):
            at = GROUP * i
            middle = near_wet(i, center) if center else 1
            sides = jnp.where(
                lane < at + 8,
                near_wet(i, left),
                jnp.where(lane < at + 24, middle, near_wet(i, right)),
            )
            value = jnp.where((lane >= at) & (lane < at + GROUP), sides, value)
        return value

    bands = (lane_wet("n", "nw", "ne"), lane_wet(None, "w", "e"), lane_wet("s", "sw", "se"))
    for r, rows in part.chunks():
        at, south = pl.ds(r, rows), pl.ds(r + 1, rows)
        z = ground[at, :]
        here, next_row = row_bands(r, rows, *bands), row_bands(r + 1, rows, *bands)
        open_x = (here == 1) & (pltpu.roll(here, SIDE - 1, 1) == 1)
        open_y = (here == 1) & (next_row == 1)
        z_east = pltpu.roll(z, SIDE - 1, 1)
        ground_x[at, :] = jnp.where(open_x, jnp.maximum(z, z_east), CLOSED)
        ground_y[at, :] = jnp.where(open_y, jnp.maximum(z, ground[south, :]), CLOSED)
        flow_x[at, :] = jnp.where(open_x, flow_x[at, :], 0.0)
        flow_y[at, :] = jnp.where(open_y, flow_y[at, :], 0.0)
        friction[at, :] = (GRAV * STEP_TIME) * friction[at, :] * friction[at, :]
        level[at, :] = level[at, :] + z


def prepare_tile(part, near_wet, i, block, ground_x, ground_y, strip_ground):
    level, flow_x, flow_y, ground, friction = block
    lane = lane_index()
    last = lane == SIDE - 1
    n, e, s = near_wet(i, "n"), near_wet(i, "e"), near_wet(i, "s")
    bands = (
        jnp.where(last, n * near_wet(i, "ne"), n),
        jnp.where(last, e, 1),
        jnp.where(last, s * near_wet(i, "se"), s),
    )
    for r, rows in part.chunks():
        at, south = pl.ds(r, rows), pl.ds(r + 1, rows)
        z = ground[i, at, :]
        z_east = jnp.where(
            last, pltpu.roll(strip_ground[at, :], to_east(i), 1), pltpu.roll(z, SIDE - 1, 1)
        )
        open_x = row_bands(r, rows, *bands) == 1
        open_y = (row_bands(r + 1, rows, n, 1, s) == 1) & (row_bands(r, rows, n, 1, s) == 1)
        ground_x[i, at, :] = jnp.where(open_x, jnp.maximum(z, z_east), CLOSED)
        ground_y[i, at, :] = jnp.where(open_y, jnp.maximum(z, ground[i, south, :]), CLOSED)
        flow_x[i, at, :] = jnp.where(open_x, flow_x[i, at, :], 0.0)
        flow_y[i, at, :] = jnp.where(open_y, flow_y[i, at, :], 0.0)
        friction[i, at, :] = (GRAV * STEP_TIME) * friction[i, at, :] * friction[i, at, :]
        level[i, at, :] = level[i, at, :] + z


def to_east(i):
    return (SIDE - 1 - GROUP * i - 24) % SIDE


def to_west(i):
    return (SIDE - GROUP * i - 7) % SIDE


def unpack_columns(part, packed, out):
    blocks, half = out.shape[0] - 1, SIDE // 2
    for start, count in part.own:
        rows = pl.ds(start, count)
        for b in range(blocks):
            out[b, rows, :] = packed[b * SIDE + start : b * SIDE + start + count, :]
        if start < half:
            n = min(count, half - start)
            out[blocks, start : start + n, :] = packed[
                blocks * SIDE + start : blocks * SIDE + start + n, :
            ]
        if start + count > half:
            low, high = max(start, half), start + count
            lower = packed[blocks * SIDE + low - half : blocks * SIDE + high - half, :]
            out[blocks, low:high, :] = pltpu.roll(lower, half, 1)


def advance_kernel(part, lanes, units, given, *refs):
    table = refs[0]
    fields = refs[1 : 1 + FIELDS]
    kinds = 2 if part.halo_rows else 1
    halos, refs = refs[1 + FIELDS : 1 + FIELDS + kinds * lanes], refs[1 + FIELDS + kinds * lanes :]
    received, refs = refs[:given], refs[given:]
    n_out = 3 if part is WHOLE else len(units)
    outs, stacks, refs = refs[:n_out], refs[n_out : n_out + kinds], refs[n_out + kinds :]
    (
        level, flow_x, flow_y, ground, friction, ground_x, ground_y,
        s_level, s_flow_x, s_flow_y, s_ground, s_friction, s_ground_x, s_ground_y,
        sem_out, sem_in,
    ) = refs
    if part is WHOLE:
        placing = arrivals(table, units, received, (MIDDLE,), outs, sem_in)
        placing(lambda copy: copy.start())
    block = (level, flow_x, flow_y, ground, friction)
    strip = (s_level, s_flow_x, s_flow_y, s_ground, s_friction)
    lane = lane_index()
    last, first = lane == SIDE - 1, lane == 0

    def entry(i):
        at = part.base + i * ENTRY
        return table[at + 1], table[at + 2], table[at + 3]

    def near_wet(i, name):
        return table[part.base + i * ENTRY + 4 + 3 * NEAR[name]]

    for k in range(lanes):
        for n in range(kinds):
            if n:
                for side in range(2):
                    for t in range(fields[0].shape[0]):
                        stacks[1][k, side, t, SPARE : SPARE + TILE_ROWS, :] = halos[kinds * k + 1][
                            side, TILE_ROWS * t : TILE_ROWS * (t + 1), :
                        ]
            else:
                unpack_columns(part, halos[kinds * k], stacks[0].at[k])
    for i in range(part.tiles):
        base = part.base + i * ENTRY
        assemble(part, table, base, i, entry(i)[1], fields, stacks, block, strip)
    prepare_strip(part, near_wet, strip, s_ground_x, s_ground_y)
    for i in range(part.tiles):
        prepare_tile(part, near_wet, i, block, ground_x, ground_y, s_ground)

    def step(_, carry):
        for r, rows in part.chunks():
            at, south = pl.ds(r, rows), pl.ds(r + 1, rows)
            e, c = s_level[at, :], s_friction[at, :]
            e_east = pltpu.roll(e, SIDE - 1, 1)
            s_flow_x[at, :] = face(s_flow_x[at, :], e, e_east, s_ground_x[at, :], c)
            s_flow_y[at, :] = face(s_flow_y[at, :], e, s_level[south, :], s_ground_y[at, :], c)
        for i in range(part.tiles):
            for r, rows in part.chunks():
                at, south = pl.ds(r, rows), pl.ds(r + 1, rows)
                e, c = level[i, at, :], friction[i, at, :]
                e_east = jnp.where(
                    last, pltpu.roll(s_level[at, :], to_east(i), 1), pltpu.roll(e, SIDE - 1, 1)
                )
                flow_x[i, at, :] = face(flow_x[i, at, :], e, e_east, ground_x[i, at, :], c)
                flow_y[i, at, :] = face(
                    flow_y[i, at, :], e, level[i, south, :], ground_y[i, at, :], c
                )
        for r, rows in part.chunks():
            at, north = pl.ds(r, rows), pl.ds(r - 1, rows)
            qx = s_flow_x[at, :]
            s_level[at, :] = s_level[at, :] + RATE * (
                (pltpu.roll(qx, 1, 1) - qx) + (s_flow_y[north, :] - s_flow_y[at, :])
            )
        for i in range(part.tiles):
            for r, rows in part.chunks():
                at, north = pl.ds(r, rows), pl.ds(r - 1, rows)
                qx = flow_x[i, at, :]
                qx_west = jnp.where(
                    first, pltpu.roll(s_flow_x[at, :], to_west(i), 1), pltpu.roll(qx, 1, 1)
                )
                level[i, at, :] = level[i, at, :] + RATE * (
                    (qx_west - qx) + (flow_y[i, north, :] - flow_y[i, at, :])
                )
        return carry

    lax.fori_loop(0, STEPS, step, 0)

    results = (level, flow_x, flow_y)
    for i in range(part.tiles):
        wet, slot, _ = entry(i)
        for start, count in part.sent:
            own, at = pl.ds(start, count), pl.ds(TOP + start, count)
            level[i, at, :] = level[i, at, :] - ground[i, at, :]
            for f in range(3):
                results[f][i, at, :] = jnp.where(
                    wet == 1, results[f][i, at, :], fields[f][slot, own, :]
                )

    if part is not WHOLE:
        for i in range(part.tiles):
            target = entry(i)[2]
            for out_ref, k in zip(outs, units):
                @pl.when(divide(target, 2) == k)
                def _():
                    out = 0
                    for start, count in part.sent:
                        for f in range(3):
                            value = results[f][i, pl.ds(TOP + start, count), :]
                            out_ref[remainder(target, 2), f, out : out + count, :] = value
                        out += count

    else:
        copies = [
            pltpu.make_async_copy(
                results[f].at[i, pl.ds(TOP, SIDE), :], outs[f].at[entry(i)[2]], sem_out.at[i, f]
            )
            for i in range(part.tiles)
            for f in range(3)
        ]
        for copy in copies:
            copy.start()
        placing(lambda copy: copy.wait())
        for copy in copies:
            copy.wait()


def advance(part, table, fields, halos, units, given=()):
    lanes = len(halos)
    sent = sum(count for _, count in part.sent)
    if part is WHOLE:
        outs = (jax.ShapeDtypeStruct(fields[0].shape, jnp.float32),) * 3
        out_specs = [pl.BlockSpec(memory_space=ANY)] * 3
    else:
        outs = (VMEM((2, 3, sent, SIDE), jnp.float32),) * len(units)
        out_specs = vmem_specs(len(units))
    if not part.halo_rows:
        halos = [group[:1] for group in halos]
    flat = [array for group in halos for array in group]
    tile_count = fields[0].shape[0]
    stacks = [VMEM((lanes, -(-tile_count * TILE_LANES // SIDE), SIDE, SIDE), jnp.float32)]
    if part.halo_rows:
        stacks.append(VMEM((lanes, 2, tile_count, SPARE + TILE_ROWS + 1, SIDE), jnp.float32))
    block = VMEM((part.tiles, ROWS, SIDE), jnp.float32)
    strip = VMEM((ROWS, SIDE), jnp.float32)
    cells = (part.tiles + 1) * sum(count for _, count in part.computed) * SIDE * STEPS
    return pl.pallas_call(
        functools.partial(advance_kernel, part, lanes, units, len(given)),
        name="advance_" + part.name,
        out_shape=outs,
        in_specs=[pl.BlockSpec(memory_space=SMEM)]
        + vmem_specs(FIELDS + len(flat) + len(given)),
        input_output_aliases={
            1 + FIELDS + len(flat) + n: n for n in range(0 if part is WHOLE else len(given))
        },
        out_specs=tuple(out_specs),
        scratch_shapes=stacks
        + [block] * 7
        + [strip] * 7
        + [
            pltpu.SemaphoreType.DMA((part.tiles, 3)),
            pltpu.SemaphoreType.DMA((max(len(given), 1), 2, 3, 1)),
        ],
        compiler_params=pltpu.CompilerParams(vmem_limit_bytes=12 * 1024 * 1024),
        cost_estimate=pl.CostEstimate(
            flops=60 * cells, bytes_accessed=8 * part.tiles * sent * SIDE * 4, transcendentals=6 * cells
        ),
    )(table, *fields, *flat, *given)


def shift_lanes(array, col_shift, sub_shift):
    cols, subs = lax.axis_size("col"), lax.axis_size("sub")
    pairs = [
        (c * subs + s, ((c + col_shift) % cols) * subs + (s + sub_shift) % subs)
        for c in range(cols)
        for s in range(subs)
    ]
    return lax.ppermute(array, ("col", "sub"), pairs)


def over_cols(array):
    return [array] + [shift_lanes(array, c, 0) for c in range(1, lax.axis_size("col"))]


def over_subs(parts):
    subs = lax.axis_size("sub")
    return [
        in_vmem(part if s == 0 else shift_lanes(part, 0, s)) for part in parts for s in range(subs)
    ]


def meet_rows(array, parity):
    rows, subs = lax.axis_size("row"), lax.axis_size("sub")
    pairs = []
    for r in range(rows):
        other = r + 1 if r % 2 == parity else r - 1
        for s in range(subs):
            if 0 <= other < rows:
                pairs.append((r * subs + s, other * subs + s))
            else:
                pairs.append((r * subs + s, r * subs + (s + 1) % subs))
    return lax.ppermute(array, ("row", "sub"), pairs)


def shards(
    water_depth, flow_east, flow_south, bed_level, manning_n, placed_before, placed_after, wet_tiles
):
    cols, subs = lax.axis_size("col"), lax.axis_size("sub")
    tile_count = water_depth.shape[0]
    *fields, columns, pair_even, pair_odd = load(
        (water_depth, flow_east, flow_south, bed_level, manning_n)
    )
    fields = [in_vmem(field) for field in fields]
    columns = over_cols(columns)
    met_even, met_odd = meet_rows(pair_even, 0), meet_rows(pair_odd, 1)
    table = make_table(
        (cols, subs, tile_count, placed_before.shape[0]), placed_before, placed_after, wet_tiles
    )
    joined = join(met_even, met_odd)
    near_rows = over_cols(joined)
    columns[1:], joined, table = lax.optimization_barrier((columns[1:], joined, table))
    near_rows[0] = joined
    table = pltpu.with_memory_space_constraint(table, SMEM)
    near_rows = over_subs(near_rows)
    columns = over_subs(columns)

    def send(part, k):
        return in_vmem(shift_lanes(part, k // subs, k % subs))

    units = tuple(range(1, cols * subs))
    ahead, others = subs, tuple(k for k in units if k != subs)
    alone = [(part,) for part in columns]
    first, *rest = advance(EARLY[0], table, fields, alone, (ahead,) + others)
    rest = advance(EARLY[1], table, fields, alone, others, [in_vmem(part) for part in rest])
    middle = {ahead: send(first, ahead)}
    middle.update((k, send(part, k)) for k, part in zip(others, rest))
    halos = list(zip(columns, near_rows))
    edges = list(advance(LATE, table, fields, halos, units))
    middle[ahead], edges[0] = lax.optimization_barrier((middle[ahead], edges[0]))
    middle[ahead] = in_vmem(middle[ahead])
    edges = [send(part, k) for k, part in zip(units, edges)]
    soon = tuple(range(1, subs)) + (ahead,)
    last = tuple(k for k in units if k not in soon)
    outs = advance(WHOLE, table, fields, halos, soon, [middle[k] for k in soon])
    groups = tuple((k, (MIDDLE,)) for k in last) + tuple((k, LATE.sent) for k in units)
    return place(groups, table, [middle[k] for k in last] + edges, outs)


def solution(mesh):
    tiles = P(("basin", "row", "col", "sub"), None, None)
    return jax.shard_map(
        shards,
        mesh=mesh,
        in_specs=(tiles,) * FIELDS + (P("basin"),) * 3,
        out_specs=(tiles,) * 3,
        check_vma=False,
    )
```

```python
import functools
import math

import jax
import jax.numpy as jnp
from jax import lax
from jax.experimental import pallas as pl
from jax.experimental.pallas import tpu as pltpu
from jax.sharding import PartitionSpec as P

STEPS = 6
GRAV = 9.81
STEP_TIME = 0.5
SPACING = 5.0
RATE = 0.1
DEPTH_FLOOR = 0.3

FIELDS = 5
HALO = STEPS
LAST_COLS = (HALO, HALO, HALO - 1, HALO, HALO)
FIRST_COLS = (HALO, HALO - 1, HALO - 1, HALO, HALO - 1)
LAST_ROWS = (HALO - 1, HALO - 1, HALO, HALO - 1, HALO - 1)
FIRST_ROWS = (HALO, HALO - 1, HALO - 1, HALO, HALO - 1)


def starts(counts):
    return [sum(counts[:f]) for f in range(len(counts))]


BOTH_COLS = tuple(a + b for a, b in zip(LAST_COLS, FIRST_COLS))
TILE_LANES = sum(BOTH_COLS)
TILE_ROWS = max(sum(LAST_ROWS), sum(FIRST_ROWS))
COL_AT, LAST_AT, FIRST_AT = starts(BOTH_COLS), starts(LAST_ROWS), starts(FIRST_ROWS)
SIDE = 128
TOP = 16
ROWS = SIDE + 32
LO = 8
HI = SIDE + 24
CHUNK = 24
SPARE = 3
FIXED = TOP - HALO
NT = 4
GROUP = SIDE // NT
CLOSED = 1e30
POWER = -(7.0 / 3.0) / math.log(2.0)

ENTRY = 32
NEAR = {"w": 0, "e": 1, "n": 2, "s": 3, "nw": 4, "ne": 5, "sw": 6, "se": 7}
STEP_TO = ((0, -1), (0, 1), (-1, 0), (1, 0), (-1, -1), (-1, 1), (1, -1), (1, 1))
LEAVE, STAY, RECEIVE = 0, NT * ENTRY, 2 * NT * ENTRY

SMEM = pltpu.SMEM
VMEM = pltpu.VMEM
ANY = pl.ANY
SMALL = pltpu.CompilerParams(vmem_limit_bytes=2 * 1024 * 1024)


def lane_index():
    return lax.broadcasted_iota(jnp.int32, (1, SIDE), 1)


def divide(value, size):
    if size & (size - 1):
        return lax.div(value, size)
    return lax.shift_right_logical(value, size.bit_length() - 1)


def remainder(value, size):
    if size & (size - 1):
        return lax.rem(value, size)
    return value & (size - 1)


def index_kernel(shape, before_ref, after_ref, wet_ref, table, inv_before, inv_after, count):
    cols, subs, tile_count, total = shape
    lanes = cols * subs
    row_tiles = lanes * tile_count
    tile_rows = total // row_tiles
    my_row, my_col, my_sub = (lax.axis_index(name) for name in ("row", "col", "sub"))
    me = my_row * lanes + my_col * subs + my_sub
    spare = RECEIVE + 2 * lanes

    def invert(s, carry):
        for u in range(16):
            inv_before[before_ref[s * 16 + u]] = s * 16 + u
            inv_after[after_ref[s * 16 + u]] = s * 16 + u
        return carry

    lax.fori_loop(0, total // 16, invert, 0)
    for i in range(lanes * 2):
        table[RECEIVE + i] = -1
    for i in range(lanes + 1):
        count[i] = 0

    def relative(lane, sign):
        col = remainder(sign * (divide(lane, subs) - my_col) + cols, cols)
        sub = remainder(sign * (remainder(lane, subs) - my_sub) + subs, subs)
        return col * subs + sub

    def own(s, carry):
        tile = before_ref[me * tile_count + s]
        device = divide(inv_after[tile], tile_count)
        stays = device == me
        to = relative(remainder(device, lanes), 1)
        nth = count[to]
        count[to] = nth + 1
        other = jnp.where(stays | (to == subs), 0, 1)
        left = count[lanes]
        count[lanes] = left + other
        place = jnp.minimum(jnp.where(other == 1, NT - 1 - left, nth), NT - 1)
        base = jnp.where(stays, STAY, LEAVE) + jnp.maximum(place, 0) * ENTRY
        table[base + 1] = wet_ref[tile]
        table[base + 2] = s
        table[base + 3] = jnp.where(stays, s, to * 2 + jnp.minimum(nth, 1))
        row, col = divide(tile, row_tiles), remainder(tile, row_tiles)
        for n, (dr, dc) in enumerate(STEP_TO):
            r, c = row + dr, col + dc
            there = (r >= 0) & (r < tile_rows) & (c >= 0) & (c < row_tiles)
            near = jnp.where(there, tile + (dr * row_tiles + dc), tile)
            at = inv_before[near]
            table[base + 4 + 3 * n] = jnp.where(there, wet_ref[near], 0)
            table[base + 5 + 3 * n] = relative(remainder(divide(at, tile_count), lanes), -1)
            table[base + 6 + 3 * n] = remainder(at, tile_count)
        return carry

    lax.fori_loop(0, tile_count, own, 0)

    for rel in range(1, lanes):
        col = remainder(my_col + (cols - rel // subs), cols)
        sub = remainder(my_sub + (subs - rel % subs), subs)
        device = my_row * lanes + col * subs + sub
        found = jnp.int32(0)
        for s in range(tile_count):
            at = inv_after[before_ref[device * tile_count + s]]
            mine = divide(at, tile_count) == me
            place = RECEIVE + rel * 2 + jnp.minimum(found, 1)
            table[jnp.where(mine, place, spare)] = remainder(at, tile_count)
            found = found + jnp.where(mine, 1, 0)


def make_table(shape, before, after, wet):
    cols, subs, _, total = shape
    return pl.pallas_call(
        functools.partial(index_kernel, shape),
        name="index_table",
        out_shape=SMEM((RECEIVE + 2 * cols * subs + 1,), jnp.int32),
        in_specs=[pl.BlockSpec(memory_space=SMEM)] * 3,
        out_specs=pl.BlockSpec(memory_space=SMEM),
        scratch_shapes=[
            SMEM((total,), jnp.int32),
            SMEM((total,), jnp.int32),
            SMEM((cols * subs + 1,), jnp.int32),
        ],
        compiler_params=SMALL,
    )(before, after, wet)


def in_vmem(array):
    return pltpu.with_memory_space_constraint(array, VMEM)


def vmem_specs(count):
    return [pl.BlockSpec(memory_space=VMEM)] * count


def load_kernel(*refs):
    sources, refs = refs[:FIELDS], refs[FIELDS:]
    fields, (columns, pair_even, pair_odd, first, last, sem, _) = refs[:FIELDS], refs[FIELDS:]
    spill = refs[-1]
    lane = lane_index()
    odd = remainder(lax.axis_index("row"), 2) == 1
    copies = [
        pltpu.make_async_copy(sources[f], fields[f], sem.at[f]) for f in range(FIELDS)
    ]
    for copy in copies:
        copy.start()
    tile_count = fields[0].shape[0]
    blocks = tile_count * TILE_LANES // SIDE
    for f in range(FIELDS):
        copies[f].wait()
        for b in range(blocks + 1):
            target, place = (columns, pl.ds(b * SIDE, SIDE)) if b < blocks else (spill, slice(None))
            packed = target[place, :]
            for t in range(tile_count):
                at = TILE_LANES * t + COL_AT[f] - b * SIDE
                if at < SIDE and at + BOTH_COLS[f] > 0:
                    moved = pltpu.roll(fields[f][t], (at + LAST_COLS[f]) % SIDE, 1)
                    packed = jnp.where((lane >= at) & (lane < at + BOTH_COLS[f]), moved, packed)
            target[place, :] = packed
        for t in range(tile_count):
            at, count = TILE_ROWS * t + FIRST_AT[f], FIRST_ROWS[f]
            first[at : at + count, :] = fields[f][t, :count, :]
            at, count = TILE_ROWS * t + LAST_AT[f], LAST_ROWS[f]
            last[at : at + count, :] = fields[f][t, SIDE - count :, :]
    row = SIDE - HALO
    level = [fields[0][:, r, :] + fields[3][:, r, :] for r in (row, row + 1)]
    ground = jnp.maximum(fields[3][:, row, :], fields[3][:, row + 1, :])
    drag = (GRAV * STEP_TIME) * fields[4][:, row, :] * fields[4][:, row, :]
    flow = face(fields[2][:, row, :], level[0], level[1], ground, drag)
    for t in range(tile_count):
        at = TILE_ROWS * t + LAST_AT[2]
        last[at : at + 1, :] = flow[t : t + 1, :]
    half = SIDE // 2
    columns[blocks * SIDE :, :] = jnp.where(
        lane < half, spill[:half, :], pltpu.roll(spill[half:, :], half, 1)
    )
    pair_even[...] = jnp.where(odd, first[...], last[...])
    pair_odd[...] = jnp.where(odd, last[...], first[...])


def load(arrays):
    tile_count = arrays[0].shape[0]
    rows = VMEM((tile_count * TILE_ROWS, SIDE), jnp.float32)
    outs = [VMEM(array.shape, array.dtype) for array in arrays]
    outs += [VMEM((tile_count * TILE_LANES, SIDE), jnp.float32), rows, rows]
    return pl.pallas_call(
        load_kernel,
        name="load_and_pack",
        out_shape=tuple(outs),
        in_specs=[pl.BlockSpec(memory_space=pltpu.HBM)] * FIELDS,
        out_specs=tuple(vmem_specs(len(outs))),
        scratch_shapes=[
            rows,
            rows,
            pltpu.SemaphoreType.DMA((FIELDS,)),
            VMEM((SIDE, SIDE), jnp.float32),
        ],
        compiler_params=SMALL,
    )(*[pltpu.with_memory_space_constraint(array, pltpu.HBM) for array in arrays])


def join_kernel(met_even, met_odd, joined):
    odd = remainder(lax.axis_index("row"), 2) == 1
    joined[0] = jnp.where(odd, met_even[...], met_odd[...])
    joined[1] = jnp.where(odd, met_odd[...], met_even[...])


def join(met_even, met_odd):
    return pl.pallas_call(
        join_kernel,
        name="join_row_halos",
        out_shape=VMEM((2,) + met_even.shape, met_even.dtype),
        in_specs=vmem_specs(2),
        out_specs=pl.BlockSpec(memory_space=VMEM),
        compiler_params=SMALL,
    )(in_vmem(met_even), in_vmem(met_odd))


def arrivals(table, units, received, spans, outs, sem):
    def each(act):
        for n, k in enumerate(units):
            for j in range(2):
                slot = table[RECEIVE + 2 * k + j]

                @pl.when(slot >= 0)
                def _():
                    at = 0
                    for m, (start, count) in enumerate(spans):
                        for f in range(3):
                            act(
                                pltpu.make_async_copy(
                                    received[n].at[j, f, pl.ds(at, count), :],
                                    outs[f].at[slot, pl.ds(start, count), :],
                                    sem.at[n, j, f, m],
                                )
                            )
                        at += count

    return each


def place_kernel(groups, *refs):
    table, received, refs = refs[0], refs[1 : 1 + len(groups)], refs[1 + len(groups) :]
    outs, sem = refs[3:6], refs[6]
    copies = [
        arrivals(table, (k,), (array,), spans, outs, sem.at[pl.ds(n, 1)])
        for n, ((k, spans), array) in enumerate(zip(groups, received))
    ]
    for each in copies:
        each(lambda copy: copy.start())
    for each in copies:
        each(lambda copy: copy.wait())


def place(groups, table, received, partial_outs):
    count = len(received)
    return pl.pallas_call(
        functools.partial(place_kernel, groups),
        name="place_arrivals",
        out_shape=tuple(jax.ShapeDtypeStruct(o.shape, o.dtype) for o in partial_outs),
        in_specs=[pl.BlockSpec(memory_space=SMEM)]
        + vmem_specs(count)
        + [pl.BlockSpec(memory_space=ANY)] * 3,
        out_specs=tuple(pl.BlockSpec(memory_space=ANY) for _ in partial_outs),
        scratch_shapes=[pltpu.SemaphoreType.DMA((count, 2, 3, 2))],
        input_output_aliases={1 + count + f: f for f in range(3)},
        compiler_params=SMALL,
    )(table, *received, *partial_outs)


def face(flow, level, level_next, ground, friction):
    wetted = jnp.maximum(level, level_next) - ground
    drive = (GRAV * STEP_TIME / SPACING) * jnp.maximum(wetted, 0.0) * (level_next - level)
    power = jnp.exp2(POWER * jnp.log(jnp.maximum(wetted, DEPTH_FLOOR)))
    return (flow - drive) / (1.0 + friction * jnp.abs(flow) * power)


class Part:
    def __init__(self, name, base, tiles, computed, own, halo_rows, sent):
        self.name = name
        self.base = base
        self.tiles = tiles
        self.computed = computed
        self.own = own
        self.halo_rows = halo_rows
        self.sent = sent

    def chunks(self):
        for start, count in self.computed:
            for r in range(start, start + count, CHUNK):
                yield r, min(CHUNK, start + count - r)


def row_span(span):
    return pl.ds(span[0], span[1])


EDGE = 8
BAND = 24
MIDDLE = (EDGE, SIDE - 2 * EDGE)
EARLY = (
    Part("leaving_first", LEAVE, 2, ((TOP, SIDE),), ((0, SIDE),), False, (MIDDLE,)),
    Part("leaving_second", LEAVE + 2 * ENTRY, 2, ((TOP, SIDE),), ((0, SIDE),), False, (MIDDLE,)),
)
LATE = Part(
    "leaving_edges",
    LEAVE,
    NT,
    ((LO, BAND), (HI - BAND, BAND)),
    ((0, BAND - 8), (SIDE - BAND + 8, BAND - 8)),
    True,
    ((0, EDGE), (SIDE - EDGE, EDGE)),
)
WHOLE = Part("staying", STAY, NT, ((LO, HI - LO),), ((0, SIDE),), True, ((0, SIDE),))


def row_bands(r, rows, above, middle, below):
    row = r + lax.broadcasted_iota(jnp.int32, (rows, 1), 0)
    return jnp.where(row < TOP, above, jnp.where(row < TOP + SIDE, middle, below))


def fixed_row(r, rows):
    if not r <= FIXED < r + rows:
        return None
    return r + lax.broadcasted_iota(jnp.int32, (rows, 1), 0) == FIXED


def unless(where, value, other):
    return value if where is None else jnp.where(where, other, value)


def assemble(part, table, base, i, slot, fields, stacks, block, strip):
    halo_cols = stacks[0]
    lane = lane_index()
    at = GROUP * i

    def near(name):
        place = base + 5 + 3 * NEAR[name]
        return table[place], table[place + 1]

    def inside(lo, hi):
        return (lane >= at + lo) & (lane < at + hi)

    west, east = near("w"), near("e")
    for f in range(FIELDS):

        def ends(side, start, middle, left, right, out):
            rows = pl.ds(start, 8)
            mid, left_end, right_end = (
                stacks[1][place[0], side, place[1], rows, :] for place in (middle, left, right)
            )
            block[f][i, out : out + 8, :] = mid
            lower = jnp.where(lane < SIDE // 2, mid, left_end)
            upper = jnp.where(lane < SIDE // 2, right_end, mid)
            value = jnp.where(
                inside(0, 16),
                pltpu.roll(lower, (at + 8) % SIDE, 1),
                pltpu.roll(upper, (at + 24) % SIDE, 1),
            )
            if i:
                value = jnp.where(inside(0, GROUP), value, strip[f][out : out + 8, :])
            strip[f][out : out + 8, :] = value

        if part.halo_rows:
            start = SPARE + LAST_AT[f] + LAST_ROWS[f] - 8
            ends(0, start, near("n"), near("nw"), near("ne"), LO)
            ends(1, SPARE + FIRST_AT[f], near("s"), near("sw"), near("se"), TOP + SIDE)

        for start, count in part.own:
            own, out = pl.ds(start, count), pl.ds(TOP + start, count)

            def shifted(place, offset, goal):
                lanes_at = TILE_LANES * place[1] + (COL_AT[f] + offset)
                b, source = divide(lanes_at, SIDE), remainder(lanes_at, SIDE)
                beyond = jnp.minimum(b + 1, halo_cols.shape[1] - 1)
                value = jnp.where(
                    lane >= source, halo_cols[place[0], b, own, :], halo_cols[place[0], beyond, own, :]
                )
                return pltpu.roll(value, remainder(goal - source + SIDE, SIDE), 1)

            core = fields[f][slot, own, :]
            block[f][i, out, :] = core
            value = shifted(west, 0, at + 8 - LAST_COLS[f])
            if i:
                value = jnp.where(inside(0, 8), value, strip[f][out, :])
            value = jnp.where(inside(8, 16), pltpu.roll(core, (at + 8) % SIDE, 1), value)
            value = jnp.where(inside(16, 24), pltpu.roll(core, (at + 24) % SIDE, 1), value)
            value = jnp.where(inside(24, GROUP), shifted(east, LAST_COLS[f], at + 24), value)
            strip[f][out, :] = value


def prepare_strip(part, near_wet, strip, ground_x, ground_y):
    level, flow_x, flow_y, ground, friction = strip
    lane = lane_index()

    def lane_wet(center, left, right):
        value = jnp.zeros((1, SIDE), jnp.int32)
        for i in range(part.tiles):
            at = GROUP * i
            middle = near_wet(i, center) if center else 1
            sides = jnp.where(
                lane < at + 8,
                near_wet(i, left),
                jnp.where(lane < at + 24, middle, near_wet(i, right)),
            )
            value = jnp.where((lane >= at) & (lane < at + GROUP), sides, value)
        return value

    bands = (lane_wet("n", "nw", "ne"), lane_wet(None, "w", "e"), lane_wet("s", "sw", "se"))
    for r, rows in part.chunks():
        at, south = pl.ds(r, rows), pl.ds(r + 1, rows)
        z = ground[at, :]
        here, next_row = row_bands(r, rows, *bands), row_bands(r + 1, rows, *bands)
        open_x = (here == 1) & (pltpu.roll(here, SIDE - 1, 1) == 1)
        open_y = (here == 1) & (next_row == 1)
        z_east = pltpu.roll(z, SIDE - 1, 1)
        fixed = fixed_row(r, rows)
        ground_x[at, :] = jnp.where(open_x, jnp.maximum(z, z_east), CLOSED)
        ground_y[at, :] = unless(
            fixed, jnp.where(open_y, jnp.maximum(z, ground[south, :]), CLOSED), CLOSED
        )
        flow_x[at, :] = jnp.where(open_x, flow_x[at, :], 0.0)
        flow_y[at, :] = jnp.where(open_y, flow_y[at, :], 0.0)
        friction[at, :] = unless(
            fixed, (GRAV * STEP_TIME) * friction[at, :] * friction[at, :], 0.0
        )
        level[at, :] = level[at, :] + z


def prepare_tile(part, near_wet, i, block, ground_x, ground_y, strip_ground):
    level, flow_x, flow_y, ground, friction = block
    lane = lane_index()
    last = lane == SIDE - 1
    n, e, s = near_wet(i, "n"), near_wet(i, "e"), near_wet(i, "s")
    bands = (
        jnp.where(last, n * near_wet(i, "ne"), n),
        jnp.where(last, e, 1),
        jnp.where(last, s * near_wet(i, "se"), s),
    )
    for r, rows in part.chunks():
        at, south = pl.ds(r, rows), pl.ds(r + 1, rows)
        z = ground[i, at, :]
        z_east = jnp.where(
            last, pltpu.roll(strip_ground[at, :], to_east(i), 1), pltpu.roll(z, SIDE - 1, 1)
        )
        open_x = row_bands(r, rows, *bands) == 1
        open_y = (row_bands(r + 1, rows, n, 1, s) == 1) & (row_bands(r, rows, n, 1, s) == 1)
        fixed = fixed_row(r, rows)
        ground_x[i, at, :] = jnp.where(open_x, jnp.maximum(z, z_east), CLOSED)
        ground_y[i, at, :] = unless(
            fixed, jnp.where(open_y, jnp.maximum(z, ground[i, south, :]), CLOSED), CLOSED
        )
        flow_x[i, at, :] = jnp.where(open_x, flow_x[i, at, :], 0.0)
        flow_y[i, at, :] = jnp.where(open_y, flow_y[i, at, :], 0.0)
        friction[i, at, :] = unless(
            fixed, (GRAV * STEP_TIME) * friction[i, at, :] * friction[i, at, :], 0.0
        )
        level[i, at, :] = level[i, at, :] + z


def to_east(i):
    return (SIDE - 1 - GROUP * i - 24) % SIDE


def to_west(i):
    return (SIDE - GROUP * i - 7) % SIDE


def unpack_columns(part, packed, out):
    blocks, half = out.shape[0] - 1, SIDE // 2
    for start, count in part.own:
        rows = pl.ds(start, count)
        for b in range(blocks):
            out[b, rows, :] = packed[b * SIDE + start : b * SIDE + start + count, :]
        if start < half:
            n = min(count, half - start)
            out[blocks, start : start + n, :] = packed[
                blocks * SIDE + start : blocks * SIDE + start + n, :
            ]
        if start + count > half:
            low, high = max(start, half), start + count
            lower = packed[blocks * SIDE + low - half : blocks * SIDE + high - half, :]
            out[blocks, low:high, :] = pltpu.roll(lower, half, 1)


def advance_kernel(part, lanes, units, given, *refs):
    table = refs[0]
    fields = refs[1 : 1 + FIELDS]
    kinds = 2 if part.halo_rows else 1
    halos, refs = refs[1 + FIELDS : 1 + FIELDS + kinds * lanes], refs[1 + FIELDS + kinds * lanes :]
    received, refs = refs[:given], refs[given:]
    n_out = 3 if part is WHOLE else len(units)
    outs, stacks, refs = refs[:n_out], refs[n_out : n_out + kinds], refs[n_out + kinds :]
    (
        level, flow_x, flow_y, ground, friction, ground_x, ground_y,
        s_level, s_flow_x, s_flow_y, s_ground, s_friction, s_ground_x, s_ground_y,
        sem_out, sem_in,
    ) = refs
    if part is WHOLE:
        placing = arrivals(table, units, received, (MIDDLE,), outs, sem_in)
        placing(lambda copy: copy.start())
    block = (level, flow_x, flow_y, ground, friction)
    strip = (s_level, s_flow_x, s_flow_y, s_ground, s_friction)
    lane = lane_index()
    last, first = lane == SIDE - 1, lane == 0

    def entry(i):
        at = part.base + i * ENTRY
        return table[at + 1], table[at + 2], table[at + 3]

    def near_wet(i, name):
        return table[part.base + i * ENTRY + 4 + 3 * NEAR[name]]

    for k in range(lanes):
        for n in range(kinds):
            if n:
                for side in range(2):
                    for t in range(fields[0].shape[0]):
                        stacks[1][k, side, t, :SPARE, :] = jnp.zeros((SPARE, SIDE), jnp.float32)
                        stacks[1][k, side, t, SPARE : SPARE + TILE_ROWS, :] = halos[kinds * k + 1][
                            side, TILE_ROWS * t : TILE_ROWS * (t + 1), :
                        ]
            else:
                unpack_columns(part, halos[kinds * k], stacks[0].at[k])
    for i in range(part.tiles):
        base = part.base + i * ENTRY
        assemble(part, table, base, i, entry(i)[1], fields, stacks, block, strip)
    prepare_strip(part, near_wet, strip, s_ground_x, s_ground_y)
    for i in range(part.tiles):
        prepare_tile(part, near_wet, i, block, ground_x, ground_y, s_ground)

    def step(_, carry):
        for r, rows in part.chunks():
            at, south = pl.ds(r, rows), pl.ds(r + 1, rows)
            e, c = s_level[at, :], s_friction[at, :]
            e_east = pltpu.roll(e, SIDE - 1, 1)
            s_flow_x[at, :] = face(s_flow_x[at, :], e, e_east, s_ground_x[at, :], c)
            s_flow_y[at, :] = face(s_flow_y[at, :], e, s_level[south, :], s_ground_y[at, :], c)
        for i in range(part.tiles):
            for r, rows in part.chunks():
                at, south = pl.ds(r, rows), pl.ds(r + 1, rows)
                e, c = level[i, at, :], friction[i, at, :]
                e_east = jnp.where(
                    last, pltpu.roll(s_level[at, :], to_east(i), 1), pltpu.roll(e, SIDE - 1, 1)
                )
                flow_x[i, at, :] = face(flow_x[i, at, :], e, e_east, ground_x[i, at, :], c)
                flow_y[i, at, :] = face(
                    flow_y[i, at, :], e, level[i, south, :], ground_y[i, at, :], c
                )
        for r, rows in part.chunks():
            at, north = pl.ds(r, rows), pl.ds(r - 1, rows)
            qx = s_flow_x[at, :]
            s_level[at, :] = s_level[at, :] + RATE * (
                (pltpu.roll(qx, 1, 1) - qx) + (s_flow_y[north, :] - s_flow_y[at, :])
            )
        for i in range(part.tiles):
            for r, rows in part.chunks():
                at, north = pl.ds(r, rows), pl.ds(r - 1, rows)
                qx = flow_x[i, at, :]
                qx_west = jnp.where(
                    first, pltpu.roll(s_flow_x[at, :], to_west(i), 1), pltpu.roll(qx, 1, 1)
                )
                level[i, at, :] = level[i, at, :] + RATE * (
                    (qx_west - qx) + (flow_y[i, north, :] - flow_y[i, at, :])
                )
        return carry

    lax.fori_loop(0, STEPS, step, 0, unroll=True)

    results = (level, flow_x, flow_y)
    for i in range(part.tiles):
        wet, slot, _ = entry(i)
        for start, count in part.sent:
            own, at = pl.ds(start, count), pl.ds(TOP + start, count)
            level[i, at, :] = level[i, at, :] - ground[i, at, :]
            for f in range(3):
                results[f][i, at, :] = jnp.where(
                    wet == 1, results[f][i, at, :], fields[f][slot, own, :]
                )

    if part is not WHOLE:
        for i in range(part.tiles):
            target = entry(i)[2]
            for out_ref, k in zip(outs, units):
                @pl.when(divide(target, 2) == k)
                def _():
                    out = 0
                    for start, count in part.sent:
                        for f in range(3):
                            value = results[f][i, pl.ds(TOP + start, count), :]
                            out_ref[remainder(target, 2), f, out : out + count, :] = value
                        out += count

    else:
        copies = [
            pltpu.make_async_copy(
                results[f].at[i, pl.ds(TOP, SIDE), :], outs[f].at[entry(i)[2]], sem_out.at[i, f]
            )
            for i in range(part.tiles)
            for f in range(3)
        ]
        for copy in copies:
            copy.start()
        placing(lambda copy: copy.wait())
        for copy in copies:
            copy.wait()


def advance(part, table, fields, halos, units, given=()):
    lanes = len(halos)
    sent = sum(count for _, count in part.sent)
    if part is WHOLE:
        outs = (jax.ShapeDtypeStruct(fields[0].shape, jnp.float32),) * 3
        out_specs = [pl.BlockSpec(memory_space=ANY)] * 3
    else:
        outs = (VMEM((2, 3, sent, SIDE), jnp.float32),) * len(units)
        out_specs = vmem_specs(len(units))
    if not part.halo_rows:
        halos = [group[:1] for group in halos]
    flat = [array for group in halos for array in group]
    tile_count = fields[0].shape[0]
    stacks = [VMEM((lanes, -(-tile_count * TILE_LANES // SIDE), SIDE, SIDE), jnp.float32)]
    if part.halo_rows:
        stacks.append(VMEM((lanes, 2, tile_count, SPARE + TILE_ROWS + 10, SIDE), jnp.float32))
    block = VMEM((part.tiles, ROWS, SIDE), jnp.float32)
    strip = VMEM((ROWS, SIDE), jnp.float32)
    cells = (part.tiles + 1) * sum(count for _, count in part.computed) * SIDE * STEPS
    return pl.pallas_call(
        functools.partial(advance_kernel, part, lanes, units, len(given)),
        name="advance_" + part.name,
        out_shape=outs,
        in_specs=[pl.BlockSpec(memory_space=SMEM)]
        + vmem_specs(FIELDS + len(flat) + len(given)),
        input_output_aliases={
            1 + FIELDS + len(flat) + n: n for n in range(0 if part is WHOLE else len(given))
        },
        out_specs=tuple(out_specs),
        scratch_shapes=stacks
        + [block] * 7
        + [strip] * 7
        + [
            pltpu.SemaphoreType.DMA((part.tiles, 3)),
            pltpu.SemaphoreType.DMA((max(len(given), 1), 2, 3, 1)),
        ],
        compiler_params=pltpu.CompilerParams(vmem_limit_bytes=12 * 1024 * 1024),
        cost_estimate=pl.CostEstimate(
            flops=60 * cells, bytes_accessed=8 * part.tiles * sent * SIDE * 4, transcendentals=6 * cells
        ),
    )(table, *fields, *flat, *given)


def shift_lanes(array, col_shift, sub_shift):
    cols, subs = lax.axis_size("col"), lax.axis_size("sub")
    pairs = [
        (c * subs + s, ((c + col_shift) % cols) * subs + (s + sub_shift) % subs)
        for c in range(cols)
        for s in range(subs)
    ]
    return lax.ppermute(array, ("col", "sub"), pairs)


def over_cols(array):
    return [array] + [shift_lanes(array, c, 0) for c in range(1, lax.axis_size("col"))]


def over_subs(parts):
    subs = lax.axis_size("sub")
    return [
        in_vmem(part if s == 0 else shift_lanes(part, 0, s)) for part in parts for s in range(subs)
    ]


def meet_rows(array, parity):
    rows, subs = lax.axis_size("row"), lax.axis_size("sub")
    pairs = []
    for r in range(rows):
        other = r + 1 if r % 2 == parity else r - 1
        for s in range(subs):
            if 0 <= other < rows:
                pairs.append((r * subs + s, other * subs + s))
            else:
                pairs.append((r * subs + s, r * subs + (s + 1) % subs))
    return lax.ppermute(array, ("row", "sub"), pairs)


def shards(
    water_depth, flow_east, flow_south, bed_level, manning_n, placed_before, placed_after, wet_tiles
):
    cols, subs = lax.axis_size("col"), lax.axis_size("sub")
    tile_count = water_depth.shape[0]
    *fields, columns, pair_even, pair_odd = load(
        (water_depth, flow_east, flow_south, bed_level, manning_n)
    )
    fields = [in_vmem(field) for field in fields]
    columns = over_cols(columns)
    met_even, met_odd = meet_rows(pair_even, 0), meet_rows(pair_odd, 1)
    table = make_table(
        (cols, subs, tile_count, placed_before.shape[0]), placed_before, placed_after, wet_tiles
    )
    joined = join(met_even, met_odd)
    near_rows = over_cols(joined)
    columns[1:], joined, table = lax.optimization_barrier((columns[1:], joined, table))
    near_rows[0] = joined
    table = pltpu.with_memory_space_constraint(table, SMEM)
    near_rows = over_subs(near_rows)
    columns = over_subs(columns)

    def send(part, k):
        return in_vmem(shift_lanes(part, k // subs, k % subs))

    units = tuple(range(1, cols * subs))
    ahead, others = subs, tuple(k for k in units if k != subs)
    alone = [(part,) for part in columns]
    first, *rest = advance(EARLY[0], table, fields, alone, (ahead,) + others)
    rest = advance(EARLY[1], table, fields, alone, others, [in_vmem(part) for part in rest])
    middle = {ahead: send(first, ahead)}
    middle.update((k, send(part, k)) for k, part in zip(others, rest))
    halos = list(zip(columns, near_rows))
    edges = list(advance(LATE, table, fields, halos, units))
    middle[ahead], edges[0] = lax.optimization_barrier((middle[ahead], edges[0]))
    middle[ahead] = in_vmem(middle[ahead])
    edges = [send(part, k) for k, part in zip(units, edges)]
    soon = tuple(range(1, subs)) + (ahead,)
    last = tuple(k for k in units if k not in soon)
    outs = advance(WHOLE, table, fields, halos, soon, [middle[k] for k in soon])
    groups = tuple((k, (MIDDLE,)) for k in last) + tuple((k, LATE.sent) for k in units)
    return place(groups, table, [middle[k] for k in last] + edges, outs)


def solution(mesh):
    tiles = P(("basin", "row", "col", "sub"), None, None)
    return jax.shard_map(
        shards,
        mesh=mesh,
        in_specs=(tiles,) * FIELDS + (P("basin"),) * 3,
        out_specs=(tiles,) * 3,
        check_vma=False,
    )
```

```python
import functools
import math

import jax
import jax.numpy as jnp
from jax import lax
from jax.experimental import pallas as pl
from jax.experimental.pallas import tpu as pltpu
from jax.sharding import PartitionSpec as P

STEPS = 6
GRAV = 9.81
STEP_TIME = 0.5
SPACING = 5.0
RATE = 0.1
DEPTH_FLOOR = 0.3

FIELDS = 5
HALO = STEPS
LAST_COLS = (HALO, HALO, HALO - 1, HALO, HALO)
FIRST_COLS = (HALO, HALO - 1, HALO - 1, HALO, HALO - 1)
LAST_ROWS = (HALO - 1, HALO - 1, HALO, HALO - 1, HALO - 1)
FIRST_ROWS = (HALO, HALO - 1, HALO - 1, HALO, HALO - 1)


def starts(counts):
    return [sum(counts[:f]) for f in range(len(counts))]


BOTH_COLS = tuple(a + b for a, b in zip(LAST_COLS, FIRST_COLS))
TILE_LANES = sum(BOTH_COLS)
TILE_ROWS = max(sum(LAST_ROWS), sum(FIRST_ROWS))
COL_AT, LAST_AT, FIRST_AT = starts(BOTH_COLS), starts(LAST_ROWS), starts(FIRST_ROWS)
SIDE = 128
TOP = 16
ROWS = SIDE + 32
LO = 8
HI = SIDE + 24
CHUNK = 24
SPARE = 3
FIXED = TOP - HALO
NT = 4
GROUP = SIDE // NT
CLOSED = 1e30
POWER = -(7.0 / 3.0) / math.log(2.0)

ENTRY = 32
NEAR = {"w": 0, "e": 1, "n": 2, "s": 3, "nw": 4, "ne": 5, "sw": 6, "se": 7}
STEP_TO = ((0, -1), (0, 1), (-1, 0), (1, 0), (-1, -1), (-1, 1), (1, -1), (1, 1))
LEAVE, STAY, RECEIVE = 0, NT * ENTRY, 2 * NT * ENTRY

SMEM = pltpu.SMEM
VMEM = pltpu.VMEM
ANY = pl.ANY
SMALL = pltpu.CompilerParams(vmem_limit_bytes=2 * 1024 * 1024)


def lane_index():
    return lax.broadcasted_iota(jnp.int32, (1, SIDE), 1)


def divide(value, size):
    if size & (size - 1):
        return lax.div(value, size)
    return lax.shift_right_logical(value, size.bit_length() - 1)


def remainder(value, size):
    if size & (size - 1):
        return lax.rem(value, size)
    return value & (size - 1)


def index_kernel(shape, before_ref, after_ref, wet_ref, table, inv_before, inv_after, count):
    cols, subs, tile_count, total = shape
    lanes = cols * subs
    row_tiles = lanes * tile_count
    tile_rows = total // row_tiles
    my_row, my_col, my_sub = (lax.axis_index(name) for name in ("row", "col", "sub"))
    me = my_row * lanes + my_col * subs + my_sub
    spare = RECEIVE + 2 * lanes

    def invert(s, carry):
        for u in range(16):
            inv_before[before_ref[s * 16 + u]] = s * 16 + u
            inv_after[after_ref[s * 16 + u]] = s * 16 + u
        return carry

    lax.fori_loop(0, total // 16, invert, 0)
    for i in range(lanes * 2):
        table[RECEIVE + i] = -1
    for i in range(lanes + 1):
        count[i] = 0

    def relative(lane, sign):
        col = remainder(sign * (divide(lane, subs) - my_col) + cols, cols)
        sub = remainder(sign * (remainder(lane, subs) - my_sub) + subs, subs)
        return col * subs + sub

    def own(s, carry):
        tile = before_ref[me * tile_count + s]
        device = divide(inv_after[tile], tile_count)
        stays = device == me
        to = relative(remainder(device, lanes), 1)
        nth = count[to]
        count[to] = nth + 1
        other = jnp.where(stays | (to == subs), 0, 1)
        left = count[lanes]
        count[lanes] = left + other
        place = jnp.minimum(jnp.where(other == 1, NT - 1 - left, nth), NT - 1)
        base = jnp.where(stays, STAY, LEAVE) + jnp.maximum(place, 0) * ENTRY
        table[base + 1] = wet_ref[tile]
        table[base + 2] = s
        table[base + 3] = jnp.where(stays, s, to * 2 + jnp.minimum(nth, 1))
        row, col = divide(tile, row_tiles), remainder(tile, row_tiles)
        for n, (dr, dc) in enumerate(STEP_TO):
            r, c = row + dr, col + dc
            there = (r >= 0) & (r < tile_rows) & (c >= 0) & (c < row_tiles)
            near = jnp.where(there, tile + (dr * row_tiles + dc), tile)
            at = inv_before[near]
            table[base + 4 + 3 * n] = jnp.where(there, wet_ref[near], 0)
            table[base + 5 + 3 * n] = relative(remainder(divide(at, tile_count), lanes), -1)
            table[base + 6 + 3 * n] = remainder(at, tile_count)
        return carry

    lax.fori_loop(0, tile_count, own, 0)

    for rel in range(1, lanes):
        col = remainder(my_col + (cols - rel // subs), cols)
        sub = remainder(my_sub + (subs - rel % subs), subs)
        device = my_row * lanes + col * subs + sub
        found = jnp.int32(0)
        for s in range(tile_count):
            at = inv_after[before_ref[device * tile_count + s]]
            mine = divide(at, tile_count) == me
            place = RECEIVE + rel * 2 + jnp.minimum(found, 1)
            table[jnp.where(mine, place, spare)] = remainder(at, tile_count)
            found = found + jnp.where(mine, 1, 0)


def make_table(shape, before, after, wet):
    cols, subs, _, total = shape
    return pl.pallas_call(
        functools.partial(index_kernel, shape),
        name="index_table",
        out_shape=SMEM((RECEIVE + 2 * cols * subs + 1,), jnp.int32),
        in_specs=[pl.BlockSpec(memory_space=SMEM)] * 3,
        out_specs=pl.BlockSpec(memory_space=SMEM),
        scratch_shapes=[
            SMEM((total,), jnp.int32),
            SMEM((total,), jnp.int32),
            SMEM((cols * subs + 1,), jnp.int32),
        ],
        compiler_params=SMALL,
    )(before, after, wet)


def in_vmem(array):
    return pltpu.with_memory_space_constraint(array, VMEM)


def vmem_specs(count):
    return [pl.BlockSpec(memory_space=VMEM)] * count


def load_kernel(*refs):
    sources, refs = refs[:FIELDS], refs[FIELDS:]
    fields, (columns, pair_even, pair_odd, first, last, sem, _) = refs[:FIELDS], refs[FIELDS:]
    spill = refs[-1]
    lane = lane_index()
    odd = remainder(lax.axis_index("row"), 2) == 1
    copies = [
        pltpu.make_async_copy(sources[f], fields[f], sem.at[f]) for f in range(FIELDS)
    ]
    for copy in copies:
        copy.start()
    tile_count = fields[0].shape[0]
    blocks = tile_count * TILE_LANES // SIDE
    for f in range(FIELDS):
        copies[f].wait()
        for b in range(blocks + 1):
            target, place = (columns, pl.ds(b * SIDE, SIDE)) if b < blocks else (spill, slice(None))
            packed = target[place, :]
            for t in range(tile_count):
                at = TILE_LANES * t + COL_AT[f] - b * SIDE
                if at < SIDE and at + BOTH_COLS[f] > 0:
                    moved = pltpu.roll(fields[f][t], (at + LAST_COLS[f]) % SIDE, 1)
                    packed = jnp.where((lane >= at) & (lane < at + BOTH_COLS[f]), moved, packed)
            target[place, :] = packed
        for t in range(tile_count):
            at, count = TILE_ROWS * t + FIRST_AT[f], FIRST_ROWS[f]
            first[at : at + count, :] = fields[f][t, :count, :]
            at, count = TILE_ROWS * t + LAST_AT[f], LAST_ROWS[f]
            last[at : at + count, :] = fields[f][t, SIDE - count :, :]
    row = SIDE - HALO
    level = [fields[0][:, r, :] + fields[3][:, r, :] for r in (row, row + 1)]
    ground = jnp.maximum(fields[3][:, row, :], fields[3][:, row + 1, :])
    drag = (GRAV * STEP_TIME) * fields[4][:, row, :] * fields[4][:, row, :]
    flow = face(fields[2][:, row, :], level[0], level[1], ground, drag)
    for t in range(tile_count):
        at = TILE_ROWS * t + LAST_AT[2]
        last[at : at + 1, :] = flow[t : t + 1, :]
    half = SIDE // 2
    columns[blocks * SIDE :, :] = jnp.where(
        lane < half, spill[:half, :], pltpu.roll(spill[half:, :], half, 1)
    )
    pair_even[...] = jnp.where(odd, first[...], last[...])
    pair_odd[...] = jnp.where(odd, last[...], first[...])


def load(arrays):
    tile_count = arrays[0].shape[0]
    rows = VMEM((tile_count * TILE_ROWS, SIDE), jnp.float32)
    outs = [VMEM(array.shape, array.dtype) for array in arrays]
    outs += [VMEM((tile_count * TILE_LANES, SIDE), jnp.float32), rows, rows]
    return pl.pallas_call(
        load_kernel,
        name="load_and_pack",
        out_shape=tuple(outs),
        in_specs=[pl.BlockSpec(memory_space=pltpu.HBM)] * FIELDS,
        out_specs=tuple(vmem_specs(len(outs))),
        scratch_shapes=[
            rows,
            rows,
            pltpu.SemaphoreType.DMA((FIELDS,)),
            VMEM((SIDE, SIDE), jnp.float32),
        ],
        compiler_params=SMALL,
    )(*[pltpu.with_memory_space_constraint(array, pltpu.HBM) for array in arrays])


def join_kernel(met_even, met_odd, joined):
    odd = remainder(lax.axis_index("row"), 2) == 1
    joined[0] = jnp.where(odd, met_even[...], met_odd[...])
    joined[1] = jnp.where(odd, met_odd[...], met_even[...])


def join(met_even, met_odd):
    return pl.pallas_call(
        join_kernel,
        name="join_row_halos",
        out_shape=VMEM((2,) + met_even.shape, met_even.dtype),
        in_specs=vmem_specs(2),
        out_specs=pl.BlockSpec(memory_space=VMEM),
        compiler_params=SMALL,
    )(in_vmem(met_even), in_vmem(met_odd))


def arrivals(table, units, received, spans, outs, sem):
    def each(act):
        for n, k in enumerate(units):
            for j in range(2):
                slot = table[RECEIVE + 2 * k + j]

                @pl.when(slot >= 0)
                def _():
                    at = 0
                    for m, (start, count) in enumerate(spans):
                        for f in range(3):
                            act(
                                pltpu.make_async_copy(
                                    received[n].at[j, f, pl.ds(at, count), :],
                                    outs[f].at[slot, pl.ds(start, count), :],
                                    sem.at[n, j, f, m],
                                )
                            )
                        at += count

    return each


def place_kernel(groups, *refs):
    table, received, refs = refs[0], refs[1 : 1 + len(groups)], refs[1 + len(groups) :]
    outs, sem = refs[3:6], refs[6]
    copies = [
        arrivals(table, (k,), (array,), spans, outs, sem.at[pl.ds(n, 1)])
        for n, ((k, spans), array) in enumerate(zip(groups, received))
    ]
    for each in copies:
        each(lambda copy: copy.start())
    for each in copies:
        each(lambda copy: copy.wait())


def place(groups, table, received, partial_outs):
    count = len(received)
    return pl.pallas_call(
        functools.partial(place_kernel, groups),
        name="place_arrivals",
        out_shape=tuple(jax.ShapeDtypeStruct(o.shape, o.dtype) for o in partial_outs),
        in_specs=[pl.BlockSpec(memory_space=SMEM)]
        + vmem_specs(count)
        + [pl.BlockSpec(memory_space=ANY)] * 3,
        out_specs=tuple(pl.BlockSpec(memory_space=ANY) for _ in partial_outs),
        scratch_shapes=[pltpu.SemaphoreType.DMA((count, 2, 3, 2))],
        input_output_aliases={1 + count + f: f for f in range(3)},
        compiler_params=SMALL,
    )(table, *received, *partial_outs)


def face(flow, level, level_next, ground, friction):
    wetted = jnp.maximum(level, level_next) - ground
    drive = (GRAV * STEP_TIME / SPACING) * jnp.maximum(wetted, 0.0) * (level_next - level)
    power = jnp.exp2(POWER * jnp.log(jnp.maximum(wetted, DEPTH_FLOOR)))
    return (flow - drive) / (1.0 + friction * jnp.abs(flow) * power)


class Part:
    def __init__(self, name, base, tiles, computed, own, halo_rows, sent):
        self.name = name
        self.base = base
        self.tiles = tiles
        self.computed = computed
        self.own = own
        self.halo_rows = halo_rows
        self.sent = sent

    def chunks(self):
        for start, count in self.computed:
            for r in range(start, start + count, CHUNK):
                yield r, min(CHUNK, start + count - r)


def row_span(span):
    return pl.ds(span[0], span[1])


EDGE = 8
BAND = 24
MIDDLE = (EDGE, SIDE - 2 * EDGE)
EARLY = (
    Part("leaving_first", LEAVE, 2, ((TOP, SIDE),), ((0, SIDE),), False, (MIDDLE,)),
    Part("leaving_second", LEAVE + 2 * ENTRY, 2, ((TOP, SIDE),), ((0, SIDE),), False, (MIDDLE,)),
)
LATE = Part(
    "leaving_edges",
    LEAVE,
    NT,
    ((LO, BAND), (HI - BAND, BAND)),
    ((0, BAND - 8), (SIDE - BAND + 8, BAND - 8)),
    True,
    ((0, EDGE), (SIDE - EDGE, EDGE)),
)
WHOLE = Part("staying", STAY, NT, ((LO, HI - LO),), ((0, SIDE),), True, ((0, SIDE),))


def row_bands(r, rows, above, middle, below):
    row = r + lax.broadcasted_iota(jnp.int32, (rows, 1), 0)
    return jnp.where(row < TOP, above, jnp.where(row < TOP + SIDE, middle, below))


def fixed_row(r, rows):
    if not r <= FIXED < r + rows:
        return None
    return r + lax.broadcasted_iota(jnp.int32, (rows, 1), 0) == FIXED


def unless(where, value, other):
    return value if where is None else jnp.where(where, other, value)


def assemble(part, table, base, i, slot, fields, stacks, block, strip):
    halo_cols = stacks[0]
    lane = lane_index()
    at = GROUP * i

    def near(name):
        place = base + 5 + 3 * NEAR[name]
        return table[place], table[place + 1]

    def inside(lo, hi):
        return (lane >= at + lo) & (lane < at + hi)

    west, east = near("w"), near("e")
    for f in range(FIELDS):

        def ends(side, start, middle, left, right, out):
            rows = pl.ds(start, 8)
            mid, left_end, right_end = (
                stacks[1][place[0], side, place[1], rows, :] for place in (middle, left, right)
            )
            block[f][i, out : out + 8, :] = mid
            lower = jnp.where(lane < SIDE // 2, mid, left_end)
            upper = jnp.where(lane < SIDE // 2, right_end, mid)
            value = jnp.where(
                inside(0, 16),
                pltpu.roll(lower, (at + 8) % SIDE, 1),
                pltpu.roll(upper, (at + 24) % SIDE, 1),
            )
            if i:
                value = jnp.where(inside(0, GROUP), value, strip[f][out : out + 8, :])
            strip[f][out : out + 8, :] = value

        if part.halo_rows:
            start = SPARE + LAST_AT[f] + LAST_ROWS[f] - 8
            ends(0, start, near("n"), near("nw"), near("ne"), LO)
            ends(1, SPARE + FIRST_AT[f], near("s"), near("sw"), near("se"), TOP + SIDE)

        for start, count in part.own:
            own, out = pl.ds(start, count), pl.ds(TOP + start, count)

            def shifted(place, offset, goal):
                lanes_at = TILE_LANES * place[1] + (COL_AT[f] + offset)
                b, source = divide(lanes_at, SIDE), remainder(lanes_at, SIDE)
                beyond = jnp.minimum(b + 1, halo_cols.shape[1] - 1)
                value = jnp.where(
                    lane >= source, halo_cols[place[0], b, own, :], halo_cols[place[0], beyond, own, :]
                )
                return pltpu.roll(value, remainder(goal - source + SIDE, SIDE), 1)

            core = fields[f][slot, own, :]
            block[f][i, out, :] = core
            value = shifted(west, 0, at + 8 - LAST_COLS[f])
            if i:
                value = jnp.where(inside(0, 8), value, strip[f][out, :])
            value = jnp.where(inside(8, 16), pltpu.roll(core, (at + 8) % SIDE, 1), value)
            value = jnp.where(inside(16, 24), pltpu.roll(core, (at + 24) % SIDE, 1), value)
            value = jnp.where(inside(24, GROUP), shifted(east, LAST_COLS[f], at + 24), value)
            strip[f][out, :] = value


def prepare_strip(part, near_wet, strip, ground_x, ground_y):
    level, flow_x, flow_y, ground, friction = strip
    lane = lane_index()

    def lane_wet(center, left, right):
        value = jnp.zeros((1, SIDE), jnp.int32)
        for i in range(part.tiles):
            at = GROUP * i
            middle = near_wet(i, center) if center else 1
            sides = jnp.where(
                lane < at + 8,
                near_wet(i, left),
                jnp.where(lane < at + 24, middle, near_wet(i, right)),
            )
            value = jnp.where((lane >= at) & (lane < at + GROUP), sides, value)
        return value

    bands = (lane_wet("n", "nw", "ne"), lane_wet(None, "w", "e"), lane_wet("s", "sw", "se"))
    for r, rows in part.chunks():
        at, south = pl.ds(r, rows), pl.ds(r + 1, rows)
        z = ground[at, :]
        here, next_row = row_bands(r, rows, *bands), row_bands(r + 1, rows, *bands)
        open_x = (here == 1) & (pltpu.roll(here, SIDE - 1, 1) == 1)
        open_y = (here == 1) & (next_row == 1)
        z_east = pltpu.roll(z, SIDE - 1, 1)
        fixed = fixed_row(r, rows)
        ground_x[at, :] = jnp.where(open_x, jnp.maximum(z, z_east), CLOSED)
        ground_y[at, :] = unless(
            fixed, jnp.where(open_y, jnp.maximum(z, ground[south, :]), CLOSED), CLOSED
        )
        flow_x[at, :] = jnp.where(open_x, flow_x[at, :], 0.0)
        flow_y[at, :] = jnp.where(open_y, flow_y[at, :], 0.0)
        friction[at, :] = unless(
            fixed, (GRAV * STEP_TIME) * friction[at, :] * friction[at, :], 0.0
        )
        level[at, :] = level[at, :] + z


def prepare_tile(part, near_wet, i, block, ground_x, ground_y, strip_ground):
    level, flow_x, flow_y, ground, friction = block
    lane = lane_index()
    last = lane == SIDE - 1
    n, e, s = near_wet(i, "n"), near_wet(i, "e"), near_wet(i, "s")
    bands = (
        jnp.where(last, n * near_wet(i, "ne"), n),
        jnp.where(last, e, 1),
        jnp.where(last, s * near_wet(i, "se"), s),
    )
    for r, rows in part.chunks():
        at, south = pl.ds(r, rows), pl.ds(r + 1, rows)
        z = ground[i, at, :]
        z_east = jnp.where(
            last, pltpu.roll(strip_ground[at, :], to_east(i), 1), pltpu.roll(z, SIDE - 1, 1)
        )
        open_x = row_bands(r, rows, *bands) == 1
        open_y = (row_bands(r + 1, rows, n, 1, s) == 1) & (row_bands(r, rows, n, 1, s) == 1)
        fixed = fixed_row(r, rows)
        ground_x[i, at, :] = jnp.where(open_x, jnp.maximum(z, z_east), CLOSED)
        ground_y[i, at, :] = unless(
            fixed, jnp.where(open_y, jnp.maximum(z, ground[i, south, :]), CLOSED), CLOSED
        )
        flow_x[i, at, :] = jnp.where(open_x, flow_x[i, at, :], 0.0)
        flow_y[i, at, :] = jnp.where(open_y, flow_y[i, at, :], 0.0)
        friction[i, at, :] = unless(
            fixed, (GRAV * STEP_TIME) * friction[i, at, :] * friction[i, at, :], 0.0
        )
        level[i, at, :] = level[i, at, :] + z


def to_east(i):
    return (SIDE - 1 - GROUP * i - 24) % SIDE


def to_west(i):
    return (SIDE - GROUP * i - 7) % SIDE


def unpack_columns(part, packed, out):
    blocks, half = out.shape[0] - 1, SIDE // 2
    for start, count in part.own:
        rows = pl.ds(start, count)
        for b in range(blocks):
            out[b, rows, :] = packed[b * SIDE + start : b * SIDE + start + count, :]
        if start < half:
            n = min(count, half - start)
            out[blocks, start : start + n, :] = packed[
                blocks * SIDE + start : blocks * SIDE + start + n, :
            ]
        if start + count > half:
            low, high = max(start, half), start + count
            lower = packed[blocks * SIDE + low - half : blocks * SIDE + high - half, :]
            out[blocks, low:high, :] = pltpu.roll(lower, half, 1)


def advance_kernel(part, lanes, units, given, *refs):
    table = refs[0]
    fields = refs[1 : 1 + FIELDS]
    kinds = 2 if part.halo_rows else 1
    halos, refs = refs[1 + FIELDS : 1 + FIELDS + kinds * lanes], refs[1 + FIELDS + kinds * lanes :]
    received, refs = refs[:given], refs[given:]
    n_out = 3 if part is WHOLE else len(units)
    outs, stacks, refs = refs[:n_out], refs[n_out : n_out + kinds], refs[n_out + kinds :]
    (
        level, flow_x, flow_y, ground, friction, ground_x, ground_y,
        s_level, s_flow_x, s_flow_y, s_ground, s_friction, s_ground_x, s_ground_y,
        sem_out, sem_in,
    ) = refs
    if part is WHOLE:
        placing = arrivals(table, units, received, (MIDDLE,), outs, sem_in)
        placing(lambda copy: copy.start())
    block = (level, flow_x, flow_y, ground, friction)
    strip = (s_level, s_flow_x, s_flow_y, s_ground, s_friction)
    lane = lane_index()
    last, first = lane == SIDE - 1, lane == 0

    def entry(i):
        at = part.base + i * ENTRY
        return table[at + 1], table[at + 2], table[at + 3]

    def near_wet(i, name):
        return table[part.base + i * ENTRY + 4 + 3 * NEAR[name]]

    for k in range(lanes):
        for n in range(kinds):
            if n:
                for side in range(2):
                    for t in range(fields[0].shape[0]):
                        stacks[1][k, side, t, :SPARE, :] = jnp.zeros((SPARE, SIDE), jnp.float32)
                        stacks[1][k, side, t, SPARE : SPARE + TILE_ROWS, :] = halos[kinds * k + 1][
                            side, TILE_ROWS * t : TILE_ROWS * (t + 1), :
                        ]
            else:
                unpack_columns(part, halos[kinds * k], stacks[0].at[k])
    for i in range(part.tiles):
        base = part.base + i * ENTRY
        assemble(part, table, base, i, entry(i)[1], fields, stacks, block, strip)
    prepare_strip(part, near_wet, strip, s_ground_x, s_ground_y)
    for i in range(part.tiles):
        prepare_tile(part, near_wet, i, block, ground_x, ground_y, s_ground)

    def step(_, carry):
        for r, rows in part.chunks():
            at, south = pl.ds(r, rows), pl.ds(r + 1, rows)
            e, c = s_level[at, :], s_friction[at, :]
            e_east = pltpu.roll(e, SIDE - 1, 1)
            s_flow_x[at, :] = face(s_flow_x[at, :], e, e_east, s_ground_x[at, :], c)
            s_flow_y[at, :] = face(s_flow_y[at, :], e, s_level[south, :], s_ground_y[at, :], c)
        for i in range(part.tiles):
            for r, rows in part.chunks():
                at, south = pl.ds(r, rows), pl.ds(r + 1, rows)
                e, c = level[i, at, :], friction[i, at, :]
                e_east = jnp.where(
                    last, pltpu.roll(s_level[at, :], to_east(i), 1), pltpu.roll(e, SIDE - 1, 1)
                )
                flow_x[i, at, :] = face(flow_x[i, at, :], e, e_east, ground_x[i, at, :], c)
                flow_y[i, at, :] = face(
                    flow_y[i, at, :], e, level[i, south, :], ground_y[i, at, :], c
                )
        for r, rows in part.chunks():
            at, north = pl.ds(r, rows), pl.ds(r - 1, rows)
            qx = s_flow_x[at, :]
            s_level[at, :] = s_level[at, :] + RATE * (
                (pltpu.roll(qx, 1, 1) - qx) + (s_flow_y[north, :] - s_flow_y[at, :])
            )
        for i in range(part.tiles):
            for r, rows in part.chunks():
                at, north = pl.ds(r, rows), pl.ds(r - 1, rows)
                qx = flow_x[i, at, :]
                qx_west = jnp.where(
                    first, pltpu.roll(s_flow_x[at, :], to_west(i), 1), pltpu.roll(qx, 1, 1)
                )
                level[i, at, :] = level[i, at, :] + RATE * (
                    (qx_west - qx) + (flow_y[i, north, :] - flow_y[i, at, :])
                )
        return carry

    lax.fori_loop(0, STEPS, step, 0, unroll=True)

    results = (level, flow_x, flow_y)
    for i in range(part.tiles):
        wet, slot, _ = entry(i)
        for start, count in part.sent:
            own, at = pl.ds(start, count), pl.ds(TOP + start, count)
            level[i, at, :] = level[i, at, :] - ground[i, at, :]
            for f in range(3):
                results[f][i, at, :] = jnp.where(
                    wet == 1, results[f][i, at, :], fields[f][slot, own, :]
                )

    if part is not WHOLE:
        for i in range(part.tiles):
            target = entry(i)[2]
            for out_ref, k in zip(outs, units):
                @pl.when(divide(target, 2) == k)
                def _():
                    out = 0
                    for start, count in part.sent:
                        for f in range(3):
                            value = results[f][i, pl.ds(TOP + start, count), :]
                            out_ref[remainder(target, 2), f, out : out + count, :] = value
                        out += count

    else:
        copies = [
            pltpu.make_async_copy(
                results[f].at[i, pl.ds(TOP, SIDE), :], outs[f].at[entry(i)[2]], sem_out.at[i, f]
            )
            for i in range(part.tiles)
            for f in range(3)
        ]
        for copy in copies:
            copy.start()
        placing(lambda copy: copy.wait())
        for copy in copies:
            copy.wait()


def advance(part, table, fields, halos, units, given=()):
    lanes = len(halos)
    sent = sum(count for _, count in part.sent)
    if part is WHOLE:
        outs = (jax.ShapeDtypeStruct(fields[0].shape, jnp.float32),) * 3
        out_specs = [pl.BlockSpec(memory_space=ANY)] * 3
    else:
        outs = (VMEM((2, 3, sent, SIDE), jnp.float32),) * len(units)
        out_specs = vmem_specs(len(units))
    if not part.halo_rows:
        halos = [group[:1] for group in halos]
    flat = [array for group in halos for array in group]
    tile_count = fields[0].shape[0]
    stacks = [VMEM((lanes, -(-tile_count * TILE_LANES // SIDE), SIDE, SIDE), jnp.float32)]
    if part.halo_rows:
        stacks.append(VMEM((lanes, 2, tile_count, SPARE + TILE_ROWS + 10, SIDE), jnp.float32))
    block = VMEM((part.tiles, ROWS, SIDE), jnp.float32)
    strip = VMEM((ROWS, SIDE), jnp.float32)
    cells = (part.tiles + 1) * sum(count for _, count in part.computed) * SIDE * STEPS
    return pl.pallas_call(
        functools.partial(advance_kernel, part, lanes, units, len(given)),
        name="advance_" + part.name,
        out_shape=outs,
        in_specs=[pl.BlockSpec(memory_space=SMEM)]
        + vmem_specs(FIELDS + len(flat) + len(given)),
        input_output_aliases={
            1 + FIELDS + len(flat) + n: n for n in range(0 if part is WHOLE else len(given))
        },
        out_specs=tuple(out_specs),
        scratch_shapes=stacks
        + [block] * 7
        + [strip] * 7
        + [
            pltpu.SemaphoreType.DMA((part.tiles, 3)),
            pltpu.SemaphoreType.DMA((max(len(given), 1), 2, 3, 1)),
        ],
        compiler_params=pltpu.CompilerParams(vmem_limit_bytes=12 * 1024 * 1024),
        cost_estimate=pl.CostEstimate(
            flops=60 * cells, bytes_accessed=8 * part.tiles * sent * SIDE * 4, transcendentals=6 * cells
        ),
    )(table, *fields, *flat, *given)


def shift_lanes(array, col_shift, sub_shift):
    cols, subs = lax.axis_size("col"), lax.axis_size("sub")
    pairs = [
        (c * subs + s, ((c + col_shift) % cols) * subs + (s + sub_shift) % subs)
        for c in range(cols)
        for s in range(subs)
    ]
    return lax.ppermute(array, ("col", "sub"), pairs)


def over_cols(array):
    return [array] + [shift_lanes(array, c, 0) for c in range(1, lax.axis_size("col"))]


def over_subs(parts):
    subs = lax.axis_size("sub")
    return [
        in_vmem(part if s == 0 else shift_lanes(part, 0, s)) for part in parts for s in range(subs)
    ]


def meet_rows(array, parity):
    rows, subs = lax.axis_size("row"), lax.axis_size("sub")
    pairs = []
    for r in range(rows):
        other = r + 1 if r % 2 == parity else r - 1
        for s in range(subs):
            if 0 <= other < rows:
                pairs.append((r * subs + s, other * subs + s))
            else:
                pairs.append((r * subs + s, r * subs + (s + 1) % subs))
    return lax.ppermute(array, ("row", "sub"), pairs)


def shards(
    water_depth, flow_east, flow_south, bed_level, manning_n, placed_before, placed_after, wet_tiles
):
    cols, subs = lax.axis_size("col"), lax.axis_size("sub")
    tile_count = water_depth.shape[0]
    *fields, columns, pair_even, pair_odd = load(
        (water_depth, flow_east, flow_south, bed_level, manning_n)
    )
    fields = [in_vmem(field) for field in fields]
    columns = over_cols(columns)
    met_even, met_odd = meet_rows(pair_even, 0), meet_rows(pair_odd, 1)
    table = make_table(
        (cols, subs, tile_count, placed_before.shape[0]), placed_before, placed_after, wet_tiles
    )
    joined = join(met_even, met_odd)
    near_rows = over_cols(joined)
    columns[1:], joined, table = lax.optimization_barrier((columns[1:], joined, table))
    near_rows[0] = joined
    table = pltpu.with_memory_space_constraint(table, SMEM)
    near_rows = over_subs(near_rows)
    columns = over_subs(columns)

    def send(part, k):
        return in_vmem(shift_lanes(part, k // subs, k % subs))

    units = tuple(range(1, cols * subs))
    ahead, others = subs, tuple(k for k in units if k != subs)
    alone = [(part,) for part in columns]
    first, *rest = advance(EARLY[0], table, fields, alone, (ahead,) + others)
    rest = advance(EARLY[1], table, fields, alone, others, [in_vmem(part) for part in rest])
    middle = {ahead: send(first, ahead)}
    middle.update((k, send(part, k)) for k, part in zip(others, rest))
    halos = list(zip(columns, near_rows))
    edges = list(advance(LATE, table, fields, halos, units))
    middle[ahead], edges[0] = lax.optimization_barrier((middle[ahead], edges[0]))
    middle[ahead] = in_vmem(middle[ahead])
    edges = [send(part, k) for k, part in zip(units, edges)]
    soon = tuple(range(1, subs)) + (ahead,)
    last = tuple(k for k in units if k not in soon)
    outs = advance(WHOLE, table, fields, halos, soon, [middle[k] for k in soon])
    near = [n for n, k in enumerate(units) if k < subs]
    far = [n for n, k in enumerate(units) if k >= subs]
    groups = tuple((k, (MIDDLE,)) for k in last) + tuple((units[n], LATE.sent) for n in near)
    outs = place(groups, table, [middle[k] for k in last] + [edges[n] for n in near], outs)
    groups = tuple((units[n], LATE.sent) for n in far)
    return place(groups, table, [edges[n] for n in far], outs)


def solution(mesh):
    tiles = P(("basin", "row", "col", "sub"), None, None)
    return jax.shard_map(
        shards,
        mesh=mesh,
        in_specs=(tiles,) * FIELDS + (P("basin"),) * 3,
        out_specs=(tiles,) * 3,
        check_vma=False,
    )
```

```python
import functools
import math

import jax
import jax.numpy as jnp
from jax import lax
from jax.experimental import pallas as pl
from jax.experimental.pallas import tpu as pltpu
from jax.sharding import PartitionSpec as P

STEPS = 6
GRAV = 9.81
STEP_TIME = 0.5
SPACING = 5.0
RATE = 0.1
DEPTH_FLOOR = 0.3

FIELDS = 5
HALO = STEPS
LAST_COLS = (HALO, HALO, HALO - 1, HALO, HALO)
FIRST_COLS = (HALO, HALO - 1, HALO - 1, HALO, HALO - 1)
LAST_ROWS = (HALO - 1, HALO - 1, HALO, HALO - 1, HALO - 1)
FIRST_ROWS = (HALO, HALO - 1, HALO - 1, HALO, HALO - 1)


def starts(counts):
    return [sum(counts[:f]) for f in range(len(counts))]


BOTH_COLS = tuple(a + b for a, b in zip(LAST_COLS, FIRST_COLS))
TILE_LANES = sum(BOTH_COLS)
TILE_ROWS = max(sum(LAST_ROWS), sum(FIRST_ROWS))
COL_AT, LAST_AT, FIRST_AT = starts(BOTH_COLS), starts(LAST_ROWS), starts(FIRST_ROWS)
SIDE = 128
TOP = 16
ROWS = SIDE + 32
LO = 8
HI = SIDE + 24
CHUNK = 24
SPARE = 3
FIXED = TOP - HALO
NT = 4
GROUP = SIDE // NT
CLOSED = 1e30
POWER = -(7.0 / 3.0) / math.log(2.0)

ENTRY = 32
NEAR = {"w": 0, "e": 1, "n": 2, "s": 3, "nw": 4, "ne": 5, "sw": 6, "se": 7}
STEP_TO = ((0, -1), (0, 1), (-1, 0), (1, 0), (-1, -1), (-1, 1), (1, -1), (1, 1))
LEAVE, STAY, RECEIVE = 0, NT * ENTRY, 2 * NT * ENTRY

SMEM = pltpu.SMEM
VMEM = pltpu.VMEM
ANY = pl.ANY
SMALL = pltpu.CompilerParams(vmem_limit_bytes=2 * 1024 * 1024)


def lane_index():
    return lax.broadcasted_iota(jnp.int32, (1, SIDE), 1)


def divide(value, size):
    if size & (size - 1):
        return lax.div(value, size)
    return lax.shift_right_logical(value, size.bit_length() - 1)


def remainder(value, size):
    if size & (size - 1):
        return lax.rem(value, size)
    return value & (size - 1)


def index_kernel(shape, before_ref, after_ref, wet_ref, table, inv_before, inv_after, count):
    cols, subs, tile_count, total = shape
    lanes = cols * subs
    row_tiles = lanes * tile_count
    tile_rows = total // row_tiles
    my_row, my_col, my_sub = (lax.axis_index(name) for name in ("row", "col", "sub"))
    me = my_row * lanes + my_col * subs + my_sub
    spare = RECEIVE + 2 * lanes

    def invert(s, carry):
        for u in range(16):
            inv_before[before_ref[s * 16 + u]] = s * 16 + u
            inv_after[after_ref[s * 16 + u]] = s * 16 + u
        return carry

    lax.fori_loop(0, total // 16, invert, 0)
    for i in range(lanes * 2):
        table[RECEIVE + i] = -1
    for i in range(lanes + 1):
        count[i] = 0

    def relative(lane, sign):
        col = remainder(sign * (divide(lane, subs) - my_col) + cols, cols)
        sub = remainder(sign * (remainder(lane, subs) - my_sub) + subs, subs)
        return col * subs + sub

    def own(s, carry):
        tile = before_ref[me * tile_count + s]
        device = divide(inv_after[tile], tile_count)
        stays = device == me
        to = relative(remainder(device, lanes), 1)
        nth = count[to]
        count[to] = nth + 1
        other = jnp.where(stays | (to == subs), 0, 1)
        left = count[lanes]
        count[lanes] = left + other
        place = jnp.minimum(jnp.where(other == 1, NT - 1 - left, nth), NT - 1)
        base = jnp.where(stays, STAY, LEAVE) + jnp.maximum(place, 0) * ENTRY
        table[base + 1] = wet_ref[tile]
        table[base + 2] = s
        table[base + 3] = jnp.where(stays, s, to * 2 + jnp.minimum(nth, 1))
        row, col = divide(tile, row_tiles), remainder(tile, row_tiles)
        for n, (dr, dc) in enumerate(STEP_TO):
            r, c = row + dr, col + dc
            there = (r >= 0) & (r < tile_rows) & (c >= 0) & (c < row_tiles)
            near = jnp.where(there, tile + (dr * row_tiles + dc), tile)
            at = inv_before[near]
            table[base + 4 + 3 * n] = jnp.where(there, wet_ref[near], 0)
            table[base + 5 + 3 * n] = relative(remainder(divide(at, tile_count), lanes), -1)
            table[base + 6 + 3 * n] = remainder(at, tile_count)
        return carry

    lax.fori_loop(0, tile_count, own, 0)

    for rel in range(1, lanes):
        col = remainder(my_col + (cols - rel // subs), cols)
        sub = remainder(my_sub + (subs - rel % subs), subs)
        device = my_row * lanes + col * subs + sub
        found = jnp.int32(0)
        for s in range(tile_count):
            at = inv_after[before_ref[device * tile_count + s]]
            mine = divide(at, tile_count) == me
            place = RECEIVE + rel * 2 + jnp.minimum(found, 1)
            table[jnp.where(mine, place, spare)] = remainder(at, tile_count)
            found = found + jnp.where(mine, 1, 0)


def make_table(shape, before, after, wet):
    cols, subs, _, total = shape
    return pl.pallas_call(
        functools.partial(index_kernel, shape),
        name="index_table",
        out_shape=SMEM((RECEIVE + 2 * cols * subs + 1,), jnp.int32),
        in_specs=[pl.BlockSpec(memory_space=SMEM)] * 3,
        out_specs=pl.BlockSpec(memory_space=SMEM),
        scratch_shapes=[
            SMEM((total,), jnp.int32),
            SMEM((total,), jnp.int32),
            SMEM((cols * subs + 1,), jnp.int32),
        ],
        compiler_params=SMALL,
    )(before, after, wet)


def in_vmem(array):
    return pltpu.with_memory_space_constraint(array, VMEM)


def vmem_specs(count):
    return [pl.BlockSpec(memory_space=VMEM)] * count


def load_kernel(*refs):
    sources, refs = refs[:FIELDS], refs[FIELDS:]
    fields, (columns, pair_even, pair_odd, first, last, sem, _) = refs[:FIELDS], refs[FIELDS:]
    spill = refs[-1]
    lane = lane_index()
    odd = remainder(lax.axis_index("row"), 2) == 1
    copies = [
        pltpu.make_async_copy(sources[f], fields[f], sem.at[f]) for f in range(FIELDS)
    ]
    for copy in copies:
        copy.start()
    tile_count = fields[0].shape[0]
    blocks = tile_count * TILE_LANES // SIDE
    for f in range(FIELDS):
        copies[f].wait()
        for b in range(blocks + 1):
            target, place = (columns, pl.ds(b * SIDE, SIDE)) if b < blocks else (spill, slice(None))
            packed = target[place, :]
            for t in range(tile_count):
                at = TILE_LANES * t + COL_AT[f] - b * SIDE
                if at < SIDE and at + BOTH_COLS[f] > 0:
                    moved = pltpu.roll(fields[f][t], (at + LAST_COLS[f]) % SIDE, 1)
                    packed = jnp.where((lane >= at) & (lane < at + BOTH_COLS[f]), moved, packed)
            target[place, :] = packed
        for t in range(tile_count):
            at, count = TILE_ROWS * t + FIRST_AT[f], FIRST_ROWS[f]
            first[at : at + count, :] = fields[f][t, :count, :]
            at, count = TILE_ROWS * t + LAST_AT[f], LAST_ROWS[f]
            last[at : at + count, :] = fields[f][t, SIDE - count :, :]
    row = SIDE - HALO
    level = [fields[0][:, r, :] + fields[3][:, r, :] for r in (row, row + 1)]
    ground = jnp.maximum(fields[3][:, row, :], fields[3][:, row + 1, :])
    drag = (GRAV * STEP_TIME) * fields[4][:, row, :] * fields[4][:, row, :]
    flow = face(fields[2][:, row, :], level[0], level[1], ground, drag)
    for t in range(tile_count):
        at = TILE_ROWS * t + LAST_AT[2]
        last[at : at + 1, :] = flow[t : t + 1, :]
    half = SIDE // 2
    columns[blocks * SIDE :, :] = jnp.where(
        lane < half, spill[:half, :], pltpu.roll(spill[half:, :], half, 1)
    )
    pair_even[...] = jnp.where(odd, first[...], last[...])
    pair_odd[...] = jnp.where(odd, last[...], first[...])


def load(arrays):
    tile_count = arrays[0].shape[0]
    rows = VMEM((tile_count * TILE_ROWS, SIDE), jnp.float32)
    outs = [VMEM(array.shape, array.dtype) for array in arrays]
    outs += [VMEM((tile_count * TILE_LANES, SIDE), jnp.float32), rows, rows]
    return pl.pallas_call(
        load_kernel,
        name="load_and_pack",
        out_shape=tuple(outs),
        in_specs=[pl.BlockSpec(memory_space=pltpu.HBM)] * FIELDS,
        out_specs=tuple(vmem_specs(len(outs))),
        scratch_shapes=[
            rows,
            rows,
            pltpu.SemaphoreType.DMA((FIELDS,)),
            VMEM((SIDE, SIDE), jnp.float32),
        ],
        compiler_params=SMALL,
    )(*[pltpu.with_memory_space_constraint(array, pltpu.HBM) for array in arrays])


def join_kernel(met_even, met_odd, joined):
    odd = remainder(lax.axis_index("row"), 2) == 1
    joined[0] = jnp.where(odd, met_even[...], met_odd[...])
    joined[1] = jnp.where(odd, met_odd[...], met_even[...])


def join(met_even, met_odd):
    return pl.pallas_call(
        join_kernel,
        name="join_row_halos",
        out_shape=VMEM((2,) + met_even.shape, met_even.dtype),
        in_specs=vmem_specs(2),
        out_specs=pl.BlockSpec(memory_space=VMEM),
        compiler_params=SMALL,
    )(in_vmem(met_even), in_vmem(met_odd))


def arrivals(table, units, received, spans, outs, sem):
    def each(act):
        for n, k in enumerate(units):
            for j in range(2):
                slot = table[RECEIVE + 2 * k + j]

                @pl.when(slot >= 0)
                def _():
                    act(n, j, slot)

    def start(n, j, slot):
        at = 0
        for begin, count in spans:
            for f in range(3):
                pltpu.make_async_copy(
                    received[n].at[j, f, pl.ds(at, count), :],
                    outs[f].at[slot, pl.ds(begin, count), :],
                    sem.at[n, j],
                ).start()
            at += count

    def wait(n, j, slot):
        tile = received[n].at[j]
        pltpu.make_async_copy(tile, tile, sem.at[n, j]).wait()

    return lambda: each(start), lambda: each(wait)


def place_kernel(groups, *refs):
    table, received, refs = refs[0], refs[1 : 1 + len(groups)], refs[1 + len(groups) :]
    outs, sem = refs[3:6], refs[6]
    copies = [
        arrivals(table, (k,), (array,), spans, outs, sem.at[pl.ds(n, 1)])
        for n, ((k, spans), array) in enumerate(zip(groups, received))
    ]
    for start, _ in copies:
        start()
    for _, wait in copies:
        wait()


def place(groups, table, received, partial_outs):
    count = len(received)
    return pl.pallas_call(
        functools.partial(place_kernel, groups),
        name="place_arrivals",
        out_shape=tuple(jax.ShapeDtypeStruct(o.shape, o.dtype) for o in partial_outs),
        in_specs=[pl.BlockSpec(memory_space=SMEM)]
        + vmem_specs(count)
        + [pl.BlockSpec(memory_space=ANY)] * 3,
        out_specs=tuple(pl.BlockSpec(memory_space=ANY) for _ in partial_outs),
        scratch_shapes=[pltpu.SemaphoreType.DMA((count, 2))],
        input_output_aliases={1 + count + f: f for f in range(3)},
        compiler_params=SMALL,
    )(table, *received, *partial_outs)


def face(flow, level, level_next, ground, friction):
    wetted = jnp.maximum(level, level_next) - ground
    drive = (GRAV * STEP_TIME / SPACING) * jnp.maximum(wetted, 0.0) * (level_next - level)
    power = jnp.exp2(POWER * jnp.log(jnp.maximum(wetted, DEPTH_FLOOR)))
    return (flow - drive) / (1.0 + friction * jnp.abs(flow) * power)


class Part:
    def __init__(self, name, base, tiles, computed, own, halo_rows, sent):
        self.name = name
        self.base = base
        self.tiles = tiles
        self.computed = computed
        self.own = own
        self.halo_rows = halo_rows
        self.sent = sent

    def chunks(self):
        for start, count in self.computed:
            for r in range(start, start + count, CHUNK):
                yield r, min(CHUNK, start + count - r)


def row_span(span):
    return pl.ds(span[0], span[1])


EDGE = 8
BAND = 24
MIDDLE = (EDGE, SIDE - 2 * EDGE)
EARLY = (
    Part("leaving_first", LEAVE, 2, ((TOP, SIDE),), ((0, SIDE),), False, (MIDDLE,)),
    Part("leaving_second", LEAVE + 2 * ENTRY, 2, ((TOP, SIDE),), ((0, SIDE),), False, (MIDDLE,)),
)
LATE = Part(
    "leaving_edges",
    LEAVE,
    NT,
    ((LO, BAND), (HI - BAND, BAND)),
    ((0, BAND - 8), (SIDE - BAND + 8, BAND - 8)),
    True,
    ((0, EDGE), (SIDE - EDGE, EDGE)),
)
WHOLE = Part("staying", STAY, NT, ((LO, HI - LO),), ((0, SIDE),), True, ((0, SIDE),))


def row_bands(r, rows, above, middle, below):
    row = r + lax.broadcasted_iota(jnp.int32, (rows, 1), 0)
    return jnp.where(row < TOP, above, jnp.where(row < TOP + SIDE, middle, below))


def fixed_row(r, rows):
    if not r <= FIXED < r + rows:
        return None
    return r + lax.broadcasted_iota(jnp.int32, (rows, 1), 0) == FIXED


def unless(where, value, other):
    return value if where is None else jnp.where(where, other, value)


def assemble(part, table, base, i, slot, fields, stacks, block, strip):
    halo_cols = stacks[0]
    lane = lane_index()
    at = GROUP * i

    def near(name):
        place = base + 5 + 3 * NEAR[name]
        return table[place], table[place + 1]

    def inside(lo, hi):
        return (lane >= at + lo) & (lane < at + hi)

    west, east = near("w"), near("e")
    for f in range(FIELDS):

        def ends(side, start, middle, left, right, out):
            rows = pl.ds(start, 8)
            mid, left_end, right_end = (
                stacks[1][place[0], side, place[1], rows, :] for place in (middle, left, right)
            )
            block[f][i, out : out + 8, :] = mid
            lower = jnp.where(lane < SIDE // 2, mid, left_end)
            upper = jnp.where(lane < SIDE // 2, right_end, mid)
            value = jnp.where(
                inside(0, 16),
                pltpu.roll(lower, (at + 8) % SIDE, 1),
                pltpu.roll(upper, (at + 24) % SIDE, 1),
            )
            if i:
                value = jnp.where(inside(0, GROUP), value, strip[f][out : out + 8, :])
            strip[f][out : out + 8, :] = value

        if part.halo_rows:
            start = SPARE + LAST_AT[f] + LAST_ROWS[f] - 8
            ends(0, start, near("n"), near("nw"), near("ne"), LO)
            ends(1, SPARE + FIRST_AT[f], near("s"), near("sw"), near("se"), TOP + SIDE)

        for start, count in part.own:
            own, out = pl.ds(start, count), pl.ds(TOP + start, count)

            def shifted(place, offset, goal):
                lanes_at = TILE_LANES * place[1] + (COL_AT[f] + offset)
                b, source = divide(lanes_at, SIDE), remainder(lanes_at, SIDE)
                beyond = jnp.minimum(b + 1, halo_cols.shape[1] - 1)
                value = jnp.where(
                    lane >= source, halo_cols[place[0], b, own, :], halo_cols[place[0], beyond, own, :]
                )
                return pltpu.roll(value, remainder(goal - source + SIDE, SIDE), 1)

            core = fields[f][slot, own, :]
            block[f][i, out, :] = core
            value = shifted(west, 0, at + 8 - LAST_COLS[f])
            if i:
                value = jnp.where(inside(0, 8), value, strip[f][out, :])
            value = jnp.where(inside(8, 16), pltpu.roll(core, (at + 8) % SIDE, 1), value)
            value = jnp.where(inside(16, 24), pltpu.roll(core, (at + 24) % SIDE, 1), value)
            value = jnp.where(inside(24, GROUP), shifted(east, LAST_COLS[f], at + 24), value)
            strip[f][out, :] = value


def prepare_strip(part, near_wet, strip, ground_x, ground_y):
    level, flow_x, flow_y, ground, friction = strip
    lane = lane_index()

    def lane_wet(center, left, right):
        value = jnp.zeros((1, SIDE), jnp.int32)
        for i in range(part.tiles):
            at = GROUP * i
            middle = near_wet(i, center) if center else 1
            sides = jnp.where(
                lane < at + 8,
                near_wet(i, left),
                jnp.where(lane < at + 24, middle, near_wet(i, right)),
            )
            value = jnp.where((lane >= at) & (lane < at + GROUP), sides, value)
        return value

    bands = (lane_wet("n", "nw", "ne"), lane_wet(None, "w", "e"), lane_wet("s", "sw", "se"))
    for r, rows in part.chunks():
        at, south = pl.ds(r, rows), pl.ds(r + 1, rows)
        z = ground[at, :]
        here, next_row = row_bands(r, rows, *bands), row_bands(r + 1, rows, *bands)
        open_x = (here == 1) & (pltpu.roll(here, SIDE - 1, 1) == 1)
        open_y = (here == 1) & (next_row == 1)
        z_east = pltpu.roll(z, SIDE - 1, 1)
        fixed = fixed_row(r, rows)
        ground_x[at, :] = jnp.where(open_x, jnp.maximum(z, z_east), CLOSED)
        ground_y[at, :] = unless(
            fixed, jnp.where(open_y, jnp.maximum(z, ground[south, :]), CLOSED), CLOSED
        )
        flow_x[at, :] = jnp.where(open_x, flow_x[at, :], 0.0)
        flow_y[at, :] = jnp.where(open_y, flow_y[at, :], 0.0)
        friction[at, :] = unless(
            fixed, (GRAV * STEP_TIME) * friction[at, :] * friction[at, :], 0.0
        )
        level[at, :] = level[at, :] + z


def prepare_tile(part, near_wet, i, block, ground_x, ground_y, strip_ground):
    level, flow_x, flow_y, ground, friction = block
    lane = lane_index()
    last = lane == SIDE - 1
    n, e, s = near_wet(i, "n"), near_wet(i, "e"), near_wet(i, "s")
    bands = (
        jnp.where(last, n * near_wet(i, "ne"), n),
        jnp.where(last, e, 1),
        jnp.where(last, s * near_wet(i, "se"), s),
    )
    for r, rows in part.chunks():
        at, south = pl.ds(r, rows), pl.ds(r + 1, rows)
        z = ground[i, at, :]
        z_east = jnp.where(
            last, pltpu.roll(strip_ground[at, :], to_east(i), 1), pltpu.roll(z, SIDE - 1, 1)
        )
        open_x = row_bands(r, rows, *bands) == 1
        open_y = (row_bands(r + 1, rows, n, 1, s) == 1) & (row_bands(r, rows, n, 1, s) == 1)
        fixed = fixed_row(r, rows)
        ground_x[i, at, :] = jnp.where(open_x, jnp.maximum(z, z_east), CLOSED)
        ground_y[i, at, :] = unless(
            fixed, jnp.where(open_y, jnp.maximum(z, ground[i, south, :]), CLOSED), CLOSED
        )
        flow_x[i, at, :] = jnp.where(open_x, flow_x[i, at, :], 0.0)
        flow_y[i, at, :] = jnp.where(open_y, flow_y[i, at, :], 0.0)
        friction[i, at, :] = unless(
            fixed, (GRAV * STEP_TIME) * friction[i, at, :] * friction[i, at, :], 0.0
        )
        level[i, at, :] = level[i, at, :] + z


def to_east(i):
    return (SIDE - 1 - GROUP * i - 24) % SIDE


def to_west(i):
    return (SIDE - GROUP * i - 7) % SIDE


def unpack_columns(part, packed, out):
    blocks, half = out.shape[0] - 1, SIDE // 2
    for start, count in part.own:
        rows = pl.ds(start, count)
        for b in range(blocks):
            out[b, rows, :] = packed[b * SIDE + start : b * SIDE + start + count, :]
        if start < half:
            n = min(count, half - start)
            out[blocks, start : start + n, :] = packed[
                blocks * SIDE + start : blocks * SIDE + start + n, :
            ]
        if start + count > half:
            low, high = max(start, half), start + count
            lower = packed[blocks * SIDE + low - half : blocks * SIDE + high - half, :]
            out[blocks, low:high, :] = pltpu.roll(lower, half, 1)


def advance_kernel(part, lanes, units, given, *refs):
    table = refs[0]
    fields = refs[1 : 1 + FIELDS]
    kinds = 2 if part.halo_rows else 1
    halos, refs = refs[1 + FIELDS : 1 + FIELDS + kinds * lanes], refs[1 + FIELDS + kinds * lanes :]
    received, refs = refs[:given], refs[given:]
    n_out = 3 if part is WHOLE else len(units)
    outs, stacks, refs = refs[:n_out], refs[n_out : n_out + kinds], refs[n_out + kinds :]
    (
        level, flow_x, flow_y, ground, friction, ground_x, ground_y,
        s_level, s_flow_x, s_flow_y, s_ground, s_friction, s_ground_x, s_ground_y,
        sem_out, sem_in,
    ) = refs
    if part is WHOLE:
        start_placing, wait_placing = arrivals(table, units, received, (MIDDLE,), outs, sem_in)
        start_placing()
    block = (level, flow_x, flow_y, ground, friction)
    strip = (s_level, s_flow_x, s_flow_y, s_ground, s_friction)
    lane = lane_index()
    last, first = lane == SIDE - 1, lane == 0

    def entry(i):
        at = part.base + i * ENTRY
        return table[at + 1], table[at + 2], table[at + 3]

    def near_wet(i, name):
        return table[part.base + i * ENTRY + 4 + 3 * NEAR[name]]

    for k in range(lanes):
        for n in range(kinds):
            if n:
                for side in range(2):
                    for t in range(fields[0].shape[0]):
                        stacks[1][k, side, t, :SPARE, :] = jnp.zeros((SPARE, SIDE), jnp.float32)
                        stacks[1][k, side, t, SPARE : SPARE + TILE_ROWS, :] = halos[kinds * k + 1][
                            side, TILE_ROWS * t : TILE_ROWS * (t + 1), :
                        ]
            else:
                unpack_columns(part, halos[kinds * k], stacks[0].at[k])
    for i in range(part.tiles):
        base = part.base + i * ENTRY
        assemble(part, table, base, i, entry(i)[1], fields, stacks, block, strip)
    prepare_strip(part, near_wet, strip, s_ground_x, s_ground_y)
    for i in range(part.tiles):
        prepare_tile(part, near_wet, i, block, ground_x, ground_y, s_ground)

    def step(_, carry):
        for r, rows in part.chunks():
            at, south = pl.ds(r, rows), pl.ds(r + 1, rows)
            e, c = s_level[at, :], s_friction[at, :]
            e_east = pltpu.roll(e, SIDE - 1, 1)
            s_flow_x[at, :] = face(s_flow_x[at, :], e, e_east, s_ground_x[at, :], c)
            s_flow_y[at, :] = face(s_flow_y[at, :], e, s_level[south, :], s_ground_y[at, :], c)
        for i in range(part.tiles):
            for r, rows in part.chunks():
                at, south = pl.ds(r, rows), pl.ds(r + 1, rows)
                e, c = level[i, at, :], friction[i, at, :]
                e_east = jnp.where(
                    last, pltpu.roll(s_level[at, :], to_east(i), 1), pltpu.roll(e, SIDE - 1, 1)
                )
                flow_x[i, at, :] = face(flow_x[i, at, :], e, e_east, ground_x[i, at, :], c)
                flow_y[i, at, :] = face(
                    flow_y[i, at, :], e, level[i, south, :], ground_y[i, at, :], c
                )
        for r, rows in part.chunks():
            at, north = pl.ds(r, rows), pl.ds(r - 1, rows)
            qx = s_flow_x[at, :]
            s_level[at, :] = s_level[at, :] + RATE * (
                (pltpu.roll(qx, 1, 1) - qx) + (s_flow_y[north, :] - s_flow_y[at, :])
            )
        for i in range(part.tiles):
            for r, rows in part.chunks():
                at, north = pl.ds(r, rows), pl.ds(r - 1, rows)
                qx = flow_x[i, at, :]
                qx_west = jnp.where(
                    first, pltpu.roll(s_flow_x[at, :], to_west(i), 1), pltpu.roll(qx, 1, 1)
                )
                level[i, at, :] = level[i, at, :] + RATE * (
                    (qx_west - qx) + (flow_y[i, north, :] - flow_y[i, at, :])
                )
        return carry

    lax.fori_loop(0, STEPS, step, 0, unroll=True)

    results = (level, flow_x, flow_y)
    for i in range(part.tiles):
        wet, slot, _ = entry(i)
        for start, count in part.sent:
            own, at = pl.ds(start, count), pl.ds(TOP + start, count)
            level[i, at, :] = level[i, at, :] - ground[i, at, :]
            for f in range(3):
                results[f][i, at, :] = jnp.where(
                    wet == 1, results[f][i, at, :], fields[f][slot, own, :]
                )

    if part is not WHOLE:
        for i in range(part.tiles):
            target = entry(i)[2]
            for out_ref, k in zip(outs, units):
                @pl.when(divide(target, 2) == k)
                def _():
                    out = 0
                    for start, count in part.sent:
                        for f in range(3):
                            value = results[f][i, pl.ds(TOP + start, count), :]
                            out_ref[remainder(target, 2), f, out : out + count, :] = value
                        out += count

    else:
        copies = [
            pltpu.make_async_copy(
                results[f].at[i, pl.ds(TOP, SIDE), :], outs[f].at[entry(i)[2]], sem_out.at[i, f]
            )
            for i in range(part.tiles)
            for f in range(3)
        ]
        for copy in copies:
            copy.start()
        wait_placing()
        for copy in copies:
            copy.wait()


def advance(part, table, fields, halos, units, given=()):
    lanes = len(halos)
    sent = sum(count for _, count in part.sent)
    if part is WHOLE:
        outs = (jax.ShapeDtypeStruct(fields[0].shape, jnp.float32),) * 3
        out_specs = [pl.BlockSpec(memory_space=ANY)] * 3
    else:
        outs = (VMEM((2, 3, sent, SIDE), jnp.float32),) * len(units)
        out_specs = vmem_specs(len(units))
    if not part.halo_rows:
        halos = [group[:1] for group in halos]
    flat = [array for group in halos for array in group]
    tile_count = fields[0].shape[0]
    stacks = [VMEM((lanes, -(-tile_count * TILE_LANES // SIDE), SIDE, SIDE), jnp.float32)]
    if part.halo_rows:
        stacks.append(VMEM((lanes, 2, tile_count, SPARE + TILE_ROWS + 10, SIDE), jnp.float32))
    block = VMEM((part.tiles, ROWS, SIDE), jnp.float32)
    strip = VMEM((ROWS, SIDE), jnp.float32)
    cells = (part.tiles + 1) * sum(count for _, count in part.computed) * SIDE * STEPS
    return pl.pallas_call(
        functools.partial(advance_kernel, part, lanes, units, len(given)),
        name="advance_" + part.name,
        out_shape=outs,
        in_specs=[pl.BlockSpec(memory_space=SMEM)]
        + vmem_specs(FIELDS + len(flat) + len(given)),
        input_output_aliases={
            1 + FIELDS + len(flat) + n: n for n in range(0 if part is WHOLE else len(given))
        },
        out_specs=tuple(out_specs),
        scratch_shapes=stacks
        + [block] * 7
        + [strip] * 7
        + [
            pltpu.SemaphoreType.DMA((part.tiles, 3)),
            pltpu.SemaphoreType.DMA((max(len(given), 1), 2)),
        ],
        compiler_params=pltpu.CompilerParams(vmem_limit_bytes=12 * 1024 * 1024),
        cost_estimate=pl.CostEstimate(
            flops=60 * cells, bytes_accessed=8 * part.tiles * sent * SIDE * 4, transcendentals=6 * cells
        ),
    )(table, *fields, *flat, *given)


def shift_lanes(array, col_shift, sub_shift):
    cols, subs = lax.axis_size("col"), lax.axis_size("sub")
    pairs = [
        (c * subs + s, ((c + col_shift) % cols) * subs + (s + sub_shift) % subs)
        for c in range(cols)
        for s in range(subs)
    ]
    return lax.ppermute(array, ("col", "sub"), pairs)


def over_cols(array):
    return [array] + [shift_lanes(array, c, 0) for c in range(1, lax.axis_size("col"))]


def over_subs(parts):
    subs = lax.axis_size("sub")
    return [
        in_vmem(part if s == 0 else shift_lanes(part, 0, s)) for part in parts for s in range(subs)
    ]


def meet_rows(array, parity):
    rows, subs = lax.axis_size("row"), lax.axis_size("sub")
    pairs = []
    for r in range(rows):
        other = r + 1 if r % 2 == parity else r - 1
        for s in range(subs):
            if 0 <= other < rows:
                pairs.append((r * subs + s, other * subs + s))
            else:
                pairs.append((r * subs + s, r * subs + (s + 1) % subs))
    return lax.ppermute(array, ("row", "sub"), pairs)


def shards(
    water_depth, flow_east, flow_south, bed_level, manning_n, placed_before, placed_after, wet_tiles
):
    cols, subs = lax.axis_size("col"), lax.axis_size("sub")
    tile_count = water_depth.shape[0]
    *fields, columns, pair_even, pair_odd = load(
        (water_depth, flow_east, flow_south, bed_level, manning_n)
    )
    fields = [in_vmem(field) for field in fields]
    columns = over_cols(columns)
    met_even, met_odd = meet_rows(pair_even, 0), meet_rows(pair_odd, 1)
    table = make_table(
        (cols, subs, tile_count, placed_before.shape[0]), placed_before, placed_after, wet_tiles
    )
    joined = join(met_even, met_odd)
    near_rows = over_cols(joined)
    columns[1:], joined, table = lax.optimization_barrier((columns[1:], joined, table))
    near_rows[0] = joined
    table = pltpu.with_memory_space_constraint(table, SMEM)
    near_rows = over_subs(near_rows)
    columns = over_subs(columns)

    def send(part, k):
        return in_vmem(shift_lanes(part, k // subs, k % subs))

    units = tuple(range(1, cols * subs))
    ahead, others = subs, tuple(k for k in units if k != subs)
    alone = [(part,) for part in columns]
    first, *rest = advance(EARLY[0], table, fields, alone, (ahead,) + others)
    rest = advance(EARLY[1], table, fields, alone, others, [in_vmem(part) for part in rest])
    middle = {ahead: send(first, ahead)}
    middle.update((k, send(part, k)) for k, part in zip(others, rest))
    halos = list(zip(columns, near_rows))
    edges = list(advance(LATE, table, fields, halos, units))
    middle[ahead], edges[0] = lax.optimization_barrier((middle[ahead], edges[0]))
    middle[ahead] = in_vmem(middle[ahead])
    edges = [send(part, k) for k, part in zip(units, edges)]
    soon = tuple(range(1, subs)) + (ahead,)
    last = tuple(k for k in units if k not in soon)
    outs = advance(WHOLE, table, fields, halos, soon, [middle[k] for k in soon])
    outs = place(tuple((k, (MIDDLE,)) for k in last), table, [middle[k] for k in last], outs)
    return place(tuple((k, LATE.sent) for k in units), table, edges, outs)


def solution(mesh):
    tiles = P(("basin", "row", "col", "sub"), None, None)
    return jax.shard_map(
        shards,
        mesh=mesh,
        in_specs=(tiles,) * FIELDS + (P("basin"),) * 3,
        out_specs=(tiles,) * 3,
        check_vma=False,
    )
```

```python
import functools
import math

import jax
import jax.numpy as jnp
from jax import lax
from jax.experimental import pallas as pl
from jax.experimental.pallas import tpu as pltpu
from jax.sharding import PartitionSpec as P

STEPS = 6
GRAV = 9.81
STEP_TIME = 0.5
SPACING = 5.0
RATE = 0.1
DEPTH_FLOOR = 0.3

FIELDS = 5
HALO = STEPS
LAST_COLS = (HALO, HALO, HALO - 1, HALO, HALO)
FIRST_COLS = (HALO, HALO - 1, HALO - 1, HALO, HALO - 1)
LAST_ROWS = (HALO - 1, HALO - 1, HALO, HALO - 1, HALO - 1)
FIRST_ROWS = (HALO, HALO - 1, HALO - 1, HALO, HALO - 1)


def starts(counts):
    return [sum(counts[:f]) for f in range(len(counts))]


BOTH_COLS = tuple(a + b for a, b in zip(LAST_COLS, FIRST_COLS))
TILE_LANES = sum(BOTH_COLS)
TILE_ROWS = max(sum(LAST_ROWS), sum(FIRST_ROWS))
COL_AT, LAST_AT, FIRST_AT = starts(BOTH_COLS), starts(LAST_ROWS), starts(FIRST_ROWS)
SIDE = 128
TOP = 16
ROWS = SIDE + 32
LO = 8
HI = SIDE + 24
CHUNK = 24
SPARE = 3
FIXED = TOP - HALO
NT = 4
GROUP = SIDE // NT
CLOSED = 1e30
POWER = -(7.0 / 3.0) / math.log(2.0)

ENTRY = 32
NEAR = {"w": 0, "e": 1, "n": 2, "s": 3, "nw": 4, "ne": 5, "sw": 6, "se": 7}
STEP_TO = ((0, -1), (0, 1), (-1, 0), (1, 0), (-1, -1), (-1, 1), (1, -1), (1, 1))
LEAVE, STAY, RECEIVE = 0, NT * ENTRY, 2 * NT * ENTRY

SMEM = pltpu.SMEM
VMEM = pltpu.VMEM
ANY = pl.ANY
SMALL = pltpu.CompilerParams(vmem_limit_bytes=2 * 1024 * 1024)


def lane_index():
    return lax.broadcasted_iota(jnp.int32, (1, SIDE), 1)


def divide(value, size):
    if size & (size - 1):
        return lax.div(value, size)
    return lax.shift_right_logical(value, size.bit_length() - 1)


def remainder(value, size):
    if size & (size - 1):
        return lax.rem(value, size)
    return value & (size - 1)


def index_kernel(shape, before_ref, after_ref, wet_ref, table, inv_before, inv_after, count):
    cols, subs, tile_count, total = shape
    lanes = cols * subs
    row_tiles = lanes * tile_count
    tile_rows = total // row_tiles
    my_row, my_col, my_sub = (lax.axis_index(name) for name in ("row", "col", "sub"))
    me = my_row * lanes + my_col * subs + my_sub
    spare = RECEIVE + 2 * lanes

    def invert(s, carry):
        for u in range(16):
            inv_before[before_ref[s * 16 + u]] = s * 16 + u
            inv_after[after_ref[s * 16 + u]] = s * 16 + u
        return carry

    lax.fori_loop(0, total // 16, invert, 0)
    for i in range(lanes * 2):
        table[RECEIVE + i] = -1
    for i in range(lanes + 1):
        count[i] = 0

    def relative(lane, sign):
        col = remainder(sign * (divide(lane, subs) - my_col) + cols, cols)
        sub = remainder(sign * (remainder(lane, subs) - my_sub) + subs, subs)
        return col * subs + sub

    def own(s, carry):
        tile = before_ref[me * tile_count + s]
        device = divide(inv_after[tile], tile_count)
        stays = device == me
        to = relative(remainder(device, lanes), 1)
        nth = count[to]
        count[to] = nth + 1
        other = jnp.where(stays | (to == subs), 0, 1)
        left = count[lanes]
        count[lanes] = left + other
        place = jnp.minimum(jnp.where(other == 1, NT - 1 - left, nth), NT - 1)
        base = jnp.where(stays, STAY, LEAVE) + jnp.maximum(place, 0) * ENTRY
        table[base + 1] = wet_ref[tile]
        table[base + 2] = s
        table[base + 3] = jnp.where(stays, s, to * 2 + jnp.minimum(nth, 1))
        row, col = divide(tile, row_tiles), remainder(tile, row_tiles)
        for n, (dr, dc) in enumerate(STEP_TO):
            r, c = row + dr, col + dc
            there = (r >= 0) & (r < tile_rows) & (c >= 0) & (c < row_tiles)
            near = jnp.where(there, tile + (dr * row_tiles + dc), tile)
            at = inv_before[near]
            table[base + 4 + 3 * n] = jnp.where(there, wet_ref[near], 0)
            table[base + 5 + 3 * n] = relative(remainder(divide(at, tile_count), lanes), -1)
            table[base + 6 + 3 * n] = remainder(at, tile_count)
        return carry

    lax.fori_loop(0, tile_count, own, 0)

    for rel in range(1, lanes):
        col = remainder(my_col + (cols - rel // subs), cols)
        sub = remainder(my_sub + (subs - rel % subs), subs)
        device = my_row * lanes + col * subs + sub
        found = jnp.int32(0)
        for s in range(tile_count):
            at = inv_after[before_ref[device * tile_count + s]]
            mine = divide(at, tile_count) == me
            place = RECEIVE + rel * 2 + jnp.minimum(found, 1)
            table[jnp.where(mine, place, spare)] = remainder(at, tile_count)
            found = found + jnp.where(mine, 1, 0)


def make_table(shape, before, after, wet):
    cols, subs, _, total = shape
    return pl.pallas_call(
        functools.partial(index_kernel, shape),
        name="index_table",
        out_shape=SMEM((RECEIVE + 2 * cols * subs + 1,), jnp.int32),
        in_specs=[pl.BlockSpec(memory_space=SMEM)] * 3,
        out_specs=pl.BlockSpec(memory_space=SMEM),
        scratch_shapes=[
            SMEM((total,), jnp.int32),
            SMEM((total,), jnp.int32),
            SMEM((cols * subs + 1,), jnp.int32),
        ],
        compiler_params=SMALL,
    )(before, after, wet)


def in_vmem(array):
    return pltpu.with_memory_space_constraint(array, VMEM)


def vmem_specs(count):
    return [pl.BlockSpec(memory_space=VMEM)] * count


def load_kernel(*refs):
    sources, refs = refs[:FIELDS], refs[FIELDS:]
    fields, (columns, pair_even, pair_odd, first, last, sem, _) = refs[:FIELDS], refs[FIELDS:]
    spill = refs[-1]
    lane = lane_index()
    odd = remainder(lax.axis_index("row"), 2) == 1
    copies = [
        pltpu.make_async_copy(sources[f], fields[f], sem.at[f]) for f in range(FIELDS)
    ]
    for copy in copies:
        copy.start()
    tile_count = fields[0].shape[0]
    blocks = tile_count * TILE_LANES // SIDE
    for f in range(FIELDS):
        copies[f].wait()
        for b in range(blocks + 1):
            target, place = (columns, pl.ds(b * SIDE, SIDE)) if b < blocks else (spill, slice(None))
            packed = target[place, :]
            for t in range(tile_count):
                at = TILE_LANES * t + COL_AT[f] - b * SIDE
                if at < SIDE and at + BOTH_COLS[f] > 0:
                    moved = pltpu.roll(fields[f][t], (at + LAST_COLS[f]) % SIDE, 1)
                    packed = jnp.where((lane >= at) & (lane < at + BOTH_COLS[f]), moved, packed)
            target[place, :] = packed
        for t in range(tile_count):
            at, count = TILE_ROWS * t + FIRST_AT[f], FIRST_ROWS[f]
            first[at : at + count, :] = fields[f][t, :count, :]
            at, count = TILE_ROWS * t + LAST_AT[f], LAST_ROWS[f]
            last[at : at + count, :] = fields[f][t, SIDE - count :, :]
    row = SIDE - HALO
    level = [fields[0][:, r, :] + fields[3][:, r, :] for r in (row, row + 1)]
    ground = jnp.maximum(fields[3][:, row, :], fields[3][:, row + 1, :])
    drag = (GRAV * STEP_TIME) * fields[4][:, row, :] * fields[4][:, row, :]
    flow = face(fields[2][:, row, :], level[0], level[1], ground, drag)
    for t in range(tile_count):
        at = TILE_ROWS * t + LAST_AT[2]
        last[at : at + 1, :] = flow[t : t + 1, :]
    half = SIDE // 2
    columns[blocks * SIDE :, :] = jnp.where(
        lane < half, spill[:half, :], pltpu.roll(spill[half:, :], half, 1)
    )
    pair_even[...] = jnp.where(odd, first[...], last[...])
    pair_odd[...] = jnp.where(odd, last[...], first[...])


def load(arrays):
    tile_count = arrays[0].shape[0]
    rows = VMEM((tile_count * TILE_ROWS, SIDE), jnp.float32)
    outs = [VMEM(array.shape, array.dtype) for array in arrays]
    outs += [VMEM((tile_count * TILE_LANES, SIDE), jnp.float32), rows, rows]
    return pl.pallas_call(
        load_kernel,
        name="load_and_pack",
        out_shape=tuple(outs),
        in_specs=[pl.BlockSpec(memory_space=pltpu.HBM)] * FIELDS,
        out_specs=tuple(vmem_specs(len(outs))),
        scratch_shapes=[
            rows,
            rows,
            pltpu.SemaphoreType.DMA((FIELDS,)),
            VMEM((SIDE, SIDE), jnp.float32),
        ],
        compiler_params=SMALL,
    )(*[pltpu.with_memory_space_constraint(array, pltpu.HBM) for array in arrays])


def join_kernel(met_even, met_odd, joined):
    odd = remainder(lax.axis_index("row"), 2) == 1
    joined[0] = jnp.where(odd, met_even[...], met_odd[...])
    joined[1] = jnp.where(odd, met_odd[...], met_even[...])


def join(met_even, met_odd):
    return pl.pallas_call(
        join_kernel,
        name="join_row_halos",
        out_shape=VMEM((2,) + met_even.shape, met_even.dtype),
        in_specs=vmem_specs(2),
        out_specs=pl.BlockSpec(memory_space=VMEM),
        compiler_params=SMALL,
    )(in_vmem(met_even), in_vmem(met_odd))


def arrivals(table, units, received, spans, outs, sem):
    def each(act):
        for n, k in enumerate(units):
            for j in range(2):
                slot = table[RECEIVE + 2 * k + j]

                @pl.when(slot >= 0)
                def _():
                    act(n, j, slot)

    def start(n, j, slot):
        at = 0
        for begin, count in spans:
            for f in range(3):
                pltpu.make_async_copy(
                    received[n].at[j, f, pl.ds(at, count), :],
                    outs[f].at[slot, pl.ds(begin, count), :],
                    sem.at[n, j],
                ).start()
            at += count

    def wait(n, j, slot):
        tile = received[n].at[j]
        pltpu.make_async_copy(tile, tile, sem.at[n, j]).wait()

    return lambda: each(start), lambda: each(wait)


def place_kernel(groups, *refs):
    table, received, refs = refs[0], refs[1 : 1 + len(groups)], refs[1 + len(groups) :]
    outs, sem = refs[3:6], refs[6]
    copies = [
        arrivals(table, (k,), (array,), spans, outs, sem.at[pl.ds(n, 1)])
        for n, ((k, spans), array) in enumerate(zip(groups, received))
    ]
    for start, _ in copies:
        start()
    for _, wait in copies:
        wait()


def place(groups, table, received, partial_outs):
    count = len(received)
    return pl.pallas_call(
        functools.partial(place_kernel, groups),
        name="place_arrivals",
        out_shape=tuple(jax.ShapeDtypeStruct(o.shape, o.dtype) for o in partial_outs),
        in_specs=[pl.BlockSpec(memory_space=SMEM)]
        + vmem_specs(count)
        + [pl.BlockSpec(memory_space=ANY)] * 3,
        out_specs=tuple(pl.BlockSpec(memory_space=ANY) for _ in partial_outs),
        scratch_shapes=[pltpu.SemaphoreType.DMA((count, 2))],
        input_output_aliases={1 + count + f: f for f in range(3)},
        compiler_params=SMALL,
    )(table, *received, *partial_outs)


def face(flow, level, level_next, ground, friction):
    wetted = jnp.maximum(level, level_next) - ground
    drive = (GRAV * STEP_TIME / SPACING) * jnp.maximum(wetted, 0.0) * (level_next - level)
    power = jnp.exp2(POWER * jnp.log(jnp.maximum(wetted, DEPTH_FLOOR)))
    return (flow - drive) / (1.0 + friction * jnp.abs(flow) * power)


class Part:
    def __init__(self, name, base, tiles, computed, own, halo_rows, sent):
        self.name = name
        self.base = base
        self.tiles = tiles
        self.computed = computed
        self.own = own
        self.halo_rows = halo_rows
        self.sent = sent

    def chunks(self):
        for start, count in self.computed:
            for r in range(start, start + count, CHUNK):
                yield r, min(CHUNK, start + count - r)


def row_span(span):
    return pl.ds(span[0], span[1])


EDGE = 8
BAND = 24
MIDDLE = (EDGE, SIDE - 2 * EDGE)
EARLY = (
    Part("leaving_first", LEAVE, 2, ((TOP, SIDE),), ((0, SIDE),), False, (MIDDLE,)),
    Part("leaving_second", LEAVE + 2 * ENTRY, 2, ((TOP, SIDE),), ((0, SIDE),), False, (MIDDLE,)),
)
LATE = Part(
    "leaving_edges",
    LEAVE,
    NT,
    ((LO, BAND), (HI - BAND, BAND)),
    ((0, BAND - 8), (SIDE - BAND + 8, BAND - 8)),
    True,
    ((0, EDGE), (SIDE - EDGE, EDGE)),
)
WHOLE = Part("staying", STAY, NT, ((LO, HI - LO),), ((0, SIDE),), True, ((0, SIDE),))


def row_bands(r, rows, above, middle, below):
    row = r + lax.broadcasted_iota(jnp.int32, (rows, 1), 0)
    return jnp.where(row < TOP, above, jnp.where(row < TOP + SIDE, middle, below))


def fixed_row(r, rows):
    if not r <= FIXED < r + rows:
        return None
    return r + lax.broadcasted_iota(jnp.int32, (rows, 1), 0) == FIXED


def unless(where, value, other):
    return value if where is None else jnp.where(where, other, value)


def assemble(part, table, base, i, slot, fields, stacks, block, strip):
    halo_cols = stacks[0]
    lane = lane_index()
    at = GROUP * i

    def near(name):
        place = base + 5 + 3 * NEAR[name]
        return table[place], table[place + 1]

    def inside(lo, hi):
        return (lane >= at + lo) & (lane < at + hi)

    west, east = near("w"), near("e")
    for f in range(FIELDS):

        def ends(side, start, middle, left, right, out):
            rows = pl.ds(start, 8)
            mid, left_end, right_end = (
                stacks[1][place[0], side, place[1], rows, :] for place in (middle, left, right)
            )
            block[f][i, out : out + 8, :] = mid
            lower = jnp.where(lane < SIDE // 2, mid, left_end)
            upper = jnp.where(lane < SIDE // 2, right_end, mid)
            value = jnp.where(
                inside(0, 16),
                pltpu.roll(lower, (at + 8) % SIDE, 1),
                pltpu.roll(upper, (at + 24) % SIDE, 1),
            )
            if i:
                value = jnp.where(inside(0, GROUP), value, strip[f][out : out + 8, :])
            strip[f][out : out + 8, :] = value

        if part.halo_rows:
            start = SPARE + LAST_AT[f] + LAST_ROWS[f] - 8
            ends(0, start, near("n"), near("nw"), near("ne"), LO)
            ends(1, SPARE + FIRST_AT[f], near("s"), near("sw"), near("se"), TOP + SIDE)

        for start, count in part.own:
            own, out = pl.ds(start, count), pl.ds(TOP + start, count)

            def shifted(place, offset, goal):
                lanes_at = TILE_LANES * place[1] + (COL_AT[f] + offset)
                b, source = divide(lanes_at, SIDE), remainder(lanes_at, SIDE)
                beyond = jnp.minimum(b + 1, halo_cols.shape[1] - 1)
                value = jnp.where(
                    lane >= source, halo_cols[place[0], b, own, :], halo_cols[place[0], beyond, own, :]
                )
                return pltpu.roll(value, remainder(goal - source + SIDE, SIDE), 1)

            core = fields[f][slot, own, :]
            block[f][i, out, :] = core
            value = shifted(west, 0, at + 8 - LAST_COLS[f])
            if i:
                value = jnp.where(inside(0, 8), value, strip[f][out, :])
            value = jnp.where(inside(8, 16), pltpu.roll(core, (at + 8) % SIDE, 1), value)
            value = jnp.where(inside(16, 24), pltpu.roll(core, (at + 24) % SIDE, 1), value)
            value = jnp.where(inside(24, GROUP), shifted(east, LAST_COLS[f], at + 24), value)
            strip[f][out, :] = value


def prepare_strip(part, near_wet, strip, ground_x, ground_y):
    level, flow_x, flow_y, ground, friction = strip
    lane = lane_index()

    def lane_wet(center, left, right):
        value = jnp.zeros((1, SIDE), jnp.int32)
        for i in range(part.tiles):
            at = GROUP * i
            middle = near_wet(i, center) if center else 1
            sides = jnp.where(
                lane < at + 8,
                near_wet(i, left),
                jnp.where(lane < at + 24, middle, near_wet(i, right)),
            )
            value = jnp.where((lane >= at) & (lane < at + GROUP), sides, value)
        return value

    bands = (lane_wet("n", "nw", "ne"), lane_wet(None, "w", "e"), lane_wet("s", "sw", "se"))
    for r, rows in part.chunks():
        at, south = pl.ds(r, rows), pl.ds(r + 1, rows)
        z = ground[at, :]
        here, next_row = row_bands(r, rows, *bands), row_bands(r + 1, rows, *bands)
        open_x = (here == 1) & (pltpu.roll(here, SIDE - 1, 1) == 1)
        open_y = (here == 1) & (next_row == 1)
        z_east = pltpu.roll(z, SIDE - 1, 1)
        fixed = fixed_row(r, rows)
        ground_x[at, :] = jnp.where(open_x, jnp.maximum(z, z_east), CLOSED)
        ground_y[at, :] = unless(
            fixed, jnp.where(open_y, jnp.maximum(z, ground[south, :]), CLOSED), CLOSED
        )
        flow_x[at, :] = jnp.where(open_x, flow_x[at, :], 0.0)
        flow_y[at, :] = jnp.where(open_y, flow_y[at, :], 0.0)
        friction[at, :] = unless(
            fixed, (GRAV * STEP_TIME) * friction[at, :] * friction[at, :], 0.0
        )
        level[at, :] = level[at, :] + z


def prepare_tile(part, near_wet, i, block, ground_x, ground_y, strip_ground):
    level, flow_x, flow_y, ground, friction = block
    lane = lane_index()
    last = lane == SIDE - 1
    n, e, s = near_wet(i, "n"), near_wet(i, "e"), near_wet(i, "s")
    bands = (
        jnp.where(last, n * near_wet(i, "ne"), n),
        jnp.where(last, e, 1),
        jnp.where(last, s * near_wet(i, "se"), s),
    )
    for r, rows in part.chunks():
        at, south = pl.ds(r, rows), pl.ds(r + 1, rows)
        z = ground[i, at, :]
        z_east = jnp.where(
            last, pltpu.roll(strip_ground[at, :], to_east(i), 1), pltpu.roll(z, SIDE - 1, 1)
        )
        open_x = row_bands(r, rows, *bands) == 1
        open_y = (row_bands(r + 1, rows, n, 1, s) == 1) & (row_bands(r, rows, n, 1, s) == 1)
        fixed = fixed_row(r, rows)
        ground_x[i, at, :] = jnp.where(open_x, jnp.maximum(z, z_east), CLOSED)
        ground_y[i, at, :] = unless(
            fixed, jnp.where(open_y, jnp.maximum(z, ground[i, south, :]), CLOSED), CLOSED
        )
        flow_x[i, at, :] = jnp.where(open_x, flow_x[i, at, :], 0.0)
        flow_y[i, at, :] = jnp.where(open_y, flow_y[i, at, :], 0.0)
        friction[i, at, :] = unless(
            fixed, (GRAV * STEP_TIME) * friction[i, at, :] * friction[i, at, :], 0.0
        )
        level[i, at, :] = level[i, at, :] + z


def to_east(i):
    return (SIDE - 1 - GROUP * i - 24) % SIDE


def to_west(i):
    return (SIDE - GROUP * i - 7) % SIDE


def unpack_columns(part, packed, out):
    blocks, half = out.shape[0] - 1, SIDE // 2
    for start, count in part.own:
        rows = pl.ds(start, count)
        for b in range(blocks):
            out[b, rows, :] = packed[b * SIDE + start : b * SIDE + start + count, :]
        if start < half:
            n = min(count, half - start)
            out[blocks, start : start + n, :] = packed[
                blocks * SIDE + start : blocks * SIDE + start + n, :
            ]
        if start + count > half:
            low, high = max(start, half), start + count
            lower = packed[blocks * SIDE + low - half : blocks * SIDE + high - half, :]
            out[blocks, low:high, :] = pltpu.roll(lower, half, 1)


def advance_kernel(part, lanes, units, given, *refs):
    table = refs[0]
    fields = refs[1 : 1 + FIELDS]
    kinds = 2 if part.halo_rows else 1
    halos, refs = refs[1 + FIELDS : 1 + FIELDS + kinds * lanes], refs[1 + FIELDS + kinds * lanes :]
    received, refs = refs[:given], refs[given:]
    n_out = 3 if part is WHOLE else len(units)
    outs, stacks, refs = refs[:n_out], refs[n_out : n_out + kinds], refs[n_out + kinds :]
    (
        level, flow_x, flow_y, ground, friction, ground_x, ground_y,
        s_level, s_flow_x, s_flow_y, s_ground, s_friction, s_ground_x, s_ground_y,
        sem_out, sem_in,
    ) = refs
    if part is WHOLE:
        start_placing, wait_placing = arrivals(table, units, received, (MIDDLE,), outs, sem_in)
        start_placing()
    block = (level, flow_x, flow_y, ground, friction)
    strip = (s_level, s_flow_x, s_flow_y, s_ground, s_friction)
    lane = lane_index()
    last, first = lane == SIDE - 1, lane == 0

    def entry(i):
        at = part.base + i * ENTRY
        return table[at + 1], table[at + 2], table[at + 3]

    def near_wet(i, name):
        return table[part.base + i * ENTRY + 4 + 3 * NEAR[name]]

    for k in range(lanes):
        for n in range(kinds):
            if n:
                for side in range(2):
                    for t in range(fields[0].shape[0]):
                        stacks[1][k, side, t, :SPARE, :] = jnp.zeros((SPARE, SIDE), jnp.float32)
                        stacks[1][k, side, t, SPARE : SPARE + TILE_ROWS, :] = halos[kinds * k + 1][
                            side, TILE_ROWS * t : TILE_ROWS * (t + 1), :
                        ]
            else:
                unpack_columns(part, halos[kinds * k], stacks[0].at[k])
    for i in range(part.tiles):
        base = part.base + i * ENTRY
        assemble(part, table, base, i, entry(i)[1], fields, stacks, block, strip)
    prepare_strip(part, near_wet, strip, s_ground_x, s_ground_y)
    for i in range(part.tiles):
        prepare_tile(part, near_wet, i, block, ground_x, ground_y, s_ground)

    def step(_, carry):
        for r, rows in part.chunks():
            at, south = pl.ds(r, rows), pl.ds(r + 1, rows)
            e, c = s_level[at, :], s_friction[at, :]
            e_east = pltpu.roll(e, SIDE - 1, 1)
            s_flow_x[at, :] = face(s_flow_x[at, :], e, e_east, s_ground_x[at, :], c)
            s_flow_y[at, :] = face(s_flow_y[at, :], e, s_level[south, :], s_ground_y[at, :], c)
        for i in range(part.tiles):
            for r, rows in part.chunks():
                at, south = pl.ds(r, rows), pl.ds(r + 1, rows)
                e, c = level[i, at, :], friction[i, at, :]
                e_east = jnp.where(
                    last, pltpu.roll(s_level[at, :], to_east(i), 1), pltpu.roll(e, SIDE - 1, 1)
                )
                flow_x[i, at, :] = face(flow_x[i, at, :], e, e_east, ground_x[i, at, :], c)
                flow_y[i, at, :] = face(
                    flow_y[i, at, :], e, level[i, south, :], ground_y[i, at, :], c
                )
        for r, rows in part.chunks():
            at, north = pl.ds(r, rows), pl.ds(r - 1, rows)
            qx = s_flow_x[at, :]
            s_level[at, :] = s_level[at, :] + RATE * (
                (pltpu.roll(qx, 1, 1) - qx) + (s_flow_y[north, :] - s_flow_y[at, :])
            )
        for i in range(part.tiles):
            for r, rows in part.chunks():
                at, north = pl.ds(r, rows), pl.ds(r - 1, rows)
                qx = flow_x[i, at, :]
                qx_west = jnp.where(
                    first, pltpu.roll(s_flow_x[at, :], to_west(i), 1), pltpu.roll(qx, 1, 1)
                )
                level[i, at, :] = level[i, at, :] + RATE * (
                    (qx_west - qx) + (flow_y[i, north, :] - flow_y[i, at, :])
                )
        return carry

    lax.fori_loop(0, STEPS, step, 0, unroll=True)

    results = (level, flow_x, flow_y)
    for i in range(part.tiles):
        wet, slot, _ = entry(i)
        for start, count in part.sent:
            own, at = pl.ds(start, count), pl.ds(TOP + start, count)
            level[i, at, :] = level[i, at, :] - ground[i, at, :]
            for f in range(3):
                results[f][i, at, :] = jnp.where(
                    wet == 1, results[f][i, at, :], fields[f][slot, own, :]
                )

    if part is not WHOLE:
        for i in range(part.tiles):
            target = entry(i)[2]
            for out_ref, k in zip(outs, units):
                @pl.when(divide(target, 2) == k)
                def _():
                    out = 0
                    for start, count in part.sent:
                        for f in range(3):
                            value = results[f][i, pl.ds(TOP + start, count), :]
                            out_ref[remainder(target, 2), f, out : out + count, :] = value
                        out += count

    else:
        copies = [
            pltpu.make_async_copy(
                results[f].at[i, pl.ds(TOP, SIDE), :], outs[f].at[entry(i)[2]], sem_out.at[i, f]
            )
            for i in range(part.tiles)
            for f in range(3)
        ]
        for copy in copies:
            copy.start()
        wait_placing()
        for copy in copies:
            copy.wait()


def advance(part, table, fields, halos, units, given=()):
    lanes = len(halos)
    sent = sum(count for _, count in part.sent)
    if part is WHOLE:
        outs = (jax.ShapeDtypeStruct(fields[0].shape, jnp.float32),) * 3
        out_specs = [pl.BlockSpec(memory_space=ANY)] * 3
    else:
        outs = (VMEM((2, 3, sent, SIDE), jnp.float32),) * len(units)
        out_specs = vmem_specs(len(units))
    if not part.halo_rows:
        halos = [group[:1] for group in halos]
    flat = [array for group in halos for array in group]
    tile_count = fields[0].shape[0]
    stacks = [VMEM((lanes, -(-tile_count * TILE_LANES // SIDE), SIDE, SIDE), jnp.float32)]
    if part.halo_rows:
        stacks.append(VMEM((lanes, 2, tile_count, SPARE + TILE_ROWS + 10, SIDE), jnp.float32))
    block = VMEM((part.tiles, ROWS, SIDE), jnp.float32)
    strip = VMEM((ROWS, SIDE), jnp.float32)
    cells = (part.tiles + 1) * sum(count for _, count in part.computed) * SIDE * STEPS
    return pl.pallas_call(
        functools.partial(advance_kernel, part, lanes, units, len(given)),
        name="advance_" + part.name,
        out_shape=outs,
        in_specs=[pl.BlockSpec(memory_space=SMEM)]
        + vmem_specs(FIELDS + len(flat) + len(given)),
        input_output_aliases={
            1 + FIELDS + len(flat) + n: n for n in range(0 if part is WHOLE else len(given))
        },
        out_specs=tuple(out_specs),
        scratch_shapes=stacks
        + [block] * 7
        + [strip] * 7
        + [
            pltpu.SemaphoreType.DMA((part.tiles, 3)),
            pltpu.SemaphoreType.DMA((max(len(given), 1), 2)),
        ],
        compiler_params=pltpu.CompilerParams(vmem_limit_bytes=12 * 1024 * 1024),
        cost_estimate=pl.CostEstimate(
            flops=60 * cells, bytes_accessed=8 * part.tiles * sent * SIDE * 4, transcendentals=6 * cells
        ),
    )(table, *fields, *flat, *given)


def shift_lanes(array, col_shift, sub_shift):
    cols, subs = lax.axis_size("col"), lax.axis_size("sub")
    pairs = [
        (c * subs + s, ((c + col_shift) % cols) * subs + (s + sub_shift) % subs)
        for c in range(cols)
        for s in range(subs)
    ]
    return lax.ppermute(array, ("col", "sub"), pairs)


def over_cols(array):
    return [array] + [shift_lanes(array, c, 0) for c in range(1, lax.axis_size("col"))]


def over_subs(parts):
    subs = lax.axis_size("sub")
    return [
        in_vmem(part if s == 0 else shift_lanes(part, 0, s)) for part in parts for s in range(subs)
    ]


def meet_rows(array, parity):
    rows, subs = lax.axis_size("row"), lax.axis_size("sub")
    pairs = []
    for r in range(rows):
        other = r + 1 if r % 2 == parity else r - 1
        for s in range(subs):
            if 0 <= other < rows:
                pairs.append((r * subs + s, other * subs + s))
            else:
                pairs.append((r * subs + s, r * subs + (s + 1) % subs))
    return lax.ppermute(array, ("row", "sub"), pairs)


def shards(
    water_depth, flow_east, flow_south, bed_level, manning_n, placed_before, placed_after, wet_tiles
):
    cols, subs = lax.axis_size("col"), lax.axis_size("sub")
    tile_count = water_depth.shape[0]
    *fields, columns, pair_even, pair_odd = load(
        (water_depth, flow_east, flow_south, bed_level, manning_n)
    )
    fields = [in_vmem(field) for field in fields]
    columns = over_cols(columns)
    met_even, met_odd = meet_rows(pair_even, 0), meet_rows(pair_odd, 1)
    table = make_table(
        (cols, subs, tile_count, placed_before.shape[0]), placed_before, placed_after, wet_tiles
    )
    joined = join(met_even, met_odd)
    near_rows = over_cols(joined)
    columns[1:], joined, table = lax.optimization_barrier((columns[1:], joined, table))
    near_rows[0] = joined
    table = pltpu.with_memory_space_constraint(table, SMEM)
    near_rows = over_subs(near_rows)
    columns = over_subs(columns)

    def send(part, k):
        return in_vmem(shift_lanes(part, k // subs, k % subs))

    units = tuple(range(1, cols * subs))
    ahead, others = subs, tuple(k for k in units if k != subs)
    alone = [(part,) for part in columns]
    first, *rest = advance(EARLY[0], table, fields, alone, (ahead,) + others)
    rest = advance(EARLY[1], table, fields, alone, others, [in_vmem(part) for part in rest])
    middle = {ahead: send(first, ahead)}
    middle.update((k, send(part, k)) for k, part in zip(others, rest))
    halos = list(zip(columns, near_rows))
    edges = list(advance(LATE, table, fields, halos, units))
    own = units.index(ahead)
    middle[ahead], edges[own] = lax.optimization_barrier((middle[ahead], edges[own]))
    middle[ahead] = in_vmem(middle[ahead])
    edges = [send(part, k) for k, part in zip(units, edges)]
    soon = tuple(range(1, subs)) + (ahead,)
    last = tuple(k for k in units if k not in soon)
    outs = advance(WHOLE, table, fields, halos, soon, [middle[k] for k in soon])
    near = [n for n, k in enumerate(units) if k < subs]
    far = [n for n, k in enumerate(units) if k >= subs]
    groups = tuple((k, (MIDDLE,)) for k in last) + tuple((units[n], LATE.sent) for n in near)
    outs = place(groups, table, [middle[k] for k in last] + [edges[n] for n in near], outs)
    groups = tuple((units[n], LATE.sent) for n in far)
    return place(groups, table, [edges[n] for n in far], outs)


def solution(mesh):
    tiles = P(("basin", "row", "col", "sub"), None, None)
    return jax.shard_map(
        shards,
        mesh=mesh,
        in_specs=(tiles,) * FIELDS + (P("basin"),) * 3,
        out_specs=(tiles,) * 3,
        check_vma=False,
    )
```
